32 devices in a mesh: section: 2 (over y), tensor: 4 (over z), dp: 4 (over x, core).
Axes of the slice: x: 2, y: 2, z: 4, core: 2. Of those that a mesh axis runs over, the one named last changes fastest.
Arguments:
- tokens: bfloat16 [2, 4096, 1280], P(None, 'dp'), may hold values from -6 to 6
- cotangent: bfloat16 [2, 4096, 1280], P(None, 'dp'), may hold values from -6 to 6
- seg_ids: int32 [2, 4096], P(None, 'dp'), may hold values from 0 to 448, as said below
- observed: int32 [2, 4096], P(None, 'dp'), may hold values from 0 to 1, as said below
- query_key_value_weight: bfloat16 [2, 3, 1280, 1280], P('section', None, None, 'tensor'), may hold values from -0.15625 to 0.15625
- w_out: bfloat16 [2, 1280, 1280], P('section', 'tensor'), may hold values from -0.625 to 0.625
- w_in: bfloat16 [2, 1280, 5120], P('section', None, 'tensor'), may hold values from -0.15625 to 0.15625
- w_down: bfloat16 [2, 5120, 1280], P('section', 'tensor'), may hold values from -0.125 to 0.125
- norm_gains: float32 [2, 2, 1280], P('section'), may hold values from 0.25 to 1.75
Outputs:
- layer_acts: bfloat16 [2, 2, 4096, 1280], P('section', None, 'dp')
- grad_acts: bfloat16 [2, 2, 4096, 1280], P('section', None, 'dp')
- w_qkv_grad: float32 [2, 3, 1280, 1280], P('section', None, 'dp', 'tensor')
- w_out_grad: float32 [2, 1280, 1280], P('section', 'tensor', 'dp')
- w_in_grad: float32 [2, 1280, 5120], P('section', 'dp', 'tensor')
- w_down_grad: float32 [2, 5120, 1280], P('section', 'tensor', 'dp')
- norm_gains_grad: float32 [2, 2, 1280], P('section', None, 'dp')
The draws below stay inside these ranges and needn't reach their ends.
Inputs may be any that keep to these rules, and one draw needn't show every extreme that they name: `seg_ids`: within each aligned block of 512 positions the series numbers start at 0, rise by one at each new series and never fall; a series holds 1 to 64 positions, and the first series of every block holds exactly 64. `observed`: in every series the unobserved patches come first.
All inputs are finite; a program needn't handle non-finite values.
Results may differ from the reference program's by a relative error of at most 0.025.
Values may be sent and summed in bfloat16 or wider, within the bound.
A program may use at most 256 MiB of HBM per device.

```python
import math
import jax
import jax.numpy as jnp
from jax import lax

D = 1280
H = 16
HEAD_SIZE = 80
FF = 5120
HD = 1280
ROW_POSITIONS = 512
MAXLEN = 64
MICRO_BATCHES = 2
MICRO_TOKENS = 4096
N_TENSOR = 4


def series_layout(key):
    count_of_rows = MICRO_TOKENS // ROW_POSITIONS
    array_shape = (MICRO_BATCHES, count_of_rows, ROW_POSITIONS)
    lengths = jax.random.randint(jax.random.fold_in(key, 11), array_shape, 1, MAXLEN + 1)
    lengths = lengths.at[:, :, 0].set(MAXLEN)
    picked_rows = jax.random.randint(jax.random.fold_in(key, 13), (), 0, count_of_rows)
    lone_series = (jnp.arange(MICRO_BATCHES)[:, None, None] == 0) & (jnp.arange(count_of_rows)[None, :, None] == picked_rows) & (jnp.arange(ROW_POSITIONS)[None, None, :] > 0)
    lengths = jnp.where(lone_series, 1, lengths)
    ends = jnp.cumsum(lengths, axis=-1)
    target_slots = jnp.arange(ROW_POSITIONS, dtype=jnp.int32)
    series_values = jnp.sum((ends[..., None, :] <= target_slots[:, None]).astype(jnp.int32), axis=-1)
    starts = jnp.take_along_axis(ends - lengths, series_values, axis=-1)
    padding = jax.random.randint(jax.random.fold_in(key, 12), array_shape, 0, lengths)
    offsets = target_slots - starts
    visited_count = (offsets >= jnp.take_along_axis(padding, series_values, axis=-1)).astype(jnp.int32)
    return (series_values.reshape(MICRO_BATCHES, MICRO_TOKENS), visited_count.reshape(MICRO_BATCHES, MICRO_TOKENS))


def draw_seg_ids(key, part):
    series_values, visited_count = series_layout(key)
    return series_values


def draw_observed(key, part):
    series_values, visited_count = series_layout(key)
    return visited_count


def level_of(stream_key, shape, shards, smallest, top_value):
    factor_of, own = 1.0, jax.random.fold_in(stream_key, 6)
    for axis_at, parts in shards:
        heights = jnp.exp(jax.random.uniform(jax.random.fold_in(own, axis_at), (parts,), jnp.float32, smallest / len(shards), top_value / len(shards)))
        factor_of = factor_of * jnp.repeat(heights, shape[axis_at] // parts).reshape([-1 if axis == axis_at else 1 for axis in range(len(shape))])
    return factor_of


def noise(key, shape, scale, reach, shards=(), held_as=jnp.bfloat16):
    values = scale * jax.random.normal(key, shape, jnp.float32)
    if shards:
        values = values * level_of(key, shape, shards, -0.22, 0.18)
    return jnp.clip(values, -reach, reach).astype(held_as)


def setup_inputs(seed: int = 0) -> dict:
    arg_keys = jax.random.split(jax.random.key(seed), 10)
    return {
        "tokens": noise(arg_keys[0], (MICRO_BATCHES, MICRO_TOKENS, D), 1.0, 6.0, ((1, 4),)),
        "cotangent": noise(arg_keys[1], (MICRO_BATCHES, MICRO_TOKENS, D), 1.0, 6.0, ((1, 4),)),
        "seg_ids": draw_seg_ids(jax.random.fold_in(arg_keys[9], 71), 0),
        "observed": draw_observed(jax.random.fold_in(arg_keys[9], 71), 0),
        "query_key_value_weight": noise(arg_keys[4], (2, 3, D, HD), D ** -0.5, 0.15625, ((0, 2), (3, 4))),
        "w_out": noise(arg_keys[5], (2, HD, D), (HD // 16) ** -0.5, 0.625, ((0, 2), (1, 4))),
        "w_in": noise(arg_keys[6], (2, D, FF), D ** -0.5, 0.15625, ((0, 2), (2, 4))),
        "w_down": noise(arg_keys[7], (2, FF, D), (FF // 2) ** -0.5, 0.125, ((0, 2), (1, 4))),
        "norm_gains": jnp.clip(1.0 + 0.15 * jax.random.normal(arg_keys[8], (2, 2, D), jnp.float32), 0.25, 1.75),
    }


EPS = 1e-06
BIG = 1000000000.0

@jax.custom_vjp
def low(v):
    return lax.optimization_barrier(v.astype(jnp.bfloat16)).astype(jnp.float32)

@jax.custom_vjp
def low_back(v):
    return v

def low_keep(v):
    return (low(v), None)

def low_pass(kept, grad):
    return (grad,)

def back_keep(v):
    return (v, None)

def back_low(kept, grad):
    return (low(grad),)
low.defvjp(low_keep, low_pass)
low_back.defvjp(back_keep, back_low)

def matrix_product(left, right):
    return jnp.dot(left, right, precision=lax.Precision.HIGHEST, preferred_element_type=jnp.float32)

def rope_tables():
    half_size = HEAD_SIZE // 2
    frequencies = 10000.0 ** (-jnp.arange(half_size, dtype=jnp.float32) / half_size)
    rotary_angles = jnp.arange(ROW_POSITIONS, dtype=jnp.float32)[:, None] * frequencies[None, :]
    return (jnp.cos(rotary_angles)[:, None, :], jnp.sin(rotary_angles)[:, None, :])

def rotate(values, cosine, sine):
    half_size = HEAD_SIZE // 2
    first_half = values[..., :half_size]
    second_half = values[..., half_size:]
    return jnp.concatenate([first_half * cosine - second_half * sine, first_half * sine + second_half * cosine], axis=-1)

def row_attention(inputs):
    query, key_rows, value_rows, series_values, visited_count = inputs
    scores = jnp.einsum('qhd,khd->hqk', query, key_rows, precision=lax.Precision.HIGHEST) / math.sqrt(HEAD_SIZE)
    scores = low_back(scores)
    target_slots = jnp.arange(ROW_POSITIONS, dtype=jnp.int32)
    allowed = (series_values[:, None] == series_values[None, :]) & (target_slots[None, :] <= target_slots[:, None]) & ((visited_count[None, :] == 1) | (target_slots[None, :] == target_slots[:, None]))
    scores = jnp.where(allowed[None], scores, -BIG)
    shifted = scores - lax.optimization_barrier(jnp.max(scores, axis=-1, keepdims=True))
    weights = jnp.exp(shifted)
    probs = low(weights / lax.optimization_barrier(jnp.sum(weights, axis=-1, keepdims=True)))
    return jnp.einsum('hqk,khd->qhd', probs, value_rows, precision=lax.Precision.HIGHEST)

def layer(layer_in, query_key_value_weight, w_out, w_in, w_down, norm_gains, series_values, visited_count):
    cosine, sine = rope_tables()
    overall_rows = layer_in.shape[0]
    count_of_rows = overall_rows // ROW_POSITIONS
    device_heads = H // N_TENSOR
    model_width = device_heads * HEAD_SIZE
    units = FF // N_TENSOR
    rows_per_series = series_values.reshape(count_of_rows, ROW_POSITIONS)
    visited_rows = visited_count.reshape(count_of_rows, ROW_POSITIONS)
    scale_first = lax.rsqrt(lax.optimization_barrier(jnp.mean(layer_in * layer_in, axis=-1, keepdims=True)) + EPS)
    normed = low(layer_in * scale_first * norm_gains[0])
    attn_sum = jnp.zeros_like(layer_in)
    for group in range(N_TENSOR):
        common_values = low_back(normed)
        lower_bound = group * model_width

        def project(row_index):
            return matrix_product(common_values, query_key_value_weight[row_index][:, lower_bound:lower_bound + model_width]).reshape(count_of_rows, ROW_POSITIONS, device_heads, HEAD_SIZE)
        query = low(rotate(low_back(project(0)), cosine, sine))
        key_rows = low(rotate(low_back(project(1)), cosine, sine))
        value_rows = low(low_back(project(2)))
        mixed = lax.map(jax.checkpoint(row_attention), (query, key_rows, value_rows, rows_per_series, visited_rows))
        mixed = low(low_back(mixed.reshape(overall_rows, model_width)))
        attn_sum = attn_sum + low(matrix_product(mixed, w_out[lower_bound:lower_bound + model_width, :]))
    middle = layer_in + low_back(attn_sum)
    scale_second = lax.rsqrt(lax.optimization_barrier(jnp.mean(middle * middle, axis=-1, keepdims=True)) + EPS)
    normed_second = low(middle * scale_second * norm_gains[1])
    branch = jnp.zeros_like(layer_in)
    for group in range(N_TENSOR):
        common_values = low_back(normed_second)
        lower_bound = group * units
        before = low_back(matrix_product(common_values, w_in[:, lower_bound:lower_bound + units]))
        activated = low(before * lax.logistic(before))
        branch = branch + low(matrix_product(activated, w_down[lower_bound:lower_bound + units, :]))
    return middle + low_back(branch)

def reference(tokens, cotangent, seg_ids, observed, query_key_value_weight, w_out, w_in, w_down, norm_gains):
    params = [tuple((array[row_index].astype(jnp.float32) for array in (query_key_value_weight, w_out, w_in, w_down, norm_gains))) for row_index in range(2)]
    totals = [[jnp.zeros_like(array) for array in params[row_index]] for row_index in range(2)]
    first_out, second_out, first_grad, second_grad = ([], [], [], [])
    for micro in range(MICRO_BATCHES):
        series_values = seg_ids[micro]
        visited_count = observed[micro]

        def apply_layer(layer_in, w_a, w_b, w_c, w_d, w_e):
            return layer(layer_in, w_a, w_b, w_c, w_d, w_e, series_values, visited_count)
        hidden_raw, back_first = jax.vjp(apply_layer, tokens[micro].astype(jnp.float32), *params[0])
        hidden = low(hidden_raw)
        final, back_second = jax.vjp(apply_layer, hidden, *params[1])
        pulled = back_second(cotangent[micro].astype(jnp.float32))
        upstream = low(pulled[0])
        pushed = back_first(upstream)
        for row_index in range(5):
            totals[1][row_index] = totals[1][row_index] + pulled[row_index + 1]
            totals[0][row_index] = totals[0][row_index] + pushed[row_index + 1]
        first_out.append(hidden)
        second_out.append(final)
        first_grad.append(pushed[0])
        second_grad.append(upstream)
    layer_acts = jnp.stack([jnp.stack(first_out), jnp.stack(second_out)]).astype(jnp.bfloat16)
    grad_acts = jnp.stack([jnp.stack(first_grad), jnp.stack(second_grad)]).astype(jnp.bfloat16)
    grads = [jnp.stack([totals[0][row_index], totals[1][row_index]]) for row_index in range(5)]
    return (layer_acts, grad_acts, grads[0], grads[1], grads[2], grads[3], grads[4])
```

```python
import functools
import math

import jax
import jax.numpy as jnp
from jax import lax
from jax.experimental import pallas as pl
from jax.experimental.pallas import tpu as pltpu
from jax.sharding import PartitionSpec as P

HEAD_SIZE = 80
HALF = HEAD_SIZE // 2
ROW = 512
QB = 128
GROUP = 8
EPS = 1e-06
BIG = 1000000000.0
SCALE = 1.0 / math.sqrt(HEAD_SIZE)
BF16 = jnp.bfloat16
F32 = jnp.float32


def dot_nn(a, b):
    return lax.dot_general(a, b, (((1,), (0,)), ((), ())), preferred_element_type=F32)


def dot_nt(a, b):
    return lax.dot_general(a, b, (((1,), (1,)), ((), ())), preferred_element_type=F32)


def dot_tn(a, b):
    return lax.dot_general(a, b, (((0,), (0,)), ((), ())), preferred_element_type=F32)


def rope_tables():
    freq = 10000.0 ** (-jnp.arange(HALF, dtype=F32) / HALF)
    ang = jnp.arange(ROW, dtype=F32)[:, None] * freq[None, :]
    cos, sin = jnp.cos(ang), jnp.sin(ang)
    cos_full = jnp.tile(jnp.concatenate([cos, cos], axis=1), (1, GROUP))
    sin_full = jnp.tile(jnp.concatenate([-sin, sin], axis=1), (1, GROUP))
    return cos_full, sin_full


def partner(x):
    width = x.shape[1]
    lane = lax.broadcasted_iota(jnp.int32, x.shape, 1)
    first = lax.rem(lane, HEAD_SIZE) < HALF
    return jnp.where(first, pltpu.roll(x, width - HALF, 1), pltpu.roll(x, HALF, 1))


def block_mask(i, seg_col, seg_row, obs_row):
    k0 = max(i - 1, 0) * QB
    k1 = (i + 1) * QB
    shape = (QB, k1 - k0)
    qi = lax.broadcasted_iota(jnp.int32, shape, 0) + i * QB
    kj = lax.broadcasted_iota(jnp.int32, shape, 1) + k0
    same = seg_col[i * QB:(i + 1) * QB, :] == seg_row[:, k0:k1]
    seen = (obs_row[:, k0:k1] == 1) | (kj == qi)
    return k0, k1, same & (kj <= qi) & seen


def softmax_block(q, k, allowed):
    s = jnp.where(allowed, dot_nt(q, k) * SCALE, -BIG)
    e = jnp.exp(s - jnp.max(s, axis=1, keepdims=True))
    return e * (1.0 / jnp.sum(e, axis=1, keepdims=True))


def attn_fwd_kernel(qp, kp, v, seg_col, seg_row, obs_row, cos, sin, q_out, k_out, o_out):
    x = qp[...]
    q_out[...] = (x * cos[...] + partner(x) * sin[...]).astype(BF16)
    x = kp[...]
    k_out[...] = (x * cos[...] + partner(x) * sin[...]).astype(BF16)
    sc, sr, ob = seg_col[...], seg_row[...], obs_row[...]
    for i in range(ROW // QB):
        k0, k1, allowed = block_mask(i, sc, sr, ob)
        for h in range(GROUP):
            c0, c1 = h * HEAD_SIZE, (h + 1) * HEAD_SIZE
            p = softmax_block(q_out[i * QB:(i + 1) * QB, c0:c1], k_out[k0:k1, c0:c1], allowed)
            o_out[i * QB:(i + 1) * QB, c0:c1] = dot_nn(p.astype(BF16), v[k0:k1, c0:c1]).astype(BF16)


def attn_bwd_kernel(q, k, v, do, seg_col, seg_row, obs_row, cos, sin, dqp, dkp, dv, dq_s, dk_s, dv_s):
    dk_s[...] = jnp.zeros_like(dk_s)
    dv_s[...] = jnp.zeros_like(dv_s)
    sc, sr, ob = seg_col[...], seg_row[...], obs_row[...]
    for i in range(ROW // QB):
        k0, k1, allowed = block_mask(i, sc, sr, ob)
        r0, r1 = i * QB, (i + 1) * QB
        for h in range(GROUP):
            c0, c1 = h * HEAD_SIZE, (h + 1) * HEAD_SIZE
            qi, ki, vi, di = q[r0:r1, c0:c1], k[k0:k1, c0:c1], v[k0:k1, c0:c1], do[r0:r1, c0:c1]
            p = softmax_block(qi, ki, allowed)
            dv_s[k0:k1, c0:c1] += dot_tn(p.astype(BF16), di)
            dp = dot_nt(di, vi)
            ds = (p * (dp - jnp.sum(p * dp, axis=1, keepdims=True))).astype(BF16)
            dq_s[r0:r1, c0:c1] = dot_nn(ds, ki) * SCALE
            dk_s[k0:k1, c0:c1] += dot_tn(ds, qi) * SCALE
    x = dq_s[...]
    dqp[...] = (x * cos[...] - partner(x) * sin[...]).astype(BF16)
    x = dk_s[...]
    dkp[...] = (x * cos[...] - partner(x) * sin[...]).astype(BF16)
    dv[...] = dv_s[...].astype(BF16)


def attn_specs(hd, rows):
    width = GROUP * HEAD_SIZE
    wide = pl.BlockSpec((ROW, width), lambda r, g: (r, g))
    col = pl.BlockSpec((ROW, 1), lambda r, g: (r, 0))
    row = pl.BlockSpec((1, ROW), lambda r, g: (0, r))
    table = pl.BlockSpec((ROW, width), lambda r, g: (0, 0))
    return wide, col, row, table, (rows // ROW, hd // width), width


def attention(qp, kp, v, seg, obs, tables):
    rows, hd = qp.shape
    wide, col, row, table, grid, width = attn_specs(hd, rows)
    out = jax.ShapeDtypeStruct((rows, hd), BF16)
    return pl.pallas_call(
        attn_fwd_kernel,
        grid=grid,
        in_specs=[wide, wide, wide, col, row, row, table, table],
        out_specs=[wide, wide, wide],
        out_shape=[out, out, out],
        compiler_params=pltpu.CompilerParams(vmem_limit_bytes=40 * 2**20),
        cost_estimate=pl.CostEstimate(flops=rows * hd * 2048, bytes_accessed=rows * hd * 16, transcendentals=rows * 4096),
    )(qp, kp, v, seg[:, None], seg[None, :], obs[None, :], *tables)


def attention_back(q, k, v, do, seg, obs, tables):
    rows, hd = q.shape
    wide, col, row, table, grid, width = attn_specs(hd, rows)
    out = jax.ShapeDtypeStruct((rows, hd), BF16)
    return pl.pallas_call(
        attn_bwd_kernel,
        grid=grid,
        in_specs=[wide, wide, wide, wide, col, row, row, table, table],
        out_specs=[wide, wide, wide],
        out_shape=[out, out, out],
        scratch_shapes=[pltpu.VMEM((ROW, width), F32)] * 3,
        compiler_params=pltpu.CompilerParams(vmem_limit_bytes=40 * 2**20),
        cost_estimate=pl.CostEstimate(flops=rows * hd * 5120, bytes_accessed=rows * hd * 14, transcendentals=rows * 4096),
    )(q, k, v, do, seg[:, None], seg[None, :], obs[None, :], *tables)


def forward(x, weights, gains, seg, obs, tables):
    wq, wk, wv, wo, w_in, w_down = weights
    r1 = lax.rsqrt(jnp.mean(x * x, axis=1, keepdims=True) + EPS)
    n1 = (x * r1 * gains[0]).astype(BF16)
    q, k, o = attention(dot_nt(n1, wq), dot_nt(n1, wk), dot_nt(n1, wv).astype(BF16), seg, obs, tables)
    v = dot_nt(n1, wv).astype(BF16)
    h2 = x + dot_nn(o, wo)
    r2 = lax.rsqrt(jnp.mean(h2 * h2, axis=1, keepdims=True) + EPS)
    n2 = (h2 * r2 * gains[1]).astype(BF16)
    us = [dot_nn(n2, w) for w in w_in]
    acts = [(u * lax.logistic(u)).astype(BF16) for u in us]
    out = h2
    for a, w in zip(acts, w_down):
        out = out + dot_nn(a, w)
    return out, (x, r1, n1, q, k, v, o, h2, r2, n2, us, acts)


def norm_back(g, dn, h, r, gain):
    y = gain * dn
    return g + r * y - h * (r * r * r) * jnp.mean(h * y, axis=1, keepdims=True)


def backward(g, kept, weights, gains, seg, obs, tables, with_grads):
    wq, wk, wv, wo, w_in, w_down = weights
    x, r1, n1, q, k, v, o, h2, r2, n2, us, acts = kept
    heads = len(w_in)
    gb = g.astype(BF16)
    dn2 = None
    g_down, g_in = [None] * heads, [None] * heads
    for s in reversed(range(heads)):
        sig = lax.logistic(us[s])
        du = (dot_nt(gb, w_down[s]) * sig * (1.0 + us[s] * (1.0 - sig))).astype(BF16)
        if with_grads:
            g_down[s] = dot_tn(gb, acts[s]).astype(BF16)
            g_in[s] = dot_tn(n2, du).astype(BF16)
        term = dot_nt(du, w_in[s])
        dn2 = term if dn2 is None else dn2 + term
    dh2 = norm_back(g, dn2, h2, r2, gains[1])
    ga = dh2.astype(BF16)
    do = dot_nt(ga, wo).astype(BF16)
    dqp, dkp, dv = attention_back(q, k, v, do, seg, obs, tables)
    dn1 = dot_nn(dqp, wq) + dot_nn(dkp, wk) + dot_nn(dv, wv)
    dh = norm_back(dh2, dn1, x, r1, gains[0])
    if not with_grads:
        return dh, None
    wide = wq.shape[0] // heads
    g_attn = [None] * heads
    parts = [dot_tn(n1, d).astype(BF16) for d in (dqp, dkp, dv)] + [dot_tn(ga, o).astype(BF16)]
    for s in range(heads):
        g_attn[s] = jnp.stack([part[:, s * wide:(s + 1) * wide] for part in parts], axis=1).reshape(wq.shape[1], 4 * wide)
    gain_terms = jnp.stack([jnp.sum(dn1 * x * r1, axis=0), jnp.sum(dn2 * h2 * r2, axis=0)])
    return dh, (g_attn, g_in, g_down, gain_terms)


def bits_of(n):
    return [1 << i for i in range(n.bit_length() - 1)]


def swap(x, axis, bit):
    n = lax.axis_size(axis)
    return lax.ppermute(x, axis, [(i, i ^ bit) for i in range(n)])


def turn(x, axis, step):
    n = lax.axis_size(axis)
    return lax.ppermute(x, axis, [(i, (i + step) % n) for i in range(n)])


def gather_shards(shard):
    n_dp, n_t = lax.axis_size("dp"), lax.axis_size("tensor")
    me = lax.axis_index("dp")
    rows = shard.shape[0] // n_dp
    piece = lax.dynamic_slice_in_dim(shard, me * rows, rows, 0)
    slots = []
    for _ in range(1, n_t):
        piece = turn(piece, "tensor", -1)
        have = {0: piece}
        for bit in reversed(bits_of(n_dp)):
            have.update({j ^ bit: swap(p, "dp", bit) for j, p in list(have.items())})
        slots.append([(me ^ j, p) for j, p in have.items()])
    return rows, slots


def gather_square(shard):
    rows, slots = gather_shards(shard)
    result = [shard]
    for slot in slots:
        full = jnp.zeros(shard.shape, shard.dtype)
        for at, p in slot:
            full = lax.dynamic_update_slice_in_dim(full, p, at * rows, 0)
        result.append(full)
    return result


def gather_heads(stack):
    kinds, hd, d = stack.shape
    n_t = lax.axis_size("tensor")
    rows, slots = gather_shards(stack.reshape(kinds * hd, d))
    full = jnp.zeros((kinds, n_t * hd, d), stack.dtype)
    full = lax.dynamic_update_slice(full, stack, (0, 0, 0))
    for s, slot in enumerate(slots):
        for at, p in slot:
            first = at * rows
            full = lax.dynamic_update_slice(full, p[None], (first // hd, (s + 1) * hd + lax.rem(first, hd), 0))
    return full


def reduce_blocks(parts):
    n_dp, n_t = lax.axis_size("dp"), lax.axis_size("tensor")
    me = lax.axis_index("dp")
    rows = parts[0].shape[0] // n_dp
    total = None
    for s in reversed(range(n_t)):
        term = parts[s].reshape(n_dp, rows, -1)
        for bit in bits_of(n_dp):
            view = term.reshape(-1, 2, rows, term.shape[-1])
            own = jnp.where(me & bit == 0, 0, 1)
            keep = lax.dynamic_index_in_dim(view, own, 1, keepdims=False)
            give = lax.dynamic_index_in_dim(view, 1 - own, 1, keepdims=False)
            term = (keep.astype(F32) + swap(give, "dp", bit).astype(F32)).astype(BF16)
        term = term.reshape(rows, -1)
        if total is not None:
            term = term.astype(F32) + turn(total, "tensor", 1).astype(F32)
            term = term if s == 0 else term.astype(BF16)
        total = term
    return total.astype(F32)


def spread_rows(block):
    n_t = lax.axis_size("tensor")
    me = lax.axis_index("tensor")
    full = jnp.zeros((n_t,) + block.shape, block.dtype)
    piece = block
    for s in range(n_t):
        full = lax.dynamic_update_slice(full, piece[None], (lax.rem(me + s, n_t), 0, 0))
        if s + 1 < n_t:
            piece = turn(piece, "tensor", -1)
    return full.reshape(n_t * block.shape[0], block.shape[1])


def own_rows(x, count):
    flat = x.reshape((-1,) + x.shape[2:])
    return lax.dynamic_slice_in_dim(flat, lax.axis_index("tensor") * count, count, 0)


def on_device(tokens, cotangent, seg_ids, observed, w_qkv, w_out, w_in, w_down, norm_gains):
    n_dp, n_t = lax.axis_size("dp"), lax.axis_size("tensor")
    w_qkv, w_out, w_in, w_down, gains = w_qkv[0], w_out[0], w_in[0], w_down[0], norm_gains[0]
    micro, rows, d = tokens.shape
    hd = w_out.shape[0]
    count = micro * rows // n_t
    is_first = lax.axis_index("section") == 0
    tables = rope_tables()

    heads = gather_heads(jnp.concatenate([jnp.swapaxes(w_qkv, 1, 2), w_out[None]], axis=0))
    weights = (heads[0], heads[1], heads[2], heads[3], gather_square(w_in), gather_square(w_down))

    x0 = own_rows(tokens, count)
    g1 = own_rows(cotangent, count)
    seg, obs = own_rows(seg_ids, count), own_rows(observed, count)

    out0, _ = forward(x0.astype(F32), weights, gains, seg, obs, tables)
    arriving = lax.ppermute(out0.astype(BF16), "section", [(0, 1)])
    x1 = jnp.where(is_first, x0, arriving)
    out1, kept = forward(x1.astype(F32), weights, gains, seg, obs, tables)
    layer_acts = spread_rows(out1.astype(BF16))
    dh1, _ = backward(g1.astype(F32), kept, weights, gains, seg, obs, tables, False)
    upstream = lax.ppermute(dh1.astype(BF16), "section", [(1, 0)])
    g0 = jnp.where(is_first, upstream, g1)
    dh0, (g_attn, g_in, g_down, gain_terms) = backward(g0.astype(F32), kept, weights, gains, seg, obs, tables, True)
    grad_acts = spread_rows(dh0.astype(BF16))

    r_down = reduce_blocks(g_down)
    r_in = reduce_blocks(g_in)
    r_attn = reduce_blocks(g_attn)
    r_gain = lax.psum(gain_terms, ("tensor", "dp"))
    piece = d // n_dp
    r_gain = lax.dynamic_slice_in_dim(r_gain, lax.axis_index("dp") * piece, piece, 1)
    r_qkv = jnp.stack([r_attn[:, i * hd:(i + 1) * hd] for i in range(3)])
    r_out = r_attn[:, 3 * hd:].T
    return (
        layer_acts.reshape(1, micro, rows, d),
        grad_acts.reshape(1, micro, rows, d),
        r_qkv[None],
        r_out[None],
        r_in[None],
        r_down.T[None],
        r_gain[None],
    )


def solution(mesh):
    return jax.shard_map(
        on_device,
        mesh=mesh,
        in_specs=(
            P(None, "dp", None),
            P(None, "dp", None),
            P(None, "dp"),
            P(None, "dp"),
            P("section", None, None, "tensor"),
            P("section", "tensor", None),
            P("section", None, "tensor"),
            P("section", "tensor", None),
            P("section", None, None),
        ),
        out_specs=(
            P("section", None, "dp", None),
            P("section", None, "dp", None),
            P("section", None, "dp", "tensor"),
            P("section", "tensor", "dp"),
            P("section", "dp", "tensor"),
            P("section", "tensor", "dp"),
            P("section", None, "dp"),
        ),
        check_vma=False,
    )
```

```python
import functools
import math

import jax
import jax.numpy as jnp
from jax import lax
from jax.experimental import pallas as pl
from jax.experimental.pallas import tpu as pltpu
from jax.sharding import PartitionSpec as P

HEAD_SIZE = 80
HALF = HEAD_SIZE // 2
ROW = 512
QB = 128
GROUP = 8
EPS = 1e-06
BIG = 1000000000.0
SCALE = 1.0 / math.sqrt(HEAD_SIZE)
BF16 = jnp.bfloat16
F32 = jnp.float32
MESH = pl.DeviceIdType.MESH


def dot_nn(a, b):
    return lax.dot_general(a, b, (((1,), (0,)), ((), ())), preferred_element_type=F32)


def dot_nt(a, b):
    return lax.dot_general(a, b, (((1,), (1,)), ((), ())), preferred_element_type=F32)


def dot_tn(a, b):
    return lax.dot_general(a, b, (((0,), (0,)), ((), ())), preferred_element_type=F32)


def rope_tables():
    freq = 10000.0 ** (-jnp.arange(HALF, dtype=F32) / HALF)
    ang = jnp.arange(ROW, dtype=F32)[:, None] * freq[None, :]
    cos, sin = jnp.cos(ang), jnp.sin(ang)
    cos_full = jnp.tile(jnp.concatenate([cos, cos], axis=1), (1, GROUP))
    sin_full = jnp.tile(jnp.concatenate([-sin, sin], axis=1), (1, GROUP))
    return cos_full, sin_full


def partner(x):
    width = x.shape[1]
    lane = lax.broadcasted_iota(jnp.int32, x.shape, 1)
    first = lax.rem(lane, HEAD_SIZE) < HALF
    return jnp.where(first, pltpu.roll(x, width - HALF, 1), pltpu.roll(x, HALF, 1))


def windows():
    return [max(i - 1, 0) * QB for i in range(ROW // QB)]


def write_mask(mask, seg_col, seg_row, obs_row):
    for i, k0 in enumerate(windows()):
        r = slice(i * QB, (i + 1) * QB)
        shape = (QB, 2 * QB)
        qi = lax.broadcasted_iota(jnp.int32, shape, 0) + i * QB
        kj = lax.broadcasted_iota(jnp.int32, shape, 1) + k0
        same = seg_col[r, :] == seg_row[:, k0:k0 + 2 * QB]
        seen = (obs_row[:, k0:k0 + 2 * QB] == 1) | (kj == qi)
        mask[r, :] = (same & (kj <= qi) & seen).astype(F32)


def by_block(dot, left, right):
    return jnp.concatenate(
        [dot(left[i * QB:(i + 1) * QB], right[k0:k0 + 2 * QB]) for i, k0 in enumerate(windows())], axis=0
    )


def by_window(left, right):
    n = ROW // QB
    blocks = [None] * n
    for i, k0 in enumerate(windows()):
        r = slice(i * QB, (i + 1) * QB)
        term = dot_tn(left[r], right[r])
        for j in range(2):
            at, part = k0 // QB + j, term[j * QB:(j + 1) * QB]
            blocks[at] = part if blocks[at] is None else blocks[at] + part
    return jnp.concatenate(blocks, axis=0)


def probabilities(q, k, mask):
    s = jnp.where(mask[...] > 0, by_block(dot_nt, q, k) * SCALE, -BIG)
    e = jnp.exp(s - jnp.max(s, axis=1, keepdims=True))
    return e * (1.0 / jnp.sum(e, axis=1, keepdims=True))


def attn_fwd_kernel(qp, kp, v, seg_col, seg_row, obs_row, cos, sin, q_out, k_out, o_out, mask):
    x = qp[...]
    q_out[...] = (x * cos[...] + partner(x) * sin[...]).astype(BF16)
    x = kp[...]
    k_out[...] = (x * cos[...] + partner(x) * sin[...]).astype(BF16)
    write_mask(mask, seg_col, seg_row, obs_row)
    for h in range(GROUP):
        c = slice(h * HEAD_SIZE, (h + 1) * HEAD_SIZE)
        p = probabilities(q_out[:, c], k_out[:, c], mask).astype(BF16)
        o_out[:, c] = by_block(dot_nn, p, v[:, c]).astype(BF16)


def attn_bwd_kernel(q, k, v, do, seg_col, seg_row, obs_row, cos, sin, dqp, dkp, dv, dq_s, dk_s, mask):
    write_mask(mask, seg_col, seg_row, obs_row)
    for h in range(GROUP):
        c = slice(h * HEAD_SIZE, (h + 1) * HEAD_SIZE)
        qh, kh, vh, dh = q[:, c], k[:, c], v[:, c], do[:, c]
        p = probabilities(qh, kh, mask)
        dv[:, c] = by_window(p.astype(BF16), dh).astype(BF16)
        dp = by_block(dot_nt, dh, vh)
        ds = (p * (dp - jnp.sum(p * dp, axis=1, keepdims=True))).astype(BF16)
        dq_s[:, c] = by_block(dot_nn, ds, kh) * SCALE
        dk_s[:, c] = by_window(ds, qh) * SCALE
    x = dq_s[...]
    dqp[...] = (x * cos[...] - partner(x) * sin[...]).astype(BF16)
    x = dk_s[...]
    dkp[...] = (x * cos[...] - partner(x) * sin[...]).astype(BF16)


def attn_specs(hd, rows):
    width = GROUP * HEAD_SIZE
    wide = pl.BlockSpec((ROW, width), lambda r, g: (r, g))
    col = pl.BlockSpec((ROW, 1), lambda r, g: (r, 0))
    row = pl.BlockSpec((1, ROW), lambda r, g: (0, r))
    table = pl.BlockSpec((ROW, width), lambda r, g: (0, 0))
    return wide, col, row, table, (rows // ROW, hd // width), width


def attention(qp, kp, v, seg, obs, tables):
    rows, hd = qp.shape
    wide, col, row, table, grid, width = attn_specs(hd, rows)
    out = jax.ShapeDtypeStruct((rows, hd), BF16)
    return pl.pallas_call(
        attn_fwd_kernel,
        grid=grid,
        in_specs=[wide, wide, wide, col, row, row, table, table],
        out_specs=[wide, wide, wide],
        out_shape=[out, out, out],
        scratch_shapes=[pltpu.VMEM((ROW, 2 * QB), F32)],
        compiler_params=pltpu.CompilerParams(vmem_limit_bytes=40 * 2**20),
        cost_estimate=pl.CostEstimate(flops=rows * hd * 2048, bytes_accessed=rows * hd * 16, transcendentals=rows * 4096),
    )(qp, kp, v, seg[:, None], seg[None, :], obs[None, :], *tables)


def attention_back(q, k, v, do, seg, obs, tables):
    rows, hd = q.shape
    wide, col, row, table, grid, width = attn_specs(hd, rows)
    out = jax.ShapeDtypeStruct((rows, hd), BF16)
    return pl.pallas_call(
        attn_bwd_kernel,
        grid=grid,
        in_specs=[wide, wide, wide, wide, col, row, row, table, table],
        out_specs=[wide, wide, wide],
        out_shape=[out, out, out],
        scratch_shapes=[pltpu.VMEM((ROW, width), F32)] * 2 + [pltpu.VMEM((ROW, 2 * QB), F32)],
        compiler_params=pltpu.CompilerParams(vmem_limit_bytes=40 * 2**20),
        cost_estimate=pl.CostEstimate(flops=rows * hd * 5120, bytes_accessed=rows * hd * 14, transcendentals=rows * 4096),
    )(q, k, v, do, seg[:, None], seg[None, :], obs[None, :], *tables)


def forward(x, weights, gains, seg, obs, tables):
    wq, wk, wv, wo, w_in, w_down = weights
    r1 = lax.rsqrt(jnp.mean(x * x, axis=1, keepdims=True) + EPS)
    n1 = (x * r1 * gains[0]).astype(BF16)
    q, k, o = attention(dot_nt(n1, wq), dot_nt(n1, wk), dot_nt(n1, wv).astype(BF16), seg, obs, tables)
    v = dot_nt(n1, wv).astype(BF16)
    h2 = x + dot_nn(o, wo)
    r2 = lax.rsqrt(jnp.mean(h2 * h2, axis=1, keepdims=True) + EPS)
    n2 = (h2 * r2 * gains[1]).astype(BF16)
    us = [dot_nn(n2, w) for w in w_in]
    acts = [(u * lax.logistic(u)).astype(BF16) for u in us]
    out = h2
    for a, w in zip(acts, w_down):
        out = out + dot_nn(a, w)
    return out, (x, r1, n1, q, k, v, o, h2, r2, n2, us, acts)


def norm_back(g, dn, h, r, gain):
    y = gain * dn
    return g + r * y - h * (r * r * r) * jnp.mean(h * y, axis=1, keepdims=True)


def backward(g, kept, weights, gains, seg, obs, tables, with_grads):
    wq, wk, wv, wo, w_in, w_down = weights
    x, r1, n1, q, k, v, o, h2, r2, n2, us, acts = kept
    heads = len(w_in)
    gb = g.astype(BF16)
    dn2 = None
    g_down, g_in = [None] * heads, [None] * heads
    for s in reversed(range(heads)):
        sig = lax.logistic(us[s])
        du = (dot_nt(gb, w_down[s]) * sig * (1.0 + us[s] * (1.0 - sig))).astype(BF16)
        if with_grads:
            g_down[s] = dot_tn(gb, acts[s]).astype(BF16)
            g_in[s] = dot_tn(n2, du).astype(BF16)
        term = dot_nt(du, w_in[s])
        dn2 = term if dn2 is None else dn2 + term
    dh2 = norm_back(g, dn2, h2, r2, gains[1])
    ga = dh2.astype(BF16)
    do = dot_nt(ga, wo).astype(BF16)
    dqp, dkp, dv = attention_back(q, k, v, do, seg, obs, tables)
    dn1 = dot_nn(dqp, wq) + dot_nn(dkp, wk) + dot_nn(dv, wv)
    dh = norm_back(dh2, dn1, x, r1, gains[0])
    if not with_grads:
        return dh, None
    wide = wq.shape[0] // heads
    g_attn = [None] * heads
    parts = [dot_tn(n1, d).astype(BF16) for d in (dqp, dkp, dv)] + [dot_tn(ga, o).astype(BF16)]
    for s in range(heads):
        g_attn[s] = jnp.stack([part[:, s * wide:(s + 1) * wide] for part in parts], axis=1).reshape(wq.shape[1], 4 * wide)
    gain_terms = jnp.stack([jnp.sum(dn1 * x * r1, axis=0), jnp.sum(dn2 * h2 * r2, axis=0)])
    return dh, (g_attn, g_in, g_down, gain_terms)


def ring_bits(n):
    return [1 << i for i in range(n.bit_length() - 1)]


def low_bit(j):
    return j & -j


class Links:
    def __init__(self, n_dp, n_t):
        self.n_dp, self.n_t = n_dp, n_t
        self.me, self.z = lax.axis_index("dp"), lax.axis_index("tensor")
        self.down = lax.rem(self.z + n_t - 1, n_t)
        self.up = lax.rem(self.z + 1, n_t)
        self.bits = ring_bits(n_dp)
        self.sent = {}

    def flip(self, bit):
        return self.me + bit - 2 * bit * lax.rem(self.me // bit, 2)

    def mix(self, j):
        at = self.me
        for bit in self.bits:
            if j & bit:
                at = at + bit - 2 * bit * lax.rem(self.me // bit, 2)
        return at

    def own_bit(self, bit):
        return lax.rem(self.me // bit, 2)

    def greet(self, axes):
        barrier = pltpu.get_barrier_semaphore()
        for where in axes:
            pl.semaphore_signal(barrier, inc=1, device_id=where, device_id_type=MESH)
        pl.semaphore_wait(barrier, len(axes))

    def send(self, src, dst, send_sem, recv_sem, where, tag=None):
        copy = pltpu.make_async_remote_copy(
            src_ref=src, dst_ref=dst, send_sem=send_sem, recv_sem=recv_sem, device_id=where, device_id_type=MESH
        )
        copy.start()
        self.sent.setdefault(tag, []).append(copy)

    def finish(self, tag):
        for copy in self.sent.pop(tag, ()):
            copy.wait_send()

    def arrived(self, ref, sem, send_sem, where):
        pltpu.make_async_remote_copy(
            src_ref=ref, dst_ref=ref, send_sem=send_sem, recv_sem=sem, device_id=where, device_id_type=MESH
        ).wait_recv()

    def drain(self):
        for tag in list(self.sent):
            self.finish(tag)


class Gather:
    def __init__(self, links, own, full, z_send, z_recv, p_send, p_recv):
        self.l, self.own, self.full = links, own, full
        self.z_send, self.z_recv, self.p_send, self.p_recv = z_send, z_recv, p_send, p_recv
        self.rows = own[0].shape[0] // links.n_dp
        self.split, self.units = gather_units(self.rows, links.n_t)
        self.part = self.rows // self.split
        self.at = {u: i for i, u in enumerate(self.units)}
        self.next = 0

    def piece(self, m, slot, index, h):
        first = pl.multiple_of(index * self.rows + h * self.part, 16)
        if slot == 0:
            return self.own[m].at[pl.ds(first, self.part), :]
        return self.full.at[m, slot, pl.ds(first, self.part), :]

    def send_z(self, i):
        m, k, h = self.units[i]
        l = self.l
        l.send(self.piece(m, k - 1, l.me, h), self.piece(m, k, l.me, h), self.z_send.at[i], self.z_recv.at[i], {"tensor": l.down})

    def advance(self, seen, ahead=3):
        while self.next < len(self.units) and self.next <= seen + ahead:
            m, k, h = self.units[self.next]
            if k > 1 and self.at[(m, k - 1, h)] > seen:
                break
            self.send_z(self.next)
            self.next += 1

    def share(self, i, j):
        m, k, h = self.units[i]
        l = self.l
        for bit in reversed(l.bits):
            if j == 0 or bit < low_bit(j):
                ref = self.piece(m, k, l.mix(j), h)
                l.send(ref, ref, self.p_send.at[i, j ^ bit], self.p_recv.at[i, j ^ bit], {"dp": l.flip(bit)})

    def take(self, i):
        m, k, h = self.units[i]
        l = self.l
        l.arrived(self.piece(m, k, l.me, h), self.z_recv.at[i], self.z_send.at[i], {"tensor": l.up})
        self.advance(i)
        self.share(i, 0)

    def order(self):
        return sorted(range(1, self.l.n_dp), key=lambda j: (-low_bit(j), j))

    def relay(self, i):
        m, k, h = self.units[i]
        l = self.l
        for j in self.order():
            l.arrived(self.piece(m, k, l.mix(j), h), self.p_recv.at[i, j], self.p_send.at[i, j], {"dp": l.flip(low_bit(j))})
            self.share(i, j)


def gather_units(rows, n_t):
    split = 2 if rows % 32 == 0 else 1
    units = [(0, k, h) for k in range(1, n_t) for h in range(split)]
    units += [(m, k, h) for k in range(1, n_t) for m in (1, 2) for h in range(split)]
    return split, units


def gather_kernel(n_dp, n_t, a_own, i_own, d_own, full, local, z_send, z_recv, p_send, p_recv):
    l = Links(n_dp, n_t)
    g = Gather(l, (a_own, i_own, d_own), full, z_send, z_recv, p_send, p_recv)
    l.greet([{"tensor": l.up}] + [{"dp": l.flip(b)} for b in l.bits])
    g.advance(-1)
    copies = [pltpu.make_async_copy(g.own[m], full.at[m, 0], local.at[m]) for m in range(3)]
    for c in copies:
        c.start()
    lag = 2
    for i in range(len(g.units) + lag):
        if i < len(g.units):
            g.take(i)
        if i >= lag:
            g.relay(i - lag)
    for c in copies:
        c.wait()
    l.drain()


def gather_weights(a_own, i_own, d_own):
    n_dp, n_t = lax.axis_size("dp"), lax.axis_size("tensor")
    count = len(gather_units(a_own.shape[0] // n_dp, n_t)[1])
    dma = pltpu.SemaphoreType.DMA
    return pl.pallas_call(
        functools.partial(gather_kernel, n_dp, n_t),
        out_shape=jax.ShapeDtypeStruct((3, n_t) + a_own.shape, a_own.dtype),
        in_specs=[pl.BlockSpec(memory_space=pl.ANY)] * 3,
        out_specs=pl.BlockSpec(memory_space=pl.ANY),
        scratch_shapes=[dma((3,)), dma((count,)), dma((count,)), dma((count, n_dp)), dma((count, n_dp))],
        compiler_params=pltpu.CompilerParams(collective_id=0, has_side_effects=True),
    )(a_own, i_own, d_own)


def level_start(n_dp, level):
    return sum(n_dp >> (t + 1) for t in range(level))


def add_rows(out, *terms):
    rows = out.shape[0]

    def body(r, _):
        at = pl.ds(pl.multiple_of(r * 16, 16), 16)
        total = terms[0][at, :].astype(F32)
        for t in terms[1:]:
            total = total + t[at, :].astype(F32)
        out[at, :] = total.astype(out.dtype)
        return 0

    lax.fori_loop(0, rows // 16, body, 0)


REDUCE_REFS = 19


def reduce_scratch(n_dp, n_t, count, rows, c):
    dma = pltpu.SemaphoreType.DMA
    half = n_dp // 2
    return [
        pltpu.VMEM((3, n_dp, rows, c), BF16),
        pltpu.VMEM((2, half, rows, c), BF16),
        pltpu.VMEM((2, half, rows, c), BF16),
        pltpu.VMEM((2, 3, rows, c), BF16),
        pltpu.VMEM((3, rows, c), BF16),
        pltpu.VMEM((rows, c), F32),
        dma((count, n_dp)),
        dma((count, n_dp)),
        dma((count,)),
        dma((count,)),
        dma((2,)),
        dma((2,)),
        dma((2, 3)),
        dma(()),
    ]


def reduce_hbm(n_dp, n_t, count, rows, c):
    return [
        jax.ShapeDtypeStruct((count, n_dp // 2, rows, c), BF16),
        jax.ShapeDtypeStruct((count, n_dp - 1, rows, c), BF16),
        jax.ShapeDtypeStruct((count, rows, c), BF16),
    ]


class Reduce:
    def __init__(self, links, order, out, hbm, scratch):
        self.l, self.order, self.out = links, order, out
        self.sums, self.got, self.ring = hbm
        (self.block, self.fetched, self.half, self.terms, self.moving, self.final,
         self.c_send, self.c_recv, self.z_send, self.z_recv,
         self.f_sem, self.s_sem, self.t_sem, self.o_sem) = scratch
        self.at = {o: i for i, o in enumerate(order)}
        self.levels = len(links.bits)
        self.under_way = {}
        self.storing = False

    def before(self, i):
        m, s = self.order[i]
        return self.at.get((m, s + 1))

    def offsets(self, level):
        bits = self.l.bits[level + 1:]
        return [sum(b for n, b in enumerate(bits) if k >> n & 1) for k in range(1 << len(bits))]

    def mine(self, level):
        return lax.rem(self.l.me, 1 << (level + 1))

    def give(self, i, level, source):
        l, bit = self.l, self.l.bits[level]
        there = self.mine(level) + bit - 2 * bit * l.own_bit(bit)
        for n, off in enumerate(self.offsets(level)):
            at = (i, level_start(l.n_dp, level) + n)
            l.send(source(there + off), self.got.at[at], self.c_send.at[at], self.c_recv.at[at], {"dp": l.flip(bit)}, (i, level))

    def receive(self, i, level):
        l = self.l
        for n, _ in enumerate(self.offsets(level)):
            at = (i, level_start(l.n_dp, level) + n)
            l.arrived(self.got.at[at], self.c_recv.at[at], self.c_send.at[at], {"dp": l.flip(l.bits[level])})

    def clear(self, i):
        self.l.finish((i - 3, 0))

    def give_block(self, i):
        self.give(i, 0, lambda piece: self.block.at[i % 3, piece])

    def fetch_copy(self, i):
        return pltpu.make_async_copy(self.got.at[i, pl.ds(0, self.l.n_dp // 2)], self.fetched.at[i % 2], self.f_sem.at[i % 2])

    def fetch(self, i):
        self.receive(i, 0)
        self.fetch_copy(i).start()

    def store_copy(self, i):
        return pltpu.make_async_copy(self.half.at[i % 2], self.sums.at[i], self.s_sem.at[i % 2])

    def add_first(self, i):
        self.fetch_copy(i).wait()
        for n in range(self.l.n_dp // 2):
            add_rows(self.half.at[i % 2, n], self.block.at[i % 3, 2 * n + self.l.own_bit(1)], self.fetched.at[i % 2, n])
        self.store_copy(i).start()

    def give_next(self, i):
        self.store_copy(i).wait()
        self.give(i, 1, lambda piece: self.sums.at[i, piece // 2])

    def steps(self, i):
        count = len(self.order)
        if i < count:
            self.give_block(i)
        if 0 <= i - 1 < count:
            self.fetch(i - 1)
        if 0 <= i - 2 < count:
            self.add_first(i - 2)
        if 0 <= i - 3 < count:
            self.give_next(i - 3)

    def middle(self, i, level):
        l = self.l
        self.receive(i, level)
        for n, off in enumerate(self.offsets(level)):
            piece = (self.mine(level) + off) // 2
            loads = [
                pltpu.make_async_copy(self.sums.at[i, piece], self.terms.at[0, 0], self.t_sem.at[0, 0]),
                pltpu.make_async_copy(self.got.at[i, level_start(l.n_dp, level) + n], self.terms.at[0, 1], self.t_sem.at[0, 1]),
            ]
            for c in loads:
                c.start()
            for c in loads:
                c.wait()
            add_rows(self.terms.at[0, 2], self.terms.at[0, 0], self.terms.at[0, 1])
            back = pltpu.make_async_copy(self.terms.at[0, 2], self.sums.at[i, piece], self.t_sem.at[0, 2])
            back.start()
            back.wait()
        self.give(i, level + 1, lambda piece: self.sums.at[i, piece // 2])

    def term_copies(self, i):
        l = self.l
        return [
            pltpu.make_async_copy(self.sums.at[i, l.me // 2], self.terms.at[i % 2, 0], self.t_sem.at[i % 2, 0]),
            pltpu.make_async_copy(self.got.at[i, l.n_dp - 2], self.terms.at[i % 2, 1], self.t_sem.at[i % 2, 1]),
        ]

    def ring_copy(self, i):
        return pltpu.make_async_copy(self.ring.at[self.before(i)], self.terms.at[i % 2, 2], self.t_sem.at[i % 2, 2])

    def collect(self, i):
        self.receive(i, self.levels - 1)
        for c in self.term_copies(i):
            c.start()

    def out_copy(self, m):
        return pltpu.make_async_copy(self.final, self.out.at[m], self.o_sem)

    def pass_on(self, i):
        l = self.l
        m, s = self.order[i]
        b = self.before(i)
        if b is not None:
            l.arrived(self.ring.at[b], self.z_recv.at[b], self.z_send.at[b], {"tensor": l.down})
            self.ring_copy(i).start()
        for c in self.term_copies(i):
            c.wait()
        if b is not None:
            self.ring_copy(i).wait()
        terms = [self.terms.at[i % 2, t] for t in range(2 if b is None else 3)]
        l.finish(("z", i - 3))
        if s > 0:
            add_rows(self.moving.at[i % 3], *terms)
            l.send(self.moving.at[i % 3], self.ring.at[i], self.z_send.at[i], self.z_recv.at[i], {"tensor": l.up}, ("z", i))
        else:
            if self.storing is not False:
                self.out_copy(self.storing).wait()
            add_rows(self.final, *terms)
            self.out_copy(m).start()
            self.storing = m

    def last_steps(self, i):
        count = len(self.order)
        if i < count:
            for level in range(1, self.levels - 1):
                self.middle(i, level)
            self.collect(i)
        if 0 <= i - 1 < count:
            self.pass_on(i - 1)

    def close(self):
        self.out_copy(self.storing).wait()


class Spread:
    def __init__(self, links, block, out, send, recv, local):
        self.l, self.block, self.out, self.send, self.recv = links, block, out, send, recv
        self.copy = pltpu.make_async_copy(block, out.at[links.z], local)

    def start(self):
        self.copy.start()
        l = self.l
        l.send(self.block, self.out.at[l.z], self.send.at[0], self.recv.at[0], {"tensor": l.down})

    def step(self, k):
        l = self.l
        at = lax.rem(l.z + k, l.n_t)
        l.arrived(self.out.at[at], self.recv.at[k - 1], self.send.at[k - 1], {"tensor": l.up})
        if k < l.n_t - 1:
            l.send(self.out.at[at], self.out.at[at], self.send.at[k], self.recv.at[k], {"tensor": l.down})

    def close(self):
        self.copy.wait()


class Total:
    def __init__(self, links, block, buf, send, recv):
        self.l, self.block, self.buf, self.s, self.r = links, block, buf, send, recv
        self.levels = len(links.bits)
        self.count = self.levels + links.n_t

    def step(self, s):
        l, buf = self.l, self.buf
        if s == 0:
            buf[1] = self.block[...]
        else:
            l.arrived(buf.at[2 * s], self.r.at[s - 1], self.s.at[s - 1], {"tensor": l.up})
            if s <= self.levels:
                buf[2 * s + 1] = buf[2 * s - 1] + buf[2 * s]
        if s < self.levels:
            l.send(buf.at[2 * s + 1], buf.at[2 * s + 2], self.s.at[s], self.r.at[s], {"dp": l.flip(l.bits[s])})
        elif s < self.count - 1:
            src = 2 * s + 1 if s == self.levels else 2 * s
            l.send(buf.at[src], buf.at[2 * s + 2], self.s.at[s], self.r.at[s], {"tensor": l.down})

    def result(self):
        total = self.buf[2 * self.levels + 1]
        for k in range(1, self.l.n_t):
            total = total + self.buf[2 * (self.levels + k)]
        return total


def reduce_kernel(n_dp, n_t, blocks, acts, gains, out_acts, out_sums, out_gains, *refs):
    l = Links(n_dp, n_t)
    hbm, scratch, rest = refs[:3], refs[3:17], refs[17:]
    gain_buf, g_send, g_recv, a_send, a_recv, a_local, b_sem = rest
    count = blocks.shape[0]
    mats = count // n_t
    order = [(m, s) for m in range(mats) for s in reversed(range(n_t))]
    r = Reduce(l, order, out_sums, hbm, scratch)
    spread = Spread(l, acts, out_acts, a_send, a_recv, a_local)
    total = Total(l, gains, gain_buf, g_send, g_recv)
    l.greet([{"tensor": l.up}, {"tensor": l.down}] + [{"dp": l.flip(b)} for b in l.bits])
    spread.start()

    def load(i):
        return pltpu.make_async_copy(blocks.at[i], r.block.at[i % 3], b_sem.at[i % 3])

    load(0).start()
    extra = 3
    for i in range(count + extra):
        if i < count:
            load(i).wait()
        r.steps(i)
        if i + 1 < count:
            if i + 1 >= 3:
                r.clear(i + 1)
            load(i + 1).start()
        if i < total.count:
            total.step(i)
    for i in range(count + 1):
        r.last_steps(i)
        if i % 3 == 2 and 1 + i // 3 < n_t:
            spread.step(1 + i // 3)
    out_gains[...] = total.result()
    r.close()
    spread.close()
    l.drain()


def reduce_all(blocks, acts, gains):
    n_dp, n_t = lax.axis_size("dp"), lax.axis_size("tensor")
    count, _, rows, c = blocks.shape
    mats = count // n_t
    steps = len(ring_bits(n_dp)) + n_t
    dma = pltpu.SemaphoreType.DMA
    hbm, vmem = pl.BlockSpec(memory_space=pl.ANY), pl.BlockSpec(memory_space=pltpu.VMEM)
    out = pl.pallas_call(
        functools.partial(reduce_kernel, n_dp, n_t),
        out_shape=[
            jax.ShapeDtypeStruct((n_t,) + acts.shape, BF16),
            jax.ShapeDtypeStruct((mats, rows, c), F32),
            jax.ShapeDtypeStruct(gains.shape, F32),
        ] + reduce_hbm(n_dp, n_t, count, rows, c),
        in_specs=[hbm, hbm, vmem],
        out_specs=[hbm, hbm, vmem, hbm, hbm, hbm],
        scratch_shapes=reduce_scratch(n_dp, n_t, count, rows, c) + [
            pltpu.VMEM((2 * steps,) + gains.shape, F32),
            dma((steps,)), dma((steps,)), dma((n_t,)), dma((n_t,)), dma(()), dma((3,)),
        ],
        compiler_params=pltpu.CompilerParams(collective_id=1, has_side_effects=True, vmem_limit_bytes=60 * 2**20),
    )(blocks, acts, gains)
    return out[0], out[1], out[2]


def turn(x, axis, step):
    n = lax.axis_size(axis)
    return lax.ppermute(x, axis, [(i, (i + step) % n) for i in range(n)])


def spread_rows(block):
    n_t = lax.axis_size("tensor")
    me = lax.axis_index("tensor")
    full = jnp.zeros((n_t,) + block.shape, block.dtype)
    piece = block
    for s in range(n_t):
        full = lax.dynamic_update_slice(full, piece[None], (lax.rem(me + s, n_t), 0, 0))
        if s + 1 < n_t:
            piece = turn(piece, "tensor", -1)
    return full.reshape(n_t * block.shape[0], block.shape[1])


def own_rows(x, count):
    flat = x.reshape((-1,) + x.shape[2:])
    return lax.dynamic_slice_in_dim(flat, lax.axis_index("tensor") * count, count, 0)


def on_device(tokens, cotangent, seg_ids, observed, w_qkv, w_out, w_in, w_down, norm_gains):
    n_dp, n_t = lax.axis_size("dp"), lax.axis_size("tensor")
    w_qkv, w_out, w_in, w_down, gains = w_qkv[0], w_out[0], w_in[0], w_down[0], norm_gains[0]
    micro, rows, d = tokens.shape
    hd = w_out.shape[0]
    count = micro * rows // n_t
    is_first = lax.axis_index("section") == 0
    tables = rope_tables()

    stack = jnp.concatenate([jnp.swapaxes(w_qkv, 1, 2), w_out[None]], axis=0).reshape(4 * hd, d)
    full = gather_weights(stack, w_in, w_down)
    heads = full[0].reshape(n_t, 4, hd, d)
    heads = [heads[:, kind].reshape(n_t * hd, d) for kind in range(4)]
    weights = (*heads, [full[1, s] for s in range(n_t)], [full[2, s] for s in range(n_t)])

    x0 = own_rows(tokens, count)
    g1 = own_rows(cotangent, count)
    seg, obs = own_rows(seg_ids, count), own_rows(observed, count)

    out0, _ = forward(x0.astype(F32), weights, gains, seg, obs, tables)
    arriving = lax.ppermute(out0.astype(BF16), "section", [(0, 1)])
    x1 = jnp.where(is_first, x0, arriving)
    out1, kept = forward(x1.astype(F32), weights, gains, seg, obs, tables)
    layer_acts = spread_rows(out1.astype(BF16))
    dh1, _ = backward(g1.astype(F32), kept, weights, gains, seg, obs, tables, False)
    upstream = lax.ppermute(dh1.astype(BF16), "section", [(1, 0)])
    g0 = jnp.where(is_first, upstream, g1)
    dh0, (g_attn, g_in, g_down, gain_terms) = backward(g0.astype(F32), kept, weights, gains, seg, obs, tables, True)
    piece = d // n_dp
    blocks = [g[s] for g in (g_down, g_in, g_attn) for s in reversed(range(n_t))]
    blocks = jnp.stack(blocks).reshape(3 * n_t, n_dp, piece, -1)
    gains_in = jnp.concatenate([gain_terms, jnp.zeros((6, d), F32)], axis=0)
    grad_acts, (r_down, r_in, r_attn), r_gain = reduce_all(blocks, dh0.astype(BF16), gains_in)
    r_gain = lax.dynamic_slice_in_dim(r_gain[:2], lax.axis_index("dp") * piece, piece, 1)
    r_qkv = jnp.stack([r_attn[:, i * hd:(i + 1) * hd] for i in range(3)])
    r_out = r_attn[:, 3 * hd:].T
    return (
        layer_acts.reshape(1, micro, rows, d),
        grad_acts.reshape(1, micro, rows, d),
        r_qkv[None],
        r_out[None],
        r_in[None],
        r_down.T[None],
        r_gain[None],
    )


def solution(mesh):
    return jax.shard_map(
        on_device,
        mesh=mesh,
        in_specs=(
            P(None, "dp", None),
            P(None, "dp", None),
            P(None, "dp"),
            P(None, "dp"),
            P("section", None, None, "tensor"),
            P("section", "tensor", None),
            P("section", None, "tensor"),
            P("section", "tensor", None),
            P("section", None, None),
        ),
        out_specs=(
            P("section", None, "dp", None),
            P("section", None, "dp", None),
            P("section", None, "dp", "tensor"),
            P("section", "tensor", "dp"),
            P("section", "dp", "tensor"),
            P("section", "tensor", "dp"),
            P("section", None, "dp"),
        ),
        check_vma=False,
    )
```

```python
import functools
import math

import jax
import jax.numpy as jnp
from jax import lax
from jax.experimental import pallas as pl
from jax.experimental.pallas import tpu as pltpu
from jax.sharding import PartitionSpec as P

HEAD_SIZE = 80
HALF = HEAD_SIZE // 2
ROW = 512
QB = 128
GROUP = 8
EPS = 1e-06
BIG = 1000000000.0
SCALE = 1.0 / math.sqrt(HEAD_SIZE)
BF16 = jnp.bfloat16
F32 = jnp.float32
MESH = pl.DeviceIdType.MESH


def dot_nn(a, b):
    return lax.dot_general(a, b, (((1,), (0,)), ((), ())), preferred_element_type=F32)


def dot_nt(a, b):
    return lax.dot_general(a, b, (((1,), (1,)), ((), ())), preferred_element_type=F32)


def dot_tn(a, b):
    return lax.dot_general(a, b, (((0,), (0,)), ((), ())), preferred_element_type=F32)


def rope_tables():
    freq = 10000.0 ** (-jnp.arange(HALF, dtype=F32) / HALF)
    ang = jnp.arange(ROW, dtype=F32)[:, None] * freq[None, :]
    cos, sin = jnp.cos(ang), jnp.sin(ang)
    cos_full = jnp.tile(jnp.concatenate([cos, cos], axis=1), (1, GROUP))
    sin_full = jnp.tile(jnp.concatenate([-sin, sin], axis=1), (1, GROUP))
    return cos_full, sin_full


def partner(x):
    width = x.shape[1]
    lane = lax.broadcasted_iota(jnp.int32, x.shape, 1)
    first = lax.rem(lane, HEAD_SIZE) < HALF
    return jnp.where(first, pltpu.roll(x, width - HALF, 1), pltpu.roll(x, HALF, 1))


def windows():
    return [max(i - 1, 0) * QB for i in range(ROW // QB)]


def write_mask(mask, seg_col, seg_row, obs_row):
    for i, k0 in enumerate(windows()):
        r = slice(i * QB, (i + 1) * QB)
        shape = (QB, 2 * QB)
        qi = lax.broadcasted_iota(jnp.int32, shape, 0) + i * QB
        kj = lax.broadcasted_iota(jnp.int32, shape, 1) + k0
        same = seg_col[r, :] == seg_row[:, k0:k0 + 2 * QB]
        seen = (obs_row[:, k0:k0 + 2 * QB] == 1) | (kj == qi)
        mask[r, :] = (same & (kj <= qi) & seen).astype(F32)


def by_block(dot, left, right):
    return jnp.concatenate(
        [dot(left[i * QB:(i + 1) * QB], right[k0:k0 + 2 * QB]) for i, k0 in enumerate(windows())], axis=0
    )


def by_window(left, right):
    n = ROW // QB
    blocks = [None] * n
    for i, k0 in enumerate(windows()):
        r = slice(i * QB, (i + 1) * QB)
        term = dot_tn(left[r], right[r])
        for j in range(2):
            at, part = k0 // QB + j, term[j * QB:(j + 1) * QB]
            blocks[at] = part if blocks[at] is None else blocks[at] + part
    return jnp.concatenate(blocks, axis=0)


def probabilities(q, k, mask):
    s = jnp.where(mask[...] > 0, by_block(dot_nt, q, k) * SCALE, -BIG)
    e = jnp.exp(s - jnp.max(s, axis=1, keepdims=True))
    return e * (1.0 / jnp.sum(e, axis=1, keepdims=True))


def ring_bits(n):
    return [1 << i for i in range(n.bit_length() - 1)]


def low_bit(j):
    return j & -j


class Links:
    def __init__(self, n_dp, n_t):
        self.n_dp, self.n_t = n_dp, n_t
        self.me, self.z = lax.axis_index("dp"), lax.axis_index("tensor")
        self.down = lax.rem(self.z + n_t - 1, n_t)
        self.up = lax.rem(self.z + 1, n_t)
        self.bits = ring_bits(n_dp)
        self.sent, self.recording = {}, True

    def flip(self, bit):
        return self.me + bit - 2 * bit * lax.rem(self.me // bit, 2)

    def mix(self, j):
        at = self.me
        for bit in self.bits:
            if j & bit:
                at = at + bit - 2 * bit * lax.rem(self.me // bit, 2)
        return at

    def own_bit(self, bit):
        return lax.rem(self.me // bit, 2)

    def greet(self, axes):
        barrier = pltpu.get_barrier_semaphore()
        for where in axes:
            pl.semaphore_signal(barrier, inc=1, device_id=where, device_id_type=MESH)
        pl.semaphore_wait(barrier, len(axes))

    def send(self, src, dst, send_sem, recv_sem, where, tag=None, again=None):
        pltpu.make_async_remote_copy(
            src_ref=src, dst_ref=dst, send_sem=send_sem, recv_sem=recv_sem, device_id=where, device_id_type=MESH
        ).start()
        if self.recording:
            self.sent.setdefault(tag, []).append(again or (lambda: (src, send_sem)))

    def finish(self, tag):
        for again in self.sent.pop(tag, ()):
            ref, sem = again()
            pltpu.make_async_remote_copy(
                src_ref=ref, dst_ref=ref, send_sem=sem, recv_sem=sem, device_id={"tensor": self.down}, device_id_type=MESH
            ).wait_send()

    def arrived(self, ref, sem, send_sem, where):
        pltpu.make_async_remote_copy(
            src_ref=ref, dst_ref=ref, send_sem=send_sem, recv_sem=sem, device_id=where, device_id_type=MESH
        ).wait_recv()

    def drain(self):
        for tag in list(self.sent):
            self.finish(tag)


class Gather:
    def __init__(self, links, own, full, z_send, z_recv, p_send, p_recv):
        self.l, self.own, self.full = links, own, full
        self.z_send, self.z_recv, self.p_send, self.p_recv = z_send, z_recv, p_send, p_recv
        self.rows = own[0].shape[0] // links.n_dp
        self.split, self.units = gather_units(self.rows, links.n_t)
        self.part = self.rows // self.split
        self.at = {u: i for i, u in enumerate(self.units)}

    def piece(self, m, slot, index, h):
        first = pl.multiple_of(index * self.rows + h * self.part, 16)
        if slot == 0:
            return self.own[m].at[pl.ds(first, self.part), :]
        return self.full.at[m, slot, pl.ds(first, self.part), :]

    def send_z(self, m, k, h):
        l = self.l
        i = self.at[(m, k, h)]
        l.send(self.piece(m, k - 1, l.me, h), self.piece(m, k, l.me, h), self.z_send.at[i], self.z_recv.at[i], {"tensor": l.down},
               again=lambda: (self.like(), self.z_send.at[i]))

    def like(self):
        return self.full.at[0, 1, pl.ds(0, self.part), :]

    def start(self):
        for m, k, h in self.units:
            if k == 1:
                self.send_z(m, k, h)

    def share(self, i, j):
        m, k, h = self.units[i]
        l = self.l
        for bit in reversed(l.bits):
            if j == 0 or bit < low_bit(j):
                ref = self.piece(m, k, l.mix(j), h)
                l.send(ref, ref, self.p_send.at[i, j ^ bit], self.p_recv.at[i, j ^ bit], {"dp": l.flip(bit)},
                       again=lambda at=j ^ bit: (self.like(), self.p_send.at[i, at]))

    def take(self, i):
        m, k, h = self.units[i]
        l = self.l
        l.arrived(self.piece(m, k, l.me, h), self.z_recv.at[i], self.z_send.at[i], {"tensor": l.up})
        if k + 1 < l.n_t:
            self.send_z(m, k + 1, h)
        self.share(i, 0)

    def relay(self, i):
        m, k, h = self.units[i]
        l = self.l
        for j in sorted(range(1, l.n_dp), key=lambda j: (-low_bit(j), j)):
            l.arrived(self.piece(m, k, l.mix(j), h), self.p_recv.at[i, j], self.p_send.at[i, j], {"dp": l.flip(low_bit(j))})
            self.share(i, j)

    def walk(self, lag=2):
        for i in range(len(self.units) + lag):
            if i < len(self.units):
                self.take(i)
            if i >= lag:
                self.relay(i - lag)
                yield self.units[i - lag]


def gather_units(rows, n_t):
    split = 2 if rows % 32 == 0 else 1
    return split, [(m, k, h) for k in range(1, n_t) for m in range(3) for h in range(split)]


def level_start(n_dp, level):
    return sum(n_dp >> (t + 1) for t in range(level))


def add_rows(out, *terms):
    rows = out.shape[0]

    def body(r, _):
        at = pl.ds(pl.multiple_of(r * 16, 16), 16)
        total = terms[0][at, :].astype(F32)
        for t in terms[1:]:
            total = total + t[at, :].astype(F32)
        out[at, :] = total.astype(out.dtype)
        return 0

    lax.fori_loop(0, rows // 16, body, 0)


def reduce_scratch(n_dp, n_t, count, rows, c):
    dma = pltpu.SemaphoreType.DMA
    half = n_dp // 2
    return [
        pltpu.VMEM((3, n_dp * rows, c), BF16),
        pltpu.VMEM((2, half, rows, c), BF16),
        pltpu.VMEM((3, rows, c), BF16),
        pltpu.VMEM((3, rows, c), BF16),
        pltpu.VMEM((rows, c), F32),
        dma((count, n_dp)),
        dma((count, n_dp)),
        dma((count,)),
        dma((count,)),
        dma((2,)),
        dma((2,)),
        dma((3,)),
        dma(()),
    ]


def reduce_hbm(n_dp, n_t, count, rows, c):
    return [
        jax.ShapeDtypeStruct((count, n_dp // 2, rows, c), BF16),
        jax.ShapeDtypeStruct((count, n_dp - 1, rows, c), BF16),
        jax.ShapeDtypeStruct((count, rows, c), BF16),
    ]


class Reduce:
    def __init__(self, links, order, out, hbm, scratch):
        self.l, self.order, self.out = links, order, out
        self.sums, self.got, self.ring = hbm
        (self.block, self.fetched, self.terms, self.moving, self.final,
         self.c_send, self.c_recv, self.z_send, self.z_recv,
         self.f_sem, self.s_sem, self.t_sem, self.o_sem) = scratch
        self.at = {o: i for i, o in enumerate(order)}
        self.levels = len(links.bits)
        self.rows = self.fetched.shape[2]
        self.storing = None

    def before(self, i):
        m, s = self.order[i]
        return self.at.get((m, s + 1))

    def offsets(self, level):
        bits = self.l.bits[level + 1:]
        return [sum(b for n, b in enumerate(bits) if k >> n & 1) for k in range(1 << len(bits))]

    def mine(self, level):
        return lax.rem(self.l.me, 1 << (level + 1))

    def give(self, i, level, source):
        l, bit = self.l, self.l.bits[level]
        there = self.mine(level) + bit - 2 * bit * l.own_bit(bit)
        for n, off in enumerate(self.offsets(level)):
            at = (i, level_start(l.n_dp, level) + n)
            l.send(source(there + off), self.got.at[at], self.c_send.at[at], self.c_recv.at[at], {"dp": l.flip(bit)}, (i, level),
                   again=lambda at=at: (self.got.at[at], self.c_send.at[at]))

    def receive(self, i, level):
        l = self.l
        for n, _ in enumerate(self.offsets(level)):
            at = (i, level_start(l.n_dp, level) + n)
            l.arrived(self.got.at[at], self.c_recv.at[at], self.c_send.at[at], {"dp": l.flip(l.bits[level])})

    def clear(self, i):
        self.l.finish((i - 3, 0))

    def piece(self, i, p):
        return self.block.at[i % 3, pl.ds(pl.multiple_of(p * self.rows, 16), self.rows), :]

    def give_block(self, i):
        self.give(i, 0, lambda p: self.piece(i, p))

    def fetch_copy(self, i):
        return pltpu.make_async_copy(self.got.at[i, pl.ds(0, self.l.n_dp // 2)], self.fetched.at[i % 2], self.f_sem.at[i % 2])

    def fetch(self, i):
        self.receive(i, 0)
        self.fetch_copy(i).start()

    def store_copy(self, i):
        return pltpu.make_async_copy(self.fetched.at[i % 2], self.sums.at[i], self.s_sem.at[i % 2])

    def add_first(self, i):
        self.fetch_copy(i).wait()
        for n in range(self.l.n_dp // 2):
            here = self.fetched.at[i % 2, n]
            add_rows(here, self.piece(i, 2 * n + self.l.own_bit(1)), here)
        self.store_copy(i).start()

    def give_next(self, i):
        self.store_copy(i).wait()
        self.give(i, 1, lambda piece: self.sums.at[i, piece // 2])

    def steps(self, i):
        count = len(self.order)
        if i < count:
            self.give_block(i)
        if 0 <= i - 3 < count:
            self.give_next(i - 3)
        if 0 <= i - 1 < count:
            self.fetch(i - 1)
        if 0 <= i - 2 < count:
            self.add_first(i - 2)

    def middle(self, i, level):
        l = self.l
        self.receive(i, level)
        for n, off in enumerate(self.offsets(level)):
            piece = (self.mine(level) + off) // 2
            loads = [
                pltpu.make_async_copy(self.sums.at[i, piece], self.terms.at[0], self.t_sem.at[0]),
                pltpu.make_async_copy(self.got.at[i, level_start(l.n_dp, level) + n], self.terms.at[1], self.t_sem.at[1]),
            ]
            for c in loads:
                c.start()
            for c in loads:
                c.wait()
            add_rows(self.terms.at[2], self.terms.at[0], self.terms.at[1])
            back = pltpu.make_async_copy(self.terms.at[2], self.sums.at[i, piece], self.t_sem.at[2])
            back.start()
            back.wait()
        self.give(i, level + 1, lambda piece: self.sums.at[i, piece // 2])

    def term_copies(self, i):
        l = self.l
        return [
            pltpu.make_async_copy(self.sums.at[i, l.me // 2], self.terms.at[0], self.t_sem.at[0]),
            pltpu.make_async_copy(self.got.at[i, l.n_dp - 2], self.terms.at[1], self.t_sem.at[1]),
        ]

    def ring_copy(self, i):
        return pltpu.make_async_copy(self.ring.at[self.before(i)], self.terms.at[2], self.t_sem.at[2])

    def collect(self, i):
        self.receive(i, self.levels - 1)
        for c in self.term_copies(i):
            c.start()

    def out_copy(self, m):
        return pltpu.make_async_copy(self.final, self.out.at[m], self.o_sem)

    def pass_on(self, i):
        l = self.l
        m, s = self.order[i]
        b = self.before(i)
        if b is not None:
            l.arrived(self.ring.at[b], self.z_recv.at[b], self.z_send.at[b], {"tensor": l.down})
            self.ring_copy(i).start()
        for c in self.term_copies(i):
            c.wait()
        if b is not None:
            self.ring_copy(i).wait()
        terms = [self.terms.at[t] for t in range(2 if b is None else 3)]
        l.finish(("z", i - 3))
        if s > 0:
            add_rows(self.moving.at[i % 3], *terms)
            l.send(self.moving.at[i % 3], self.ring.at[i], self.z_send.at[i], self.z_recv.at[i], {"tensor": l.up}, ("z", i),
                   again=lambda: (self.moving.at[i % 3], self.z_send.at[i]))
        else:
            if self.storing is not None:
                self.out_copy(self.storing).wait()
            add_rows(self.final, *terms)
            self.out_copy(m).start()
            self.storing = m

    def last_step(self, i):
        for level in range(1, self.levels - 1):
            self.middle(i, level)
        self.collect(i)
        self.pass_on(i)

    def close(self):
        self.out_copy(self.storing).wait()


class Spread:
    def __init__(self, links, block, out, send, recv):
        self.l, self.block, self.out, self.send, self.recv = links, block, out, send, recv

    def pass_on(self, source, at, k):
        l = self.l
        l.send(source, self.out.at[at], self.send.at[k], self.recv.at[k], {"tensor": l.down},
               again=lambda: (self.out.at[0], self.send.at[k]))

    def start(self):
        self.pass_on(self.block, self.l.z, 0)

    def step(self, k):
        l = self.l
        at = lax.rem(l.z + k, l.n_t)
        l.arrived(self.out.at[at], self.recv.at[k - 1], self.send.at[k - 1], {"tensor": l.up})
        if k < l.n_t - 1:
            self.pass_on(self.out.at[at], at, k)


class Total:
    def __init__(self, links, block, buf, send, recv):
        self.l, self.block, self.buf, self.s, self.r = links, block, buf, send, recv
        self.levels = len(links.bits)
        self.count = self.levels + links.n_t

    def step(self, s):
        l, buf = self.l, self.buf
        if s == 0:
            buf[1] = self.block[...]
        else:
            l.arrived(buf.at[2 * s], self.r.at[s - 1], self.s.at[s - 1], {"tensor": l.up})
            if s <= self.levels:
                buf[2 * s + 1] = buf[2 * s - 1] + buf[2 * s]
        if s < self.levels:
            l.send(buf.at[2 * s + 1], buf.at[2 * s + 2], self.s.at[s], self.r.at[s], {"dp": l.flip(l.bits[s])})
        elif s < self.count - 1:
            src = 2 * s + 1 if s == self.levels else 2 * s
            l.send(buf.at[src], buf.at[2 * s + 2], self.s.at[s], self.r.at[s], {"tensor": l.down})

    def result(self):
        total = self.buf[2 * self.levels + 1]
        for k in range(1, self.l.n_t):
            total = total + self.buf[2 * (self.levels + k)]
        return total


def row_loop(rows, step, body):
    def turn(r, _):
        body(pl.ds(pl.multiple_of(r * step, step), step))
        return 0

    lax.fori_loop(0, rows // step, turn, 0)


def norm_rows(source, gain, out):
    def body(at):
        h = source[at, :].astype(F32)
        r = lax.rsqrt(jnp.mean(h * h, axis=1, keepdims=True) + EPS)
        out[at, :] = (h * r * gain).astype(BF16)

    row_loop(source.shape[0], 32, body)


def attend_slot(qkv, o, mask):
    heads = o.shape[1] // HEAD_SIZE
    for h in range(heads):
        q, k, v = (slice((t * heads + h) * HEAD_SIZE, (t * heads + h + 1) * HEAD_SIZE) for t in range(3))
        p = probabilities(qkv[:, q], qkv[:, k], mask).astype(BF16)
        o[:, q] = by_block(dot_nn, p, qkv[:, v]).astype(BF16)


class Loader:
    def __init__(self, buf, sem, blocks):
        self.buf, self.sem, self.blocks = buf, sem, blocks

    def copy(self, j):
        slot = j % self.buf.shape[0]
        return pltpu.make_async_copy(self.blocks[j], self.buf.at[slot], self.sem.at[slot])

    def start(self, j):
        if j < len(self.blocks):
            self.copy(j).start()

    def wait(self, j):
        self.copy(j).wait()
        return self.buf.at[j % self.buf.shape[0]]


def forward_kernel(
    n_dp, n_t, a_own, i_own, d_own, x0, gains, seg_col, seg_row, obs_row, cos, sin,
    full, xs, qkv_out, o_out, h2_out, act_out, slope_out, out,
    x, n, proj, qkv, o, h2, acc, act, slope, outb, mask, wbuf,
    w_sem, s_sem, y_send, y_recv, x_sem, z_send, z_recv, p_send, p_recv,
):
    l = Links(n_dp, n_t)
    section = lax.axis_index("section")
    first, second = section == 0, section != 0
    own = (a_own, i_own, d_own)
    g = Gather(l, own, full, z_send, z_recv, p_send, p_recv)
    other = {"section": 1 - section}
    l.greet([{"tensor": l.up}, other] + [{"dp": l.flip(b)} for b in l.bits])
    g.start()
    rows, d = x.shape
    wide = o.shape[2]

    def block(m, slot):
        return own[m] if slot == 0 else full.at[m, slot]

    order = [(0, s) for s in range(n_t)] + [(m, s) for s in range(n_t) for m in (1, 2)]
    load = Loader(wbuf, w_sem, [block(m, s) for m, s in order])
    stores = []

    def store(src, dst, sem):
        copy = pltpu.make_async_copy(src, dst, sem)
        copy.start()
        stores.append(copy)

    @pl.when(first)
    def _():
        copy = pltpu.make_async_copy(x0, x, x_sem)
        copy.start()
        copy.wait()

    write_mask(mask, seg_col, seg_row, obs_row)
    l.recording = False

    @pl.when(second)
    def _():
        for _ in g.walk():
            pass
        load.start(0)
        load.start(1)
        pltpu.make_async_remote_copy(
            src_ref=outb, dst_ref=x, send_sem=y_send, recv_sem=y_recv, device_id=other, device_id_type=MESH
        ).wait_recv()

    l.recording = True
    walk = g.walk()

    def until(m, slot):
        if slot > 0:
            for unit in walk:
                if unit == (m, slot, g.split - 1):
                    return

    store(x, xs, s_sem.at[0])
    norm_rows(x, gains[0:1, :], n)
    for s in range(n_t):
        @pl.when(first)
        def _():
            until(0, s)
            load.start(s)

        @pl.when(second)
        def _():
            load.start(s + 2)

        w = load.wait(s)
        proj[:, 0:3 * wide] = dot_nt(n[...], w[0:3 * wide, :])

        def turn_rows(at):
            v = proj[at, 0:2 * wide]
            qkv[s, at, 0:2 * wide] = (v * cos[at, :] + partner(v) * sin[at, :]).astype(BF16)
            qkv[s, at, 2 * wide:3 * wide] = proj[at, 2 * wide:3 * wide].astype(BF16)

        row_loop(rows, 32, turn_rows)
        attend_slot(qkv.at[s], o.at[s], mask)
        term = dot_nn(o[s], w[3 * wide:, :])
        if s == 0:
            acc[...] = term
        else:
            acc[...] = acc[...] + term
        store(qkv.at[s], qkv_out.at[s], s_sem.at[1 + s])
        store(o.at[s], o_out.at[s], s_sem.at[1 + n_t + s])

    def middle(at):
        h = x[at, :].astype(F32) + acc[at, :]
        h2[at, :] = h
        acc[at, :] = h
        r = lax.rsqrt(jnp.mean(h * h, axis=1, keepdims=True) + EPS)
        n[at, :] = (h * r * gains[1:2, :]).astype(BF16)

    row_loop(rows, 32, middle)
    store(h2, h2_out, s_sem.at[1 + 2 * n_t])
    spare = 2 + 2 * n_t
    for s in range(n_t):
        j = n_t + 2 * s

        @pl.when(first)
        def _():
            until(2, s)
            load.start(j)
            load.start(j + 1)

        @pl.when(second)
        def _():
            load.start(j + 2)

        w = load.wait(j)
        proj[...] = dot_nn(n[...], w[...])
        if s >= 2:
            for copy in stores[-4:-2]:
                copy.wait()
            del stores[-4:-2]

        def silu(at):
            u = proj[at, :]
            sig = lax.logistic(u)
            act[s % 2, at, :] = (u * sig).astype(BF16)
            slope[s % 2, at, :] = (sig * (1.0 + u * (1.0 - sig))).astype(BF16)

        row_loop(rows, 32, silu)

        @pl.when(second)
        def _():
            load.start(j + 3)

        w = load.wait(j + 1)
        acc[...] = acc[...] + dot_nn(act[s % 2], w[...])
        store(act.at[s % 2], act_out.at[s], s_sem.at[spare + 2 * (s % 2)])
        store(slope.at[s % 2], slope_out.at[s], s_sem.at[spare + 2 * (s % 2) + 1])

    def finish(at):
        outb[at, :] = acc[at, :].astype(BF16)

    row_loop(rows, 32, finish)
    over = pltpu.make_async_remote_copy(
        src_ref=outb, dst_ref=x, send_sem=y_send, recv_sem=y_recv, device_id=other, device_id_type=MESH
    )

    @pl.when(first)
    def _():
        over.start()

    store(outb, out, x_sem)
    for copy in stores:
        copy.wait()

    @pl.when(first)
    def _():
        over.wait_send()

    l.drain()


def run_forward(a_own, i_own, d_own, x0, gains, seg, obs, tables):
    n_dp, n_t = lax.axis_size("dp"), lax.axis_size("tensor")
    rows, d = x0.shape
    wide = a_own.shape[0] // 4
    count = len(gather_units(a_own.shape[0] // n_dp, n_t)[1])
    dma = pltpu.SemaphoreType.DMA
    hbm, vmem = pl.BlockSpec(memory_space=pl.ANY), pl.BlockSpec(memory_space=pltpu.VMEM)

    def shape(*s, t=BF16):
        return jax.ShapeDtypeStruct(s, t)

    return pl.pallas_call(
        functools.partial(forward_kernel, n_dp, n_t),
        out_shape=[
            shape(3, n_t, *a_own.shape), shape(rows, d), shape(n_t, rows, 3 * wide), shape(n_t, rows, wide),
            shape(rows, d, t=F32), shape(n_t, rows, i_own.shape[1]), shape(n_t, rows, i_own.shape[1]), shape(rows, d),
        ],
        in_specs=[hbm] * 4 + [vmem] * 6,
        out_specs=[hbm] * 8,
        scratch_shapes=[
            pltpu.VMEM((rows, d), BF16),
            pltpu.VMEM((rows, d), BF16),
            pltpu.VMEM((rows, d), F32),
            pltpu.VMEM((n_t, rows, 3 * wide), BF16),
            pltpu.VMEM((n_t, rows, wide), BF16),
            pltpu.VMEM((rows, d), F32),
            pltpu.VMEM((rows, d), F32),
            pltpu.VMEM((2, rows, d), BF16),
            pltpu.VMEM((2, rows, d), BF16),
            pltpu.VMEM((rows, d), BF16),
            pltpu.VMEM((ROW, 2 * QB), F32),
            pltpu.VMEM((3,) + a_own.shape, BF16),
            dma((3,)), dma((6 + 2 * n_t,)), dma(()), dma(()), dma(()),
            dma((count,)), dma((count,)), dma((count, n_dp)), dma((count, n_dp)),
        ],
        compiler_params=pltpu.CompilerParams(collective_id=0, has_side_effects=True, vmem_limit_bytes=60 * 2**20),
    )(a_own, i_own, d_own, x0, gains, seg[:, None], seg[None, :], obs[None, :], *tables)


def attend_slot_back(qkv, do, dqk, dcat, mask):
    wide = do.shape[1]
    heads = wide // HEAD_SIZE
    for h in range(heads):
        q, k, v = (slice((t * heads + h) * HEAD_SIZE, (t * heads + h + 1) * HEAD_SIZE) for t in range(3))
        qh, kh, vh, dh = qkv[:, q], qkv[:, k], qkv[:, v], do[:, q]
        p = probabilities(qh, kh, mask)
        dcat[:, v] = by_window(p.astype(BF16), dh).astype(BF16)
        dp = by_block(dot_nt, dh, vh)
        ds = (p * (dp - jnp.sum(p * dp, axis=1, keepdims=True))).astype(BF16)
        dqk[:, q] = by_block(dot_nn, ds, kh) * SCALE
        dqk[:, k] = by_window(ds, qh) * SCALE


def outer_product(out, left, right):
    step = left.shape[1] // 2

    def turn(j, _):
        at = pl.ds(pl.multiple_of(j * step, 128), step)
        out[at, :] = dot_tn(left[:, at], right[...]).astype(BF16)
        return 0

    lax.fori_loop(0, 2, turn, 0)


def norm_back_rows(g, dn, h, gain, gain_sum, write):
    gain_sum[...] = jnp.zeros_like(gain_sum)
    step = 32

    def body(at):
        hr, dr = h[at, :].astype(F32), dn[at, :]
        r = lax.rsqrt(jnp.mean(hr * hr, axis=1, keepdims=True) + EPS)
        y = gain * dr
        gain_sum[...] += jnp.sum((dr * hr * r).reshape(step // 8, 8, -1), axis=0)
        write(at, g[at, :].astype(F32) + r * y - hr * (r * r * r) * jnp.mean(hr * y, axis=1, keepdims=True))

    row_loop(h.shape[0], step, body)


def backward_kernel(
    n_dp, n_t, a_own, i_own, d_own, full, cot, xs, qkv_in, o_in, h2_in, act_in, slope_in, out_in, gains,
    seg_col, seg_row, obs_row, cos, sin,
    layer_acts, grad_acts, out_sums, out_gains, hbm_sums, hbm_got, hbm_ring, du_hbm,
    gbuf, act, du, n, h2, x, dn, ga, proj, qkv, o, do, dcat, dhb, mask, wbuf, gain0, gain1, gain_buf,
    w_sem, l_sem, a_sem, u_sem, q_sem, st_sem, y_send, y_recv, s1_send, s1_recv, s2_send, s2_recv, t_send, t_recv,
    *reduce_refs,
):
    section = lax.axis_index("section")
    first, second = section == 0, section != 0
    other = {"section": 1 - section}
    l, l2 = Links(n_dp, n_t), Links(n_dp, n_t)
    own = (a_own, i_own, d_own)
    rows, d = h2.shape
    wide = do.shape[1]
    slots = list(reversed(range(n_t)))
    order = [(m, s) for s in slots for m in (2, 1)] + [(0, s) for s in slots]
    ff = 2 * n_t
    hbm = (hbm_sums, hbm_got, hbm_ring)
    r = Reduce(l, order, out_sums, hbm, reduce_refs)
    r2 = Reduce(l2, order, out_sums, hbm, reduce_refs)
    spread1 = Spread(l, out_in, layer_acts, s1_send, s1_recv)
    spread1b = Spread(l2, out_in, layer_acts, s1_send, s1_recv)
    spread2 = Spread(l, dhb, grad_acts, s2_send, s2_recv)
    load = Loader(wbuf, w_sem, [own[m] if s == 0 else full.at[m, s] for m, s in order])

    l.greet([{"tensor": l.up}, {"tensor": l.down}, other] + [{"dp": l.flip(b)} for b in l.bits])
    spread1.start()
    load.start(0)
    load.start(1)

    def local(src, dst, sem):
        return pltpu.make_async_copy(src, dst, sem)

    acts_in = local(out_in, dhb, l_sem.at[0])
    acts_out = local(dhb, layer_acts.at[l.z], l_sem.at[0])
    h2_copy = local(h2_in, h2, l_sem.at[1])
    x_copy = local(xs, x, l_sem.at[2])
    o_copy = local(o_in, o, l_sem.at[3])
    for c in (acts_in, h2_copy, x_copy, o_copy):
        c.start()

    def act_copy(j):
        return local(act_in.at[slots[j]], act.at[j % 2], a_sem.at[j % 2])

    def slope_copy(j):
        return local(slope_in.at[slots[j]], du.at[j % 2], u_sem.at[j % 2])

    def du_out(j):
        return local(du.at[j % 2], du_hbm.at[slots[j]], st_sem.at[j % 2])

    def du_in(j):
        return local(du_hbm.at[slots[j]], du.at[j % 2], u_sem.at[j % 2])

    def qkv_copy(j):
        return local(qkv_in.at[slots[j]], qkv.at[j % 2], q_sem.at[j % 2])

    act_copy(0).start()
    slope_copy(0).start()
    write_mask(mask, seg_col, seg_row, obs_row)
    h2_copy.wait()
    norm_rows(h2, gains[1:2, :], n)
    acts_in.wait()
    acts_out.start()
    arrival = pltpu.make_async_remote_copy(
        src_ref=dhb, dst_ref=gbuf, send_sem=y_send, recv_sem=y_recv, device_id=other, device_id_type=MESH
    )
    cot_copy = local(cot, gbuf, l_sem.at[4])

    @pl.when(second)
    def _():
        cot_copy.start()
        cot_copy.wait()

    @pl.when(first)
    def _():
        for k in range(1, n_t - 1):
            spread1.step(k)
        arrival.wait_recv()

    def block_of(reducer, i):
        if i >= 3:
            reducer.clear(i)
        return reducer.block.at[i % 3]

    for j in range(n_t):
        if j + 1 < n_t:
            act_copy(j + 1).start()
            if j + 1 >= 2:
                du_out(j - 1).wait()
            slope_copy(j + 1).start()
        w = load.wait(2 * j)
        proj[...] = dot_nt(gbuf[...], w[...])
        load.start(2 * j + 2)
        slope_copy(j).wait()

        def scale(at):
            du[j % 2, at, :] = (proj[at, :] * du[j % 2, at, :].astype(F32)).astype(BF16)

        row_loop(rows, 32, scale)
        du_out(j).start()
        act_copy(j).wait()

        @pl.when(first)
        def _():
            outer_product(block_of(r, 2 * j), gbuf, act.at[j % 2])
            r.steps(2 * j)

        w = load.wait(2 * j + 1)
        if j == 0:
            dn[...] = dot_nt(du[j % 2], w[...])
        else:
            dn[...] = dn[...] + dot_nt(du[j % 2], w[...])
        load.start(2 * j + 3)

        @pl.when(first)
        def _():
            outer_product(block_of(r, 2 * j + 1), n, du.at[j % 2])
            r.steps(2 * j + 1)

    for j in range(max(n_t - 2, 0), n_t):
        du_out(j).wait()

    @pl.when(second)
    def _():
        for k in range(1, n_t - 1):
            spread1b.step(k)

    qkv_copy(0).start()

    def write_middle(at, value):
        h2[at, :] = value
        ga[at, :] = value.astype(BF16)

    norm_back_rows(gbuf, dn, h2, gains[1:2, :], gain1, write_middle)
    o_copy.wait()

    for j, s in enumerate(slots):
        if j + 1 < n_t:
            qkv_copy(j + 1).start()
        w = load.wait(ff + j)
        load.start(ff + j + 2)
        do[...] = dot_nt(ga[...], w[3 * wide:, :]).astype(BF16)
        qkv_copy(j).wait()
        attend_slot_back(qkv.at[j % 2], do, proj, dcat.at[s], mask)

        def turn_back(at):
            v = proj[at, 0:2 * wide]
            dcat[s, at, 0:2 * wide] = (v * cos[at, :] - partner(v) * sin[at, :]).astype(BF16)

        row_loop(rows, 32, turn_back)
        if j == 0:
            dn[...] = dot_nn(dcat[s], w[0:3 * wide, :])
        else:
            dn[...] = dn[...] + dot_nn(dcat[s], w[0:3 * wide, :])
        if j < 2:
            @pl.when(first)
            def _():
                r.last_step(j)
    x_copy.wait()
    acts_out.wait()

    def write_input(at, value):
        dhb[at, :] = value.astype(BF16)

    norm_back_rows(h2, dn, x, gains[0:1, :], gain0, write_input)
    over = pltpu.make_async_remote_copy(
        src_ref=dhb, dst_ref=gbuf, send_sem=y_send, recv_sem=y_recv, device_id=other, device_id_type=MESH
    )

    @pl.when(second)
    def _():
        over.start()

    spread2.start()
    grads_out = local(dhb, grad_acts.at[l.z], l_sem.at[0])
    grads_out.start()

    @pl.when(second)
    def _():
        du_in(0).start()
        act_copy(0).start()
        for j in range(n_t):
            if j + 1 < n_t:
                act_copy(j + 1).start()
                du_in(j + 1).start()
            act_copy(j).wait()
            outer_product(block_of(r2, 2 * j), gbuf, act.at[j % 2])
            r2.steps(2 * j)
            du_in(j).wait()
            outer_product(block_of(r2, 2 * j + 1), n, du.at[j % 2])
            r2.steps(2 * j + 1)
        r2.last_step(0)
        r2.last_step(1)

    total = Total(l, gain0, gain_buf, t_send, t_recv)
    gain0[0:1, :] = jnp.sum(gain0[...], axis=0, keepdims=True)
    gain0[1:2, :] = jnp.sum(gain1[...], axis=0, keepdims=True)
    norm_rows(x, gains[0:1, :], n)
    for j, s in enumerate(slots):
        b = block_of(r, ff + j)
        step = d // 2

        def turn(c, _):
            at = pl.ds(pl.multiple_of(c * step, 128), step)
            b[at, 0:3 * wide] = dot_tn(n[:, at], dcat[s]).astype(BF16)
            b[at, 3 * wide:] = dot_tn(ga[:, at], o[s]).astype(BF16)
            return 0

        lax.fori_loop(0, 2, turn, 0)
        r.steps(ff + j)
        total.step(j)
    for i in range(3):
        r.steps(ff + n_t + i)
        total.step(n_t + i) if n_t + i < total.count else None
    for t in range(n_t + 3, total.count):
        total.step(t)
    for i in range(2, len(order)):
        r.last_step(i)
        if i == 3 or i == 5:
            spread2.step((i - 1) // 2)
    spread1.step(n_t - 1)
    spread2.step(n_t - 1)
    out_gains[...] = total.result()
    r.close()
    grads_out.wait()

    @pl.when(second)
    def _():
        over.wait_send()

    l.drain()


def run_backward(a_own, i_own, d_own, kept, cot, gains, seg, obs, tables):
    n_dp, n_t = lax.axis_size("dp"), lax.axis_size("tensor")
    rows, d = cot.shape
    wide = a_own.shape[0] // 4
    piece = d // n_dp
    count = 3 * n_t
    steps = len(ring_bits(n_dp)) + n_t
    dma = pltpu.SemaphoreType.DMA
    hbm, vmem = pl.BlockSpec(memory_space=pl.ANY), pl.BlockSpec(memory_space=pltpu.VMEM)

    def shape(*s, t=BF16):
        return jax.ShapeDtypeStruct(s, t)

    def buf(*s, t=BF16):
        return pltpu.VMEM(s, t)

    return pl.pallas_call(
        functools.partial(backward_kernel, n_dp, n_t),
        out_shape=[
            shape(n_t, rows, d), shape(n_t, rows, d), shape(3, piece, d, t=F32), shape(8, d, t=F32),
            *reduce_hbm(n_dp, n_t, count, piece, d), shape(n_t, rows, d),
        ],
        in_specs=[hbm] * 12 + [vmem] * 6,
        out_specs=[hbm] * 3 + [vmem] + [hbm] * 4,
        scratch_shapes=[
            buf(rows, d), buf(2, rows, d), buf(2, rows, d), buf(rows, d), buf(rows, d, t=F32), buf(rows, d),
            buf(rows, d, t=F32), buf(rows, d), buf(rows, d, t=F32), buf(2, rows, 3 * wide), buf(n_t, rows, wide),
            buf(rows, wide), buf(n_t, rows, 3 * wide), buf(rows, d), buf(ROW, 2 * QB, t=F32), buf(3, *a_own.shape),
            buf(8, d, t=F32), buf(8, d, t=F32), buf(2 * steps, 8, d, t=F32),
            dma((3,)), dma((5,)), dma((2,)), dma((2,)), dma((2,)), dma((2,)), dma(()), dma(()),
            dma((n_t,)), dma((n_t,)), dma((n_t,)), dma((n_t,)), dma((steps,)), dma((steps,)),
            *reduce_scratch(n_dp, n_t, count, piece, d),
        ],
        compiler_params=pltpu.CompilerParams(collective_id=1, has_side_effects=True, vmem_limit_bytes=62 * 2**20),
    )(a_own, i_own, d_own, kept[0], cot, *kept[1:], gains, seg[:, None], seg[None, :], obs[None, :], *tables)


def own_rows(x, count):
    flat = x.reshape((-1,) + x.shape[2:])
    return lax.dynamic_slice_in_dim(flat, lax.axis_index("tensor") * count, count, 0)


def on_device(tokens, cotangent, seg_ids, observed, w_qkv, w_out, w_in, w_down, norm_gains):
    n_dp, n_t = lax.axis_size("dp"), lax.axis_size("tensor")
    w_qkv, w_out, w_in, w_down, gains = w_qkv[0], w_out[0], w_in[0], w_down[0], norm_gains[0]
    micro, rows, d = tokens.shape
    hd = w_out.shape[0]
    count = micro * rows // n_t
    tables = rope_tables()
    stack = jnp.concatenate([jnp.swapaxes(w_qkv, 1, 2), w_out[None]], axis=0).reshape(4 * hd, d)
    x0 = own_rows(tokens, count)
    g1 = own_rows(cotangent, count)
    seg, obs = own_rows(seg_ids, count), own_rows(observed, count)
    kept = run_forward(stack, w_in, w_down, x0, gains, seg, obs, tables)
    layer_acts, grad_acts, sums, gain = run_backward(stack, w_in, w_down, kept, g1, gains, seg, obs, tables)[:4]
    piece = d // n_dp
    gain = lax.dynamic_slice_in_dim(gain[:2], lax.axis_index("dp") * piece, piece, 1)
    r_attn, r_in, r_down = sums[0], sums[1], sums[2]
    r_qkv = jnp.stack([r_attn[:, i * hd:(i + 1) * hd] for i in range(3)])
    return (
        layer_acts.reshape(1, micro, rows, d),
        grad_acts.reshape(1, micro, rows, d),
        r_qkv[None],
        r_attn[:, 3 * hd:].T[None],
        r_in[None],
        r_down.T[None],
        gain[None],
    )


def solution(mesh):
    return jax.shard_map(
        on_device,
        mesh=mesh,
        in_specs=(
            P(None, "dp", None),
            P(None, "dp", None),
            P(None, "dp"),
            P(None, "dp"),
            P("section", None, None, "tensor"),
            P("section", "tensor", None),
            P("section", None, "tensor"),
            P("section", "tensor", None),
            P("section", None, None),
        ),
        out_specs=(
            P("section", None, "dp", None),
            P("section", None, "dp", None),
            P("section", None, "dp", "tensor"),
            P("section", "tensor", "dp"),
            P("section", "dp", "tensor"),
            P("section", "tensor", "dp"),
            P("section", None, "dp"),
        ),
        check_vma=False,
    )
```

```python
import functools
import math

import jax
import jax.numpy as jnp
from jax import lax
from jax.experimental import pallas as pl
from jax.experimental.pallas import tpu as pltpu
from jax.sharding import PartitionSpec as P

HEAD_SIZE = 80
HALF = HEAD_SIZE // 2
ROW = 512
QB = 128
GROUP = 8
EPS = 1e-06
BIG = 1000000000.0
SCALE = 1.0 / math.sqrt(HEAD_SIZE)
BF16 = jnp.bfloat16
F32 = jnp.float32
MESH = pl.DeviceIdType.MESH


def dot_nn(a, b):
    return lax.dot_general(a, b, (((1,), (0,)), ((), ())), preferred_element_type=F32)


def dot_nt(a, b):
    return lax.dot_general(a, b, (((1,), (1,)), ((), ())), preferred_element_type=F32)


def dot_tn(a, b):
    return lax.dot_general(a, b, (((0,), (0,)), ((), ())), preferred_element_type=F32)


def rope_tables():
    freq = 10000.0 ** (-jnp.arange(HALF, dtype=F32) / HALF)
    ang = jnp.arange(ROW, dtype=F32)[:, None] * freq[None, :]
    cos, sin = jnp.cos(ang), jnp.sin(ang)
    cos_full = jnp.tile(jnp.concatenate([cos, cos], axis=1), (1, GROUP))
    sin_full = jnp.tile(jnp.concatenate([-sin, sin], axis=1), (1, GROUP))
    return cos_full, sin_full


def partner(x):
    width = x.shape[1]
    lane = lax.broadcasted_iota(jnp.int32, x.shape, 1)
    first = lax.rem(lane, HEAD_SIZE) < HALF
    return jnp.where(first, pltpu.roll(x, width - HALF, 1), pltpu.roll(x, HALF, 1))


def windows():
    return [max(i - 1, 0) * QB for i in range(ROW // QB)]


def write_mask(mask, seg_col, seg_row, obs_row):
    for i, k0 in enumerate(windows()):
        r = slice(i * QB, (i + 1) * QB)
        shape = (QB, 2 * QB)
        qi = lax.broadcasted_iota(jnp.int32, shape, 0) + i * QB
        kj = lax.broadcasted_iota(jnp.int32, shape, 1) + k0
        same = seg_col[r, :] == seg_row[:, k0:k0 + 2 * QB]
        seen = (obs_row[:, k0:k0 + 2 * QB] == 1) | (kj == qi)
        mask[r, :] = (same & (kj <= qi) & seen).astype(F32)


def by_block(dot, left, right):
    return jnp.concatenate(
        [dot(left[i * QB:(i + 1) * QB], right[k0:k0 + 2 * QB]) for i, k0 in enumerate(windows())], axis=0
    )


def by_window(left, right):
    n = ROW // QB
    blocks = [None] * n
    for i, k0 in enumerate(windows()):
        r = slice(i * QB, (i + 1) * QB)
        term = dot_tn(left[r], right[r])
        for j in range(2):
            at, part = k0 // QB + j, term[j * QB:(j + 1) * QB]
            blocks[at] = part if blocks[at] is None else blocks[at] + part
    return jnp.concatenate(blocks, axis=0)


def probabilities(q, k, mask):
    s = jnp.where(mask[...] > 0, by_block(dot_nt, q, k) * SCALE, -BIG)
    e = jnp.exp(s - jnp.max(s, axis=1, keepdims=True))
    return e * (1.0 / jnp.sum(e, axis=1, keepdims=True))


def ring_bits(n):
    return [1 << i for i in range(n.bit_length() - 1)]


def low_bit(j):
    return j & -j


class Links:
    def __init__(self, n_dp, n_t):
        self.n_dp, self.n_t = n_dp, n_t
        self.me, self.z = lax.axis_index("dp"), lax.axis_index("tensor")
        self.down = lax.rem(self.z + n_t - 1, n_t)
        self.up = lax.rem(self.z + 1, n_t)
        self.bits = ring_bits(n_dp)
        self.sent, self.recording = {}, True

    def flip(self, bit):
        return self.me + bit - 2 * bit * lax.rem(self.me // bit, 2)

    def mix(self, j):
        at = self.me
        for bit in self.bits:
            if j & bit:
                at = at + bit - 2 * bit * lax.rem(self.me // bit, 2)
        return at

    def place(self, table):
        n = self.n_t
        return sum(v * (1 - ((self.z - k) * (self.z - k) + n * n - 1) // (n * n)) for k, v in enumerate(table))

    def own_bit(self, bit):
        return lax.rem(self.me // bit, 2)

    def greet(self, axes):
        barrier = pltpu.get_barrier_semaphore()
        for where in axes:
            pl.semaphore_signal(barrier, inc=1, device_id=where, device_id_type=MESH)
        pl.semaphore_wait(barrier, len(axes))

    def send(self, src, dst, send_sem, recv_sem, where, tag=None, again=None, when=None):
        pltpu.make_async_remote_copy(
            src_ref=src, dst_ref=dst, send_sem=send_sem, recv_sem=recv_sem, device_id=where, device_id_type=MESH
        ).start()
        if self.recording:
            self.sent.setdefault(tag, []).append((again or (lambda: (src, send_sem)), when))

    def finish(self, tag):
        def left(again):
            ref, sem = again()
            pltpu.make_async_remote_copy(
                src_ref=ref, dst_ref=ref, send_sem=sem, recv_sem=sem, device_id={"tensor": self.down}, device_id_type=MESH
            ).wait_send()

        for again, when in self.sent.pop(tag, ()):
            if when is None:
                left(again)
            else:
                pl.when(when())(functools.partial(left, again))

    def arrived(self, ref, sem, send_sem, where):
        pltpu.make_async_remote_copy(
            src_ref=ref, dst_ref=ref, send_sem=send_sem, recv_sem=sem, device_id=where, device_id_type=MESH
        ).wait_recv()

    def drain(self):
        for tag in list(self.sent):
            self.finish(tag)


class Gather:
    def __init__(self, links, own, full, z_send, z_recv, p_send, p_recv):
        self.l, self.own, self.full = links, own, full
        self.z_send, self.z_recv, self.p_send, self.p_recv = z_send, z_recv, p_send, p_recv
        self.rows = own[0].shape[0] // links.n_dp
        self.split, self.units = gather_units(self.rows, links.n_t)
        self.part = self.rows // self.split
        self.at = {u: i for i, u in enumerate(self.units)}

    def piece(self, m, slot, index, h):
        first = pl.multiple_of(index * self.rows + h * self.part, 16)
        if slot == 0:
            return self.own[m].at[pl.ds(first, self.part), :]
        return self.full.at[m, slot, pl.ds(first, self.part), :]

    def send_z(self, m, k, h):
        l = self.l
        i = self.at[(m, k, h)]
        l.send(self.piece(m, k - 1, l.me, h), self.piece(m, k, l.me, h), self.z_send.at[i], self.z_recv.at[i], {"tensor": l.down},
               again=lambda: (self.like(), self.z_send.at[i]))

    def like(self):
        return self.full.at[0, 1, pl.ds(0, self.part), :]

    def start(self):
        for m, k, h in self.units:
            if k == 1 and m < 2:
                self.send_z(m, k, h)

    def share(self, i, j):
        m, k, h = self.units[i]
        l = self.l
        for bit in reversed(l.bits):
            if j == 0 or bit < low_bit(j):
                ref = self.piece(m, k, l.mix(j), h)
                l.send(ref, ref, self.p_send.at[i, j ^ bit], self.p_recv.at[i, j ^ bit], {"dp": l.flip(bit)},
                       again=lambda at=j ^ bit: (self.like(), self.p_send.at[i, at]))

    def take(self, i):
        m, k, h = self.units[i]
        l = self.l
        l.arrived(self.piece(m, k, l.me, h), self.z_recv.at[i], self.z_send.at[i], {"tensor": l.up})
        if k + 1 < l.n_t:
            self.send_z(m, k + 1, h)
        if (m, k) == (0, 1):
            self.send_z(2, 1, h)
        self.share(i, 0)

    def relay(self, i):
        m, k, h = self.units[i]
        l = self.l
        for j in sorted(range(1, l.n_dp), key=lambda j: (-low_bit(j), j)):
            l.arrived(self.piece(m, k, l.mix(j), h), self.p_recv.at[i, j], self.p_send.at[i, j], {"dp": l.flip(low_bit(j))})
            self.share(i, j)

    def walk(self, lag=2):
        for i in range(len(self.units) + lag):
            if i < len(self.units):
                self.take(i)
            if i >= lag:
                self.relay(i - lag)
                yield self.units[i - lag]


def gather_units(rows, n_t):
    split = 2 if rows % 32 == 0 else 1
    heads = [(0, k) for k in range(1, n_t)]
    rest = [(m, k) for k in range(1, n_t) for m in (1, 2)]
    mixed = [u for pair in zip(heads, rest) for u in pair] + rest[len(heads):]
    return split, [(m, k, h) for m, k in mixed for h in range(split)]


def level_start(n_dp, level):
    return sum(n_dp >> (t + 1) for t in range(level))


def add_rows(out, *terms):
    rows = out.shape[0]

    def body(r, _):
        at = pl.ds(pl.multiple_of(r * 16, 16), 16)
        total = terms[0][at, :].astype(F32)
        for t in terms[1:]:
            total = total + t[at, :].astype(F32)
        out[at, :] = total.astype(out.dtype)
        return 0

    lax.fori_loop(0, rows // 16, body, 0)


def reduce_scratch(n_dp, n_t, count, rows, c):
    dma = pltpu.SemaphoreType.DMA
    half = n_dp // 2
    return [
        pltpu.VMEM((3, n_dp * rows, c), BF16),
        pltpu.VMEM((2, half, rows, c), BF16),
        pltpu.VMEM((3, rows, c), BF16),
        pltpu.VMEM((3, rows, c), BF16),
        pltpu.VMEM((rows, c), F32),
        dma((count, n_dp)),
        dma((count, n_dp)),
        dma((count,)),
        dma((count // n_t, n_t, 2)),
        dma((2,)),
        dma((2,)),
        dma((3,)),
        dma(()),
    ]


def reduce_hbm(n_dp, n_t, count, rows, c):
    return [
        jax.ShapeDtypeStruct((count, n_dp // 2, rows, c), BF16),
        jax.ShapeDtypeStruct((count, n_dp - 1, rows, c), BF16),
        jax.ShapeDtypeStruct((count // n_t, n_t, 2, rows, c), BF16),
    ]


def line_order(n_t):
    return [sorted(range(n_t), key=lambda s: (-abs(s - z), -max(s, n_t - 1 - s))) for z in range(n_t)]


class Places:
    def __init__(self, links):
        n_t = links.n_t
        orders = line_order(n_t)
        self.shard = [links.place([o[j] for o in orders]) for j in range(n_t)]
        self.slot = [links.place([(o[j] - z) % n_t for z, o in enumerate(orders)]) for j in range(n_t - 1)] + [0]
        self.up = [links.place([int(o[j] > z) for z, o in enumerate(orders)]) for j in range(n_t)]
        self.below = (links.z + n_t - 1) // n_t
        self.above = (2 * n_t - 2 - links.z) // n_t


class Reduce:
    def __init__(self, links, places, order, out, hbm, scratch):
        self.l, self.places, self.order, self.out = links, places, order, out
        self.sums, self.got, self.ring = hbm
        (self.block, self.fetched, self.terms, self.moving, self.final,
         self.c_send, self.c_recv, self.z_send, self.z_recv,
         self.f_sem, self.s_sem, self.t_sem, self.o_sem) = scratch
        self.moves = []
        self.levels = len(links.bits)
        self.rows = self.fetched.shape[2]
        self.storing = None

    def offsets(self, level):
        bits = self.l.bits[level + 1:]
        return [sum(b for n, b in enumerate(bits) if k >> n & 1) for k in range(1 << len(bits))]

    def mine(self, level):
        return lax.rem(self.l.me, 1 << (level + 1))

    def give(self, i, level, source):
        l, bit = self.l, self.l.bits[level]
        there = self.mine(level) + bit - 2 * bit * l.own_bit(bit)
        for n, off in enumerate(self.offsets(level)):
            at = (i, level_start(l.n_dp, level) + n)
            l.send(source(there + off), self.got.at[at], self.c_send.at[at], self.c_recv.at[at], {"dp": l.flip(bit)}, (i, level),
                   again=lambda at=at: (self.got.at[at], self.c_send.at[at]))

    def receive(self, i, level):
        l = self.l
        for n, _ in enumerate(self.offsets(level)):
            at = (i, level_start(l.n_dp, level) + n)
            l.arrived(self.got.at[at], self.c_recv.at[at], self.c_send.at[at], {"dp": l.flip(l.bits[level])})

    def piece(self, i, p):
        return self.block.at[i % 3, pl.ds(pl.multiple_of(p * self.rows, 16), self.rows), :]

    def give_block(self, i):
        self.give(i, 0, lambda p: self.piece(i, p))

    def fetch_copy(self, i):
        return pltpu.make_async_copy(self.got.at[i, pl.ds(0, self.l.n_dp // 2)], self.fetched.at[i % 2], self.f_sem.at[i % 2])

    def fetch(self, i):
        self.receive(i, 0)
        self.fetch_copy(i).start()

    def store_copy(self, i):
        return pltpu.make_async_copy(self.fetched.at[i % 2], self.sums.at[i], self.s_sem.at[i % 2])

    def add_first(self, i):
        self.fetch_copy(i).wait()
        for n in range(self.l.n_dp // 2):
            here = self.fetched.at[i % 2, n]
            add_rows(here, self.piece(i, 2 * n + self.l.own_bit(1)), here)
        self.store_copy(i).start()

    def give_next(self, i):
        self.store_copy(i).wait()
        self.give(i, 1, lambda piece: self.sums.at[i, piece // 2])

    def push(self, i):
        self.give_block(i)
        self.moves.append([i, 0])

    def pump(self):
        for move in list(self.moves):
            i, stage = move
            if stage == 1 and any(o[0] == i - 2 for o in self.moves):
                break
            if stage > 0:
                (self.fetch, self.add_first, self.give_next)[stage - 1](i)
            move[1] += 1
            if move[1] == 4:
                self.moves.remove(move)

    def flush(self, i=None):
        while any(i is None or o[0] <= i for o in self.moves):
            self.pump()

    def clear(self, i):
        while any(o[0] == i - 3 and o[1] < 3 for o in self.moves):
            self.pump()
        self.l.finish((i - 3, 0))

    def middle(self, i, level):
        l = self.l
        self.receive(i, level)
        for n, off in enumerate(self.offsets(level)):
            piece = (self.mine(level) + off) // 2
            loads = [
                pltpu.make_async_copy(self.sums.at[i, piece], self.terms.at[0], self.t_sem.at[0]),
                pltpu.make_async_copy(self.got.at[i, level_start(l.n_dp, level) + n], self.terms.at[1], self.t_sem.at[1]),
            ]
            for c in loads:
                c.start()
            for c in loads:
                c.wait()
            add_rows(self.terms.at[2], self.terms.at[0], self.terms.at[1])
            back = pltpu.make_async_copy(self.terms.at[2], self.sums.at[i, piece], self.t_sem.at[2])
            back.start()
            back.wait()
        self.give(i, level + 1, lambda piece: self.sums.at[i, piece // 2])

    def term_copies(self, i):
        l = self.l
        return [
            pltpu.make_async_copy(self.sums.at[i, l.me // 2], self.terms.at[0], self.t_sem.at[0]),
            pltpu.make_async_copy(self.got.at[i, l.n_dp - 2], self.terms.at[1], self.t_sem.at[1]),
        ]

    def collect(self, i):
        self.receive(i, self.levels - 1)
        for c in self.term_copies(i):
            c.start()

    def out_copy(self, m):
        return pltpu.make_async_copy(self.final, self.out.at[m], self.o_sem)

    def come(self, m, s, way):
        l = self.l
        ref = self.ring.at[m, s, way]
        l.arrived(ref, self.z_recv.at[m, s, way], self.z_send.at[0], {"tensor": l.down})
        copy = pltpu.make_async_copy(ref, self.terms.at[2], self.t_sem.at[2])
        copy.start()
        copy.wait()

    def pass_on(self, i):
        l, p = self.l, self.places
        m, j = self.order[i]
        l.finish(("z", i - 3))
        terms = [self.terms.at[t] for t in range(3)]
        if j < l.n_t - 1:
            s, up, out = p.shard[j], p.up[j], self.moving.at[i % 3]
            behind = up * p.below + (1 - up) * p.above
            for c in self.term_copies(i):
                c.wait()

            @pl.when(behind == 1)
            def _():
                self.come(m, s, 1 - up)
                add_rows(out, *terms)

            @pl.when(behind == 0)
            def _():
                add_rows(out, *terms[:2])

            l.send(out, self.ring.at[m, s, 1 - up], self.z_send.at[i], self.z_recv.at[m, s, 1 - up], {"tensor": l.z + 2 * up - 1},
                   ("z", i), again=lambda: (self.moving.at[i % 3], self.z_send.at[i]))
        else:
            if self.storing is not None:
                self.out_copy(self.storing).wait()
            for c in self.term_copies(i):
                c.wait()
            add_rows(self.final, *terms[:2])
            for way, there in ((0, p.below), (1, p.above)):
                @pl.when(there == 1)
                def _():
                    self.come(m, l.z, way)
                    add_rows(self.final, self.final, terms[2])
            self.out_copy(m).start()
            self.storing = m

    def last_step(self, i):
        self.flush(i)
        for level in range(1, self.levels - 1):
            self.middle(i, level)
        self.collect(i)
        self.pass_on(i)

    def close(self):
        self.out_copy(self.storing).wait()


class Spread:
    def __init__(self, links, places, block, out, send, recv):
        self.l, self.places, self.block, self.out, self.send, self.recv = links, places, block, out, send, recv

    def pass_on(self, source, at, way, k):
        l, p = self.l, self.places
        l.send(source, self.out.at[at], self.send.at[way, k], self.recv.at[way, k], {"tensor": l.z + 1 - 2 * way},
               again=lambda: (self.out.at[0], self.send.at[way, k]),
               when=lambda: ((p.above, p.below)[way] == 1) if k == 0 else self.passes(way, k))

    def passes(self, way, k):
        z, n = self.l.z, self.l.n_t
        return (z >= k) & (z < n - 1) if way == 0 else (z < n - k) & (z > 0)

    def start(self):
        p = self.places
        for way, there in ((0, p.above), (1, p.below)):
            @pl.when(there == 1)
            def _():
                self.pass_on(self.block, self.l.z, way, 0)

    def step(self, k):
        l = self.l
        for way in range(2):
            at = l.z + k * (2 * way - 1)

            @pl.when(l.z >= k if way == 0 else l.z < l.n_t - k)
            def _():
                l.arrived(self.out.at[at], self.recv.at[way, k - 1], self.send.at[way, k - 1], {"tensor": l.down})

            if k < l.n_t - 1:
                @pl.when(self.passes(way, k))
                def _():
                    self.pass_on(self.out.at[at], at, way, k)


class Total:
    def __init__(self, links, block, buf, send, recv):
        self.l, self.block, self.buf, self.s, self.r = links, block, buf, send, recv
        self.levels = len(links.bits)
        self.count = self.levels + links.n_t

    def step(self, s):
        l, buf = self.l, self.buf
        if s == 0:
            buf[1] = self.block[...]
        else:
            l.arrived(buf.at[2 * s], self.r.at[s - 1], self.s.at[s - 1], {"tensor": l.up})
            if s <= self.levels:
                buf[2 * s + 1] = buf[2 * s - 1] + buf[2 * s]
        if s < self.levels:
            l.send(buf.at[2 * s + 1], buf.at[2 * s + 2], self.s.at[s], self.r.at[s], {"dp": l.flip(l.bits[s])})
        elif s < self.count - 1:
            src = 2 * s + 1 if s == self.levels else 2 * s
            l.send(buf.at[src], buf.at[2 * s + 2], self.s.at[s], self.r.at[s], {"tensor": l.down})

    def result(self):
        total = self.buf[2 * self.levels + 1]
        for k in range(1, self.l.n_t):
            total = total + self.buf[2 * (self.levels + k)]
        return total


def row_loop(rows, step, body):
    def turn(r, _):
        body(pl.ds(pl.multiple_of(r * step, step), step))
        return 0

    lax.fori_loop(0, rows // step, turn, 0)


def norm_rows(source, gain, out):
    def body(at):
        h = source[at, :].astype(F32)
        r = lax.rsqrt(jnp.mean(h * h, axis=1, keepdims=True) + EPS)
        out[at, :] = (h * r * gain).astype(BF16)

    row_loop(source.shape[0], 32, body)


def attend_slot(qkv, o, mask):
    heads = o.shape[1] // HEAD_SIZE
    for h in range(heads):
        q, k, v = (slice((t * heads + h) * HEAD_SIZE, (t * heads + h + 1) * HEAD_SIZE) for t in range(3))
        p = probabilities(qkv[:, q], qkv[:, k], mask).astype(BF16)
        o[:, q] = by_block(dot_nn, p, qkv[:, v]).astype(BF16)


class Loader:
    def __init__(self, buf, sem, blocks):
        self.buf, self.sem, self.blocks = buf, sem, blocks

    def copy(self, j):
        slot = j % self.buf.shape[0]
        return pltpu.make_async_copy(self.blocks[j], self.buf.at[slot], self.sem.at[slot])

    def start(self, j):
        if j < len(self.blocks):
            self.copy(j).start()

    def wait(self, j):
        self.copy(j).wait()
        return self.buf.at[j % self.buf.shape[0]]


def forward_kernel(
    n_dp, n_t, a_own, i_own, d_own, x0, gains, seg_col, seg_row, obs_row, cos, sin,
    full, xs, qkv_out, o_out, h2_out, act_out, slope_out, out,
    x, n, proj, qkv, o, h2, acc, act, slope, outb, mask, wbuf,
    w_sem, s_sem, y_send, y_recv, x_sem, z_send, z_recv, p_send, p_recv,
):
    l = Links(n_dp, n_t)
    section = lax.axis_index("section")
    first, second = section == 0, section != 0
    own = (a_own, i_own, d_own)
    g = Gather(l, own, full, z_send, z_recv, p_send, p_recv)
    other = {"section": 1 - section}
    l.greet([{"tensor": l.up}, other] + [{"dp": l.flip(b)} for b in l.bits])
    g.start()
    rows, d = x.shape
    wide = o.shape[2]

    def block(m, slot):
        return own[m] if slot == 0 else full.at[m, slot]

    order = [(0, s) for s in range(n_t)] + [(m, s) for s in range(n_t) for m in (1, 2)]
    load = Loader(wbuf, w_sem, [block(m, s) for m, s in order])
    stores = []

    def store(src, dst, sem):
        copy = pltpu.make_async_copy(src, dst, sem)
        copy.start()
        stores.append(copy)

    @pl.when(first)
    def _():
        copy = pltpu.make_async_copy(x0, x, x_sem)
        copy.start()
        copy.wait()

    write_mask(mask, seg_col, seg_row, obs_row)
    l.recording = False

    @pl.when(second)
    def _():
        for _ in g.walk():
            pass
        load.start(0)
        load.start(1)
        pltpu.make_async_remote_copy(
            src_ref=outb, dst_ref=x, send_sem=y_send, recv_sem=y_recv, device_id=other, device_id_type=MESH
        ).wait_recv()

    l.recording = True
    walk, here = g.walk(), set()

    def until(m, slot):
        while slot > 0 and (m, slot, g.split - 1) not in here:
            here.add(next(walk))

    def tick():
        @pl.when(first)
        def _():
            here.add(next(walk, None))

    store(x, xs, s_sem.at[0])
    norm_rows(x, gains[0:1, :], n)
    for s in range(n_t):
        @pl.when(first)
        def _():
            until(0, s)
            load.start(s)

        @pl.when(second)
        def _():
            load.start(s + 2)

        w = load.wait(s)
        proj[:, 0:3 * wide] = dot_nt(n[...], w[0:3 * wide, :])

        def turn_rows(at):
            v = proj[at, 0:2 * wide]
            qkv[s, at, 0:2 * wide] = (v * cos[at, :] + partner(v) * sin[at, :]).astype(BF16)
            qkv[s, at, 2 * wide:3 * wide] = proj[at, 2 * wide:3 * wide].astype(BF16)

        row_loop(rows, 32, turn_rows)
        tick()
        attend_slot(qkv.at[s], o.at[s], mask)
        tick()
        term = dot_nn(o[s], w[3 * wide:, :])
        if s == 0:
            acc[...] = term
        else:
            acc[...] = acc[...] + term
        store(qkv.at[s], qkv_out.at[s], s_sem.at[1 + s])
        store(o.at[s], o_out.at[s], s_sem.at[1 + n_t + s])

    def middle(at):
        h = x[at, :].astype(F32) + acc[at, :]
        h2[at, :] = h
        acc[at, :] = h
        r = lax.rsqrt(jnp.mean(h * h, axis=1, keepdims=True) + EPS)
        n[at, :] = (h * r * gains[1:2, :]).astype(BF16)

    row_loop(rows, 32, middle)
    store(h2, h2_out, s_sem.at[1 + 2 * n_t])
    spare = 2 + 2 * n_t
    for s in range(n_t):
        j = n_t + 2 * s

        @pl.when(first)
        def _():
            until(2, s)
            load.start(j)
            load.start(j + 1)

        @pl.when(second)
        def _():
            load.start(j + 2)

        w = load.wait(j)
        proj[...] = dot_nn(n[...], w[...])
        if s >= 2:
            for copy in stores[-4:-2]:
                copy.wait()
            del stores[-4:-2]

        def silu(at):
            u = proj[at, :]
            sig = lax.logistic(u)
            act[s % 2, at, :] = (u * sig).astype(BF16)
            slope[s % 2, at, :] = (sig * (1.0 + u * (1.0 - sig))).astype(BF16)

        row_loop(rows, 32, silu)
        if s > 0:
            tick()

        @pl.when(second)
        def _():
            load.start(j + 3)

        w = load.wait(j + 1)
        acc[...] = acc[...] + dot_nn(act[s % 2], w[...])
        store(act.at[s % 2], act_out.at[s], s_sem.at[spare + 2 * (s % 2)])
        store(slope.at[s % 2], slope_out.at[s], s_sem.at[spare + 2 * (s % 2) + 1])

    def finish(at):
        outb[at, :] = acc[at, :].astype(BF16)

    row_loop(rows, 32, finish)
    assert len(here - {None}) == len(g.units)
    over = pltpu.make_async_remote_copy(
        src_ref=outb, dst_ref=x, send_sem=y_send, recv_sem=y_recv, device_id=other, device_id_type=MESH
    )

    @pl.when(first)
    def _():
        over.start()

    store(outb, out, x_sem)
    for copy in stores:
        copy.wait()

    @pl.when(first)
    def _():
        over.wait_send()

    l.drain()


def run_forward(a_own, i_own, d_own, x0, gains, seg, obs, tables):
    n_dp, n_t = lax.axis_size("dp"), lax.axis_size("tensor")
    rows, d = x0.shape
    wide = a_own.shape[0] // 4
    count = len(gather_units(a_own.shape[0] // n_dp, n_t)[1])
    dma = pltpu.SemaphoreType.DMA
    hbm, vmem = pl.BlockSpec(memory_space=pl.ANY), pl.BlockSpec(memory_space=pltpu.VMEM)

    def shape(*s, t=BF16):
        return jax.ShapeDtypeStruct(s, t)

    return pl.pallas_call(
        functools.partial(forward_kernel, n_dp, n_t),
        out_shape=[
            shape(3, n_t, *a_own.shape), shape(rows, d), shape(n_t, rows, 3 * wide), shape(n_t, rows, wide),
            shape(rows, d, t=F32), shape(n_t, rows, i_own.shape[1]), shape(n_t, rows, i_own.shape[1]), shape(rows, d),
        ],
        in_specs=[hbm] * 4 + [vmem] * 6,
        out_specs=[hbm] * 8,
        scratch_shapes=[
            pltpu.VMEM((rows, d), BF16),
            pltpu.VMEM((rows, d), BF16),
            pltpu.VMEM((rows, d), F32),
            pltpu.VMEM((n_t, rows, 3 * wide), BF16),
            pltpu.VMEM((n_t, rows, wide), BF16),
            pltpu.VMEM((rows, d), F32),
            pltpu.VMEM((rows, d), F32),
            pltpu.VMEM((2, rows, d), BF16),
            pltpu.VMEM((2, rows, d), BF16),
            pltpu.VMEM((rows, d), BF16),
            pltpu.VMEM((ROW, 2 * QB), F32),
            pltpu.VMEM((3,) + a_own.shape, BF16),
            dma((3,)), dma((6 + 2 * n_t,)), dma(()), dma(()), dma(()),
            dma((count,)), dma((count,)), dma((count, n_dp)), dma((count, n_dp)),
        ],
        compiler_params=pltpu.CompilerParams(collective_id=0, has_side_effects=True, vmem_limit_bytes=60 * 2**20),
    )(a_own, i_own, d_own, x0, gains, seg[:, None], seg[None, :], obs[None, :], *tables)


def attend_slot_back(qkv, do, dqk, dcat, mask):
    wide = do.shape[1]
    heads = wide // HEAD_SIZE
    for h in range(heads):
        q, k, v = (slice((t * heads + h) * HEAD_SIZE, (t * heads + h + 1) * HEAD_SIZE) for t in range(3))
        qh, kh, vh, dh = qkv[:, q], qkv[:, k], qkv[:, v], do[:, q]
        p = probabilities(qh, kh, mask)
        dcat[:, v] = by_window(p.astype(BF16), dh).astype(BF16)
        dp = by_block(dot_nt, dh, vh)
        ds = (p * (dp - jnp.sum(p * dp, axis=1, keepdims=True))).astype(BF16)
        dqk[:, q] = by_block(dot_nn, ds, kh) * SCALE
        dqk[:, k] = by_window(ds, qh) * SCALE


def outer_product(out, left, right):
    step = left.shape[1] // 2

    def turn(j, _):
        at = pl.ds(pl.multiple_of(j * step, 128), step)
        out[at, :] = dot_tn(left[:, at], right[...]).astype(BF16)
        return 0

    lax.fori_loop(0, 2, turn, 0)


def norm_back_rows(g, dn, h, gain, gain_sum, write):
    gain_sum[...] = jnp.zeros_like(gain_sum)
    step = 32

    def body(at):
        hr, dr = h[at, :].astype(F32), dn[at, :]
        r = lax.rsqrt(jnp.mean(hr * hr, axis=1, keepdims=True) + EPS)
        y = gain * dr
        gain_sum[...] += jnp.sum((dr * hr * r).reshape(step // 8, 8, -1), axis=0)
        write(at, g[at, :].astype(F32) + r * y - hr * (r * r * r) * jnp.mean(hr * y, axis=1, keepdims=True))

    row_loop(h.shape[0], step, body)


def backward_kernel(
    n_dp, n_t, a_own, i_own, d_own, full, cot, xs, qkv_in, o_in, h2_in, act_in, slope_in, out_in, gains,
    seg_col, seg_row, obs_row, cos, sin,
    layer_acts, grad_acts, out_sums, out_gains, hbm_sums, hbm_got, hbm_ring, du_hbm,
    gbuf, act, du, n, h2, x, dn, ga, proj, qkv, o, do, dcat, dhb, mask, wbuf, gain0, gain1, gain_buf,
    w_sem, l_sem, o_sem, a_sem, u_sem, q_sem, st_sem, y_send, y_recv, s1_send, s1_recv, s2_send, s2_recv, t_send, t_recv,
    *reduce_refs,
):
    section = lax.axis_index("section")
    first, second = section == 0, section != 0
    other = {"section": 1 - section}
    l, l2, l3 = (Links(n_dp, n_t) for _ in range(3))
    own = (a_own, i_own, d_own)
    rows, d = h2.shape
    wide = do.shape[1]
    places = Places(l)
    slots = places.slot
    order = [(m, j) for j in range(n_t) for m in (2, 1)] + [(0, j) for j in range(n_t)]
    ff = 2 * n_t
    hbm = (hbm_sums, hbm_got, hbm_ring)
    r = Reduce(l, places, order, out_sums, hbm, reduce_refs)
    rm = Reduce(l3, places, order, out_sums, hbm, reduce_refs)
    inner = places.below * places.above == 1
    end_first, inner_first = first & ~inner, first & inner
    r2 = Reduce(l2, places, order, out_sums, hbm, reduce_refs)
    spread1 = Spread(l, places, out_in, layer_acts, s1_send, s1_recv)
    spread1b = Spread(l2, places, out_in, layer_acts, s1_send, s1_recv)
    spread2 = Spread(l, places, dhb, grad_acts, s2_send, s2_recv)
    spread2b = Spread(l2, places, dhb, grad_acts, s2_send, s2_recv)
    load = Loader(wbuf, w_sem, [own[m] if j == n_t - 1 else full.at[m, slots[j]] for m, j in order])

    l.greet([{"tensor": l.up}, {"tensor": l.down}, other] + [{"dp": l.flip(b)} for b in l.bits])
    spread1.start()
    load.start(0)
    load.start(1)

    def local(src, dst, sem):
        return pltpu.make_async_copy(src, dst, sem)

    acts_in = local(out_in, dhb, l_sem.at[0])
    acts_out = local(dhb, layer_acts.at[l.z], l_sem.at[0])
    h2_copy = local(h2_in, h2, l_sem.at[1])
    x_copy = local(xs, x, l_sem.at[2])
    o_copies = [local(o_in.at[slots[j]], o.at[j], o_sem.at[j]) for j in range(n_t)]
    for c in (acts_in, h2_copy, x_copy, *o_copies):
        c.start()

    def act_copy(j):
        return local(act_in.at[slots[j]], act.at[j % 2], a_sem.at[j % 2])

    def slope_copy(j):
        return local(slope_in.at[slots[j]], du.at[j % 2], u_sem.at[j % 2])

    def du_out(j):
        return local(du.at[j % 2], du_hbm.at[slots[j]], st_sem.at[j % 2])

    def du_in(j):
        return local(du_hbm.at[slots[j]], du.at[j % 2], u_sem.at[j % 2])

    def qkv_copy(j):
        return local(qkv_in.at[slots[j]], qkv.at[j % 2], q_sem.at[j % 2])

    act_copy(0).start()
    slope_copy(0).start()
    write_mask(mask, seg_col, seg_row, obs_row)
    h2_copy.wait()
    norm_rows(h2, gains[1:2, :], n)
    acts_in.wait()
    acts_out.start()
    arrival = pltpu.make_async_remote_copy(
        src_ref=dhb, dst_ref=gbuf, send_sem=y_send, recv_sem=y_recv, device_id=other, device_id_type=MESH
    )
    cot_copy = local(cot, gbuf, l_sem.at[4])

    @pl.when(second)
    def _():
        cot_copy.start()
        cot_copy.wait()

    @pl.when(first)
    def _():
        for k in range(1, n_t - 1):
            spread1.step(k)
        arrival.wait_recv()

    def block_of(reducer, i):
        if i >= 3:
            reducer.clear(i)
        return reducer.block.at[i % 3]

    for j in range(n_t):
        if j + 1 < n_t:
            act_copy(j + 1).start()
            if j + 1 >= 2:
                du_out(j - 1).wait()
            slope_copy(j + 1).start()
        w = load.wait(2 * j)
        proj[...] = dot_nt(gbuf[...], w[...])
        load.start(2 * j + 2)
        slope_copy(j).wait()

        def scale(at):
            du[j % 2, at, :] = (proj[at, :] * du[j % 2, at, :].astype(F32)).astype(BF16)

        row_loop(rows, 32, scale)
        du_out(j).start()
        act_copy(j).wait()

        @pl.when(first)
        def _():
            r.pump()
            outer_product(block_of(r, 2 * j), gbuf, act.at[j % 2])
            r.pump()
            r.push(2 * j)

        w = load.wait(2 * j + 1)
        if j == 0:
            dn[...] = dot_nt(du[j % 2], w[...])
        else:
            dn[...] = dn[...] + dot_nt(du[j % 2], w[...])
        load.start(2 * j + 3)

        @pl.when(first)
        def _():
            r.pump()
            outer_product(block_of(r, 2 * j + 1), n, du.at[j % 2])
            r.pump()
            r.push(2 * j + 1)

        if j >= 2:
            @pl.when(end_first)
            def _():
                r.last_step(j - 2)

    for j in range(max(n_t - 2, 0), n_t):
        du_out(j).wait()

    qkv_copy(0).start()

    def write_middle(at, value):
        h2[at, :] = value
        ga[at, :] = value.astype(BF16)

    norm_back_rows(gbuf, dn, h2, gains[1:2, :], gain1, write_middle)
    for c in o_copies:
        c.wait()

    for j in range(n_t):
        if j + 1 < n_t:
            qkv_copy(j + 1).start()
        w = load.wait(ff + j)
        load.start(ff + j + 2)
        do[...] = dot_nt(ga[...], w[3 * wide:, :]).astype(BF16)
        qkv_copy(j).wait()
        @pl.when(first)
        def _():
            r.pump()

        attend_slot_back(qkv.at[j % 2], do, proj, dcat.at[j], mask)

        def turn_back(at):
            v = proj[at, 0:2 * wide]
            dcat[j, at, 0:2 * wide] = (v * cos[at, :] - partner(v) * sin[at, :]).astype(BF16)

        row_loop(rows, 32, turn_back)
        if j == 0:
            dn[...] = dot_nn(dcat[j], w[0:3 * wide, :])
        else:
            dn[...] = dn[...] + dot_nn(dcat[j], w[0:3 * wide, :])
        @pl.when(first)
        def _():
            r.pump()

        if j != 1:
            @pl.when(end_first)
            def _():
                r.last_step((2, None, 3, 4)[j])

        if j < 2:
            @pl.when(inner_first)
            def _():
                rm.last_step(j)
    x_copy.wait()
    acts_out.wait()

    def write_input(at, value):
        dhb[at, :] = value.astype(BF16)

    norm_back_rows(h2, dn, x, gains[0:1, :], gain0, write_input)
    over = pltpu.make_async_remote_copy(
        src_ref=dhb, dst_ref=gbuf, send_sem=y_send, recv_sem=y_recv, device_id=other, device_id_type=MESH
    )

    @pl.when(second)
    def _():
        over.start()

    spread2.start()
    grads_out = local(dhb, grad_acts.at[l.z], l_sem.at[0])
    grads_out.start()

    @pl.when(second)
    def _():
        du_in(0).start()
        act_copy(0).start()
        for j in range(n_t):
            if j + 1 < n_t:
                act_copy(j + 1).start()
                du_in(j + 1).start()
            act_copy(j).wait()
            outer_product(block_of(r2, 2 * j), gbuf, act.at[j % 2])
            r2.pump()
            r2.push(2 * j)
            du_in(j).wait()
            outer_product(block_of(r2, 2 * j + 1), n, du.at[j % 2])
            r2.pump()
            r2.push(2 * j + 1)
        spread1b.step(1)
        r2.flush()

    total = Total(l, gain0, gain_buf, t_send, t_recv)
    gain0[0:1, :] = jnp.sum(gain0[...], axis=0, keepdims=True)
    gain0[1:2, :] = jnp.sum(gain1[...], axis=0, keepdims=True)
    norm_rows(x, gains[0:1, :], n)
    for j in range(n_t):
        b = block_of(r, ff + j)
        step = d // 2

        def turn(c, _):
            at = pl.ds(pl.multiple_of(c * step, 128), step)
            b[at, 0:3 * wide] = dot_tn(n[:, at], dcat[j]).astype(BF16)
            b[at, 3 * wide:] = dot_tn(ga[:, at], o[j]).astype(BF16)
            return 0

        lax.fori_loop(0, 2, turn, 0)
        r.pump()
        r.push(ff + j)
    r.flush()

    @pl.when(inner_first)
    def _():
        for i in range(2, 5):
            rm.last_step(i)

    @pl.when(second)
    def _():
        for i in range(5):
            r2.last_step(i)
        for k in range(2, n_t - 1):
            spread1b.step(k)

    for i in range(5, len(order)):
        r.last_step(i)
        if i == 5 or i == 7:
            @pl.when(inner)
            def _():
                spread2.step((i - 3) // 2)
        if i >= 6 and i - 6 < total.count:
            total.step(i - 6)
    for t in range(len(order) - 6, total.count):
        total.step(t)
    l2.recording = False

    @pl.when(~inner)
    def _():
        for k in range(1, n_t - 1):
            spread2b.step(k)

    spread1.step(n_t - 1)
    spread2.step(n_t - 1)
    out_gains[...] = total.result()
    r.close()
    grads_out.wait()

    @pl.when(second)
    def _():
        over.wait_send()

    l.drain()


def run_backward(a_own, i_own, d_own, kept, cot, gains, seg, obs, tables):
    n_dp, n_t = lax.axis_size("dp"), lax.axis_size("tensor")
    rows, d = cot.shape
    wide = a_own.shape[0] // 4
    piece = d // n_dp
    count = 3 * n_t
    steps = len(ring_bits(n_dp)) + n_t
    dma = pltpu.SemaphoreType.DMA
    hbm, vmem = pl.BlockSpec(memory_space=pl.ANY), pl.BlockSpec(memory_space=pltpu.VMEM)

    def shape(*s, t=BF16):
        return jax.ShapeDtypeStruct(s, t)

    def buf(*s, t=BF16):
        return pltpu.VMEM(s, t)

    return pl.pallas_call(
        functools.partial(backward_kernel, n_dp, n_t),
        out_shape=[
            shape(n_t, rows, d), shape(n_t, rows, d), shape(3, piece, d, t=F32), shape(8, d, t=F32),
            *reduce_hbm(n_dp, n_t, count, piece, d), shape(n_t, rows, d),
        ],
        in_specs=[hbm] * 12 + [vmem] * 6,
        out_specs=[hbm] * 3 + [vmem] + [hbm] * 4,
        scratch_shapes=[
            buf(rows, d), buf(2, rows, d), buf(2, rows, d), buf(rows, d), buf(rows, d, t=F32), buf(rows, d),
            buf(rows, d, t=F32), buf(rows, d), buf(rows, d, t=F32), buf(2, rows, 3 * wide), buf(n_t, rows, wide),
            buf(rows, wide), buf(n_t, rows, 3 * wide), buf(rows, d), buf(ROW, 2 * QB, t=F32), buf(3, *a_own.shape),
            buf(8, d, t=F32), buf(8, d, t=F32), buf(2 * steps, 8, d, t=F32),
            dma((3,)), dma((5,)), dma((n_t,)), dma((2,)), dma((2,)), dma((2,)), dma((2,)), dma(()), dma(()),
            dma((2, n_t)), dma((2, n_t)), dma((2, n_t)), dma((2, n_t)), dma((steps,)), dma((steps,)),
            *reduce_scratch(n_dp, n_t, count, piece, d),
        ],
        compiler_params=pltpu.CompilerParams(collective_id=1, has_side_effects=True, vmem_limit_bytes=62 * 2**20),
    )(a_own, i_own, d_own, kept[0], cot, *kept[1:], gains, seg[:, None], seg[None, :], obs[None, :], *tables)


def own_rows(x, count):
    flat = x.reshape((-1,) + x.shape[2:])
    return lax.dynamic_slice_in_dim(flat, lax.axis_index("tensor") * count, count, 0)


def on_device(tokens, cotangent, seg_ids, observed, w_qkv, w_out, w_in, w_down, norm_gains):
    n_dp, n_t = lax.axis_size("dp"), lax.axis_size("tensor")
    w_qkv, w_out, w_in, w_down, gains = w_qkv[0], w_out[0], w_in[0], w_down[0], norm_gains[0]
    micro, rows, d = tokens.shape
    hd = w_out.shape[0]
    count = micro * rows // n_t
    tables = rope_tables()
    stack = jnp.concatenate([jnp.swapaxes(w_qkv, 1, 2), w_out[None]], axis=0).reshape(4 * hd, d)
    x0 = own_rows(tokens, count)
    g1 = own_rows(cotangent, count)
    seg, obs = own_rows(seg_ids, count), own_rows(observed, count)
    kept = run_forward(stack, w_in, w_down, x0, gains, seg, obs, tables)
    layer_acts, grad_acts, sums, gain = run_backward(stack, w_in, w_down, kept, g1, gains, seg, obs, tables)[:4]
    piece = d // n_dp
    gain = lax.dynamic_slice_in_dim(gain[:2], lax.axis_index("dp") * piece, piece, 1)
    r_attn, r_in, r_down = sums[0], sums[1], sums[2]
    r_qkv = jnp.stack([r_attn[:, i * hd:(i + 1) * hd] for i in range(3)])
    return (
        layer_acts.reshape(1, micro, rows, d),
        grad_acts.reshape(1, micro, rows, d),
        r_qkv[None],
        r_attn[:, 3 * hd:].T[None],
        r_in[None],
        r_down.T[None],
        gain[None],
    )


def solution(mesh):
    return jax.shard_map(
        on_device,
        mesh=mesh,
        in_specs=(
            P(None, "dp", None),
            P(None, "dp", None),
            P(None, "dp"),
            P(None, "dp"),
            P("section", None, None, "tensor"),
            P("section", "tensor", None),
            P("section", None, "tensor"),
            P("section", "tensor", None),
            P("section", None, None),
        ),
        out_specs=(
            P("section", None, "dp", None),
            P("section", None, "dp", None),
            P("section", None, "dp", "tensor"),
            P("section", "tensor", "dp"),
            P("section", "dp", "tensor"),
            P("section", "tensor", "dp"),
            P("section", None, "dp"),
        ),
        check_vma=False,
    )
```

```python
import functools
import math

import jax
import jax.numpy as jnp
import numpy as np
from jax import lax
from jax.experimental import pallas as pl
from jax.experimental.pallas import tpu as pltpu
from jax.sharding import PartitionSpec as P

HEAD_SIZE = 80
HALF = HEAD_SIZE // 2
ROW = 512
QB = 128
GROUP = 8
EPS = 1e-06
BIG = 1000000000.0
SCALE = 1.0 / math.sqrt(HEAD_SIZE)
BF16 = jnp.bfloat16
F32 = jnp.float32
MESH = pl.DeviceIdType.MESH


def dot_nn(a, b):
    return lax.dot_general(a, b, (((1,), (0,)), ((), ())), preferred_element_type=F32)


def dot_nt(a, b):
    return lax.dot_general(a, b, (((1,), (1,)), ((), ())), preferred_element_type=F32)


def dot_tn(a, b):
    return lax.dot_general(a, b, (((0,), (0,)), ((), ())), preferred_element_type=F32)


def rope_tables():
    freq = 10000.0 ** (-jnp.arange(HALF, dtype=F32) / HALF)
    ang = jnp.arange(ROW, dtype=F32)[:, None] * freq[None, :]
    cos, sin = jnp.cos(ang), jnp.sin(ang)
    cos_full = jnp.tile(jnp.concatenate([cos, cos], axis=1), (1, GROUP))
    sin_full = jnp.tile(jnp.concatenate([-sin, sin], axis=1), (1, GROUP))
    return cos_full, sin_full


def partner(x):
    width = x.shape[1]
    lane = lax.broadcasted_iota(jnp.int32, x.shape, 1)
    first = lax.rem(lane, HEAD_SIZE) < HALF
    return jnp.where(first, pltpu.roll(x, width - HALF, 1), pltpu.roll(x, HALF, 1))


def windows():
    return [max(i - 1, 0) * QB for i in range(ROW // QB)]


def write_mask(mask, seg_col, seg_row, obs_col):
    for i, k0 in enumerate(windows()):
        keys, queries = slice(k0, k0 + 2 * QB), slice(i * QB, (i + 1) * QB)
        shape = (2 * QB, QB)
        kj = lax.broadcasted_iota(jnp.int32, shape, 0) + k0
        qi = lax.broadcasted_iota(jnp.int32, shape, 1) + i * QB
        same = seg_col[keys, :] == seg_row[:, queries]
        seen = (obs_col[keys, :] == 1) | (kj == qi)
        mask[:, queries] = (same & (kj <= qi) & seen).astype(F32)


def query_block(x, i):
    return x[:, i * QB:(i + 1) * QB]


def by_window(keys, queries):
    return jnp.concatenate(
        [dot_nt(keys[k0:k0 + 2 * QB], queries[i * QB:(i + 1) * QB]) for i, k0 in enumerate(windows())], axis=1
    )


def to_queries(weights, keys):
    return jnp.concatenate(
        [dot_tn(query_block(weights, i), keys[k0:k0 + 2 * QB]) for i, k0 in enumerate(windows())], axis=0
    )


def to_keys(weights, queries):
    blocks = [None] * (ROW // QB)
    for i, k0 in enumerate(windows()):
        term = dot_nn(query_block(weights, i), queries[i * QB:(i + 1) * QB])
        for j in range(2):
            at, part = k0 // QB + j, term[j * QB:(j + 1) * QB]
            blocks[at] = part if blocks[at] is None else blocks[at] + part
    return jnp.concatenate(blocks, axis=0)


def probabilities(q, k, mask):
    s = jnp.where(mask[...] > 0, by_window(k, q) * SCALE, -BIG)
    e = jnp.exp(s - jnp.max(s, axis=0, keepdims=True))
    return e * (1.0 / jnp.sum(e, axis=0, keepdims=True))


def ring_bits(n):
    return [1 << i for i in range(n.bit_length() - 1)]


def low_bit(j):
    return j & -j


class Links:
    def __init__(self, n_dp, n_t):
        self.n_dp, self.n_t = n_dp, n_t
        self.me, self.z = lax.axis_index("dp"), lax.axis_index("tensor")
        self.down = lax.rem(self.z + n_t - 1, n_t)
        self.up = lax.rem(self.z + 1, n_t)
        self.bits = ring_bits(n_dp)
        self.sent, self.recording = {}, True

    def flip(self, bit):
        return self.me + bit - 2 * bit * lax.rem(self.me // bit, 2)

    def mix(self, j):
        at = self.me
        for bit in self.bits:
            if j & bit:
                at = at + bit - 2 * bit * lax.rem(self.me // bit, 2)
        return at

    def place(self, table):
        n = self.n_t
        return sum(v * (1 - ((self.z - k) * (self.z - k) + n * n - 1) // (n * n)) for k, v in enumerate(table))

    def own_bit(self, bit):
        return lax.rem(self.me // bit, 2)

    def greet(self, axes):
        barrier = pltpu.get_barrier_semaphore()
        for where in axes:
            pl.semaphore_signal(barrier, inc=1, device_id=where, device_id_type=MESH)
        pl.semaphore_wait(barrier, len(axes))

    def send(self, src, dst, send_sem, recv_sem, where, tag=None, again=None, when=None):
        pltpu.make_async_remote_copy(
            src_ref=src, dst_ref=dst, send_sem=send_sem, recv_sem=recv_sem, device_id=where, device_id_type=MESH
        ).start()
        if self.recording:
            self.sent.setdefault(tag, []).append((again or (lambda: (src, send_sem)), when))

    def finish(self, tag):
        def left(again):
            ref, sem = again()
            pltpu.make_async_remote_copy(
                src_ref=ref, dst_ref=ref, send_sem=sem, recv_sem=sem, device_id={"tensor": self.down}, device_id_type=MESH
            ).wait_send()

        for again, when in self.sent.pop(tag, ()):
            if when is None:
                left(again)
            else:
                pl.when(when())(functools.partial(left, again))

    def arrived(self, ref, sem, send_sem, where):
        pltpu.make_async_remote_copy(
            src_ref=ref, dst_ref=ref, send_sem=send_sem, recv_sem=sem, device_id=where, device_id_type=MESH
        ).wait_recv()

    def drain(self):
        for tag in list(self.sent):
            self.finish(tag)


class Gather:
    def __init__(self, links, own, full, parts, z_send, z_recv, p_send, p_recv):
        self.l, self.own, self.full, self.parts = links, own, full, parts
        self.z_send, self.z_recv, self.p_send, self.p_recv = z_send, z_recv, p_send, p_recv
        self.rows = own[0].shape[0] // links.n_dp
        self.units = [(m, k, h) for m, k in gather_order(links.n_t) for h in range(len(parts))]
        self.at = {u: i for i, u in enumerate(self.units)}

    def piece(self, m, slot, index, h):
        off, size = self.parts[h]
        first = pl.multiple_of(index * self.rows + off, 16)
        if slot == 0:
            return self.own[m].at[pl.ds(first, size), :]
        return self.full.at[m, slot, pl.ds(first, size), :]

    def like(self, h):
        return self.full.at[0, 1, pl.ds(0, self.parts[h][1]), :]

    def send_z(self, m, k, h):
        l = self.l
        i = self.at[(m, k, h)]
        l.send(self.piece(m, k - 1, l.me, h), self.piece(m, k, l.me, h), self.z_send.at[i], self.z_recv.at[i], {"tensor": l.down},
               again=lambda: (self.like(h), self.z_send.at[i]))

    def advance(self, taken):
        for unit in due(self.units, self.issued, taken, 2 * len(self.parts)):
            self.send_z(*unit)
            self.issued += 1

    def start(self):
        self.issued = 0
        self.advance(0)

    def share(self, i, j):
        m, k, h = self.units[i]
        l = self.l
        for bit in reversed(l.bits):
            if j == 0 or bit < low_bit(j):
                ref = self.piece(m, k, l.mix(j), h)
                l.send(ref, ref, self.p_send.at[i, j ^ bit], self.p_recv.at[i, j ^ bit], {"dp": l.flip(bit)},
                       again=lambda at=j ^ bit: (self.like(h), self.p_send.at[i, at]))

    def take(self, i):
        m, k, h = self.units[i]
        l = self.l
        l.arrived(self.piece(m, k, l.me, h), self.z_recv.at[i], self.z_send.at[i], {"tensor": l.up})
        self.advance(i + 1)
        self.share(i, 0)

    def relay(self, i):
        m, k, h = self.units[i]
        l = self.l
        for j in sorted(range(1, l.n_dp), key=lambda j: (-low_bit(j), j)):
            l.arrived(self.piece(m, k, l.mix(j), h), self.p_recv.at[i, j], self.p_send.at[i, j], {"dp": l.flip(low_bit(j))})
            self.share(i, j)

    def walk(self, lent=None, lag=2):
        for i in range(len(self.units) + lag):
            if i < len(self.units):
                m, k, h = self.units[i]
                self.take(i)
                if lent is not None and h == 0:
                    lent.take_back(m, k)
            done = None
            if i >= lag:
                self.relay(i - lag)
                m, k, h = self.units[i - lag]
                if h == len(self.parts) - 1:
                    if lent is not None:
                        lent.finish_back(m, k)
                    done = (m, k)
            yield done


class Lend:
    def __init__(self, links, own, full, held, y_send, y_recv, z_send, z_recv, p_send, p_recv, b_send, b_recv):
        self.l, self.own, self.full, self.held = links, own, full, held
        self.y_send, self.y_recv, self.z_send, self.z_recv = y_send, y_recv, z_send, z_recv
        self.p_send, self.p_recv, self.b_send, self.b_recv = p_send, p_recv, b_send, b_recv
        self.rows = own[0].shape[0] // links.n_dp
        self.size = held.shape[3]
        self.even = [j for j in range(0, links.n_dp, 2)]
        self.where = {"section": 1 - lax.axis_index("section")}

    def rows_of(self, j):
        return pl.ds(pl.multiple_of(self.l.mix(j) * self.rows, 16), self.size)

    def like(self):
        return self.held.at[0, 0, 0]

    def send(self, src, dst, sems, at, where):
        self.l.send(src, dst, sems[0].at[at], sems[1].at[at], where, again=lambda: (self.like(), sems[0].at[at]))

    def arrived(self, ref, sems, at):
        self.l.arrived(ref, sems[1].at[at], sems[0].at[at], self.where)

    def give(self):
        for m in range(3):
            self.send(self.own[m].at[self.rows_of(0), :], self.held.at[m, 0, self.l.me], (self.y_send, self.y_recv), (m,), self.where)

    def take_back(self, m, k):
        for j in self.even:
            ref = self.full.at[m, k, self.rows_of(j), :]
            self.arrived(ref, (self.b_send, self.b_recv), (m, k, j))
            self.send(ref, ref, (self.p_send, self.p_recv), (m, k, j + 1), {"dp": self.l.flip(1)})

    def finish_back(self, m, k):
        for j in self.even:
            self.arrived(self.full.at[m, k, self.rows_of(j + 1), :], (self.p_send, self.p_recv), (m, k, j + 1))

    def ring(self, m, k):
        l = self.l
        self.send(self.held.at[m, k - 1, l.me], self.held.at[m, k, l.me], (self.z_send, self.z_recv), (m, k), {"tensor": l.down})

    def back(self, m, k, j):
        l = self.l
        self.send(self.held.at[m, k, l.mix(j)], self.full.at[m, k, self.rows_of(j), :], (self.b_send, self.b_recv), (m, k, j), self.where)

    def share(self, m, k, j):
        l = self.l
        for bit in reversed(l.bits[1:]):
            if j == 0 or bit < low_bit(j):
                ref = self.held.at[m, k, l.mix(j)]
                self.send(ref, ref, (self.p_send, self.p_recv), (m, k, j ^ bit), {"dp": l.flip(bit)})

    def serve(self, lag=1):
        l = self.l
        units = gather_order(l.n_t)
        issued = 0
        started = False
        for i in range(len(units) + lag):
            for m, k in due(units, issued, i, 3):
                if k == 1:
                    self.arrived(self.held.at[m, 0, l.me], (self.y_send, self.y_recv), (m,))
                self.ring(m, k)
                issued += 1
            if issued == len(units) and not started:
                started = True
                yield
            if i < len(units):
                m, k = units[i]
                self.arrived(self.held.at[m, k, l.me], (self.z_send, self.z_recv), (m, k))
                self.share(m, k, 0)
                self.back(m, k, 0)
            if i >= lag:
                m, k = units[i - lag]
                for j in sorted(self.even[1:], key=lambda j: (-low_bit(j), j)):
                    self.arrived(self.held.at[m, k, l.mix(j)], (self.p_send, self.p_recv), (m, k, j))
                    self.share(m, k, j)
                    self.back(m, k, j)


def gather_order(n_t):
    heads = [(0, k) for k in range(1, n_t)]
    rest = [(m, k) for k in range(1, n_t) for m in (1, 2)]
    return [u for pair in zip(heads, rest) for u in pair] + rest[len(heads):]


def due(units, issued, taken, ahead):
    found = []
    while issued < min(len(units), taken + ahead):
        m, k, *h = units[issued]
        if k > 1 and units.index((m, k - 1, *h)) >= taken:
            break
        found.append(units[issued])
        issued += 1
    return found


def gather_parts(rows):
    lent = rows // 4 // 16 * 16
    if rows % 32:
        return lent, [(lent, rows - lent)], [(0, rows)]
    cut = lent + (rows - lent + 31) // 32 * 16
    return lent, [(lent, cut - lent), (cut, rows - cut)], [(0, rows // 2), (rows // 2, rows // 2)]


def level_start(n_dp, level):
    return sum(n_dp >> (t + 1) for t in range(level))


def add_rows(out, *terms):
    rows = out.shape[0]

    def body(r, _):
        at = pl.ds(pl.multiple_of(r * 16, 16), 16)
        total = terms[0][at, :].astype(F32)
        for t in terms[1:]:
            total = total + t[at, :].astype(F32)
        out[at, :] = total.astype(out.dtype)
        return 0

    lax.fori_loop(0, rows // 16, body, 0)


def reduce_scratch(n_dp, n_t, count, rows, c):
    dma = pltpu.SemaphoreType.DMA
    half = n_dp // 2
    return [
        pltpu.VMEM((3, n_dp * rows, c), BF16),
        pltpu.VMEM((2, half, rows, c), BF16),
        pltpu.VMEM((3, rows, c), BF16),
        pltpu.VMEM((3, rows, c), BF16),
        pltpu.VMEM((rows, c), F32),
        dma((count, n_dp)),
        dma((count, n_dp)),
        dma((count,)),
        dma((count // n_t, n_t, 2)),
        dma((2,)),
        dma((2,)),
        dma((3,)),
        dma(()),
    ]


def reduce_hbm(n_dp, n_t, count, rows, c):
    return [
        jax.ShapeDtypeStruct((count, n_dp // 2, rows, c), BF16),
        jax.ShapeDtypeStruct((count, n_dp - 1, rows, c), BF16),
        jax.ShapeDtypeStruct((count // n_t, n_t, 2, rows, c), BF16),
    ]


def line_order(n_t):
    return [sorted(range(n_t), key=lambda s: (-abs(s - z), -max(s, n_t - 1 - s))) for z in range(n_t)]


class Places:
    def __init__(self, links):
        n_t = links.n_t
        orders = line_order(n_t)
        self.shard = [links.place([o[j] for o in orders]) for j in range(n_t)]
        self.slot = [links.place([(o[j] - z) % n_t for z, o in enumerate(orders)]) for j in range(n_t - 1)] + [0]
        self.up = [links.place([int(o[j] > z) for z, o in enumerate(orders)]) for j in range(n_t)]
        self.below = (links.z + n_t - 1) // n_t
        self.above = (2 * n_t - 2 - links.z) // n_t


class Reduce:
    def __init__(self, links, places, order, out, hbm, scratch):
        self.l, self.places, self.order, self.out = links, places, order, out
        self.sums, self.got, self.ring = hbm
        (self.block, self.fetched, self.terms, self.moving, self.final,
         self.c_send, self.c_recv, self.z_send, self.z_recv,
         self.f_sem, self.s_sem, self.t_sem, self.o_sem) = scratch
        self.moves = []
        self.levels = len(links.bits)
        self.rows = self.fetched.shape[2]
        self.storing = None

    def offsets(self, level):
        bits = self.l.bits[level + 1:]
        return [sum(b for n, b in enumerate(bits) if k >> n & 1) for k in range(1 << len(bits))]

    def mine(self, level):
        return lax.rem(self.l.me, 1 << (level + 1))

    def give(self, i, level, source):
        l, bit = self.l, self.l.bits[level]
        there = self.mine(level) + bit - 2 * bit * l.own_bit(bit)
        for n, off in enumerate(self.offsets(level)):
            at = (i, level_start(l.n_dp, level) + n)
            l.send(source(there + off), self.got.at[at], self.c_send.at[at], self.c_recv.at[at], {"dp": l.flip(bit)}, (i, level),
                   again=lambda at=at: (self.got.at[at], self.c_send.at[at]))

    def receive(self, i, level):
        l = self.l
        for n, _ in enumerate(self.offsets(level)):
            at = (i, level_start(l.n_dp, level) + n)
            l.arrived(self.got.at[at], self.c_recv.at[at], self.c_send.at[at], {"dp": l.flip(l.bits[level])})

    def piece(self, i, p):
        return self.block.at[i % 3, pl.ds(pl.multiple_of(p * self.rows, 16), self.rows), :]

    def give_block(self, i):
        self.give(i, 0, lambda p: self.piece(i, p))

    def fetch_copy(self, i):
        return pltpu.make_async_copy(self.got.at[i, pl.ds(0, self.l.n_dp // 2)], self.fetched.at[i % 2], self.f_sem.at[i % 2])

    def fetch(self, i):
        self.receive(i, 0)
        self.fetch_copy(i).start()

    def store_copy(self, i):
        return pltpu.make_async_copy(self.fetched.at[i % 2], self.sums.at[i], self.s_sem.at[i % 2])

    def add_first(self, i):
        self.fetch_copy(i).wait()
        for n in range(self.l.n_dp // 2):
            here = self.fetched.at[i % 2, n]
            add_rows(here, self.piece(i, 2 * n + self.l.own_bit(1)), here)
        self.store_copy(i).start()

    def give_next(self, i):
        self.store_copy(i).wait()
        self.give(i, 1, lambda piece: self.sums.at[i, piece // 2])

    def push(self, i):
        self.give_block(i)
        self.moves.append([i, 0])

    def pump(self):
        for move in list(self.moves):
            i, stage = move
            if stage == 1 and any(o[0] == i - 2 for o in self.moves):
                break
            if stage > 0:
                (self.fetch, self.add_first, self.give_next)[stage - 1](i)
            move[1] += 1
            if move[1] == 4:
                self.moves.remove(move)

    def flush(self, i=None):
        while any(i is None or o[0] <= i for o in self.moves):
            self.pump()

    def clear(self, i):
        while any(o[0] == i - 3 and o[1] < 3 for o in self.moves):
            self.pump()
        self.l.finish((i - 3, 0))

    def middle(self, i, level):
        l = self.l
        self.receive(i, level)
        for n, off in enumerate(self.offsets(level)):
            piece = (self.mine(level) + off) // 2
            loads = [
                pltpu.make_async_copy(self.sums.at[i, piece], self.terms.at[0], self.t_sem.at[0]),
                pltpu.make_async_copy(self.got.at[i, level_start(l.n_dp, level) + n], self.terms.at[1], self.t_sem.at[1]),
            ]
            for c in loads:
                c.start()
            for c in loads:
                c.wait()
            add_rows(self.terms.at[2], self.terms.at[0], self.terms.at[1])
            back = pltpu.make_async_copy(self.terms.at[2], self.sums.at[i, piece], self.t_sem.at[2])
            back.start()
            back.wait()
        self.give(i, level + 1, lambda piece: self.sums.at[i, piece // 2])

    def term_copies(self, i):
        l = self.l
        return [
            pltpu.make_async_copy(self.sums.at[i, l.me // 2], self.terms.at[0], self.t_sem.at[0]),
            pltpu.make_async_copy(self.got.at[i, l.n_dp - 2], self.terms.at[1], self.t_sem.at[1]),
        ]

    def collect(self, i):
        self.receive(i, self.levels - 1)
        for c in self.term_copies(i):
            c.start()

    def out_copy(self, m):
        return pltpu.make_async_copy(self.final, self.out.at[m], self.o_sem)

    def come(self, m, s, way):
        l = self.l
        ref = self.ring.at[m, s, way]
        l.arrived(ref, self.z_recv.at[m, s, way], self.z_send.at[0], {"tensor": l.down})
        copy = pltpu.make_async_copy(ref, self.terms.at[2], self.t_sem.at[2])
        copy.start()
        copy.wait()

    def pass_on(self, i):
        l, p = self.l, self.places
        m, j = self.order[i]
        l.finish(("z", i - 3))
        terms = [self.terms.at[t] for t in range(3)]
        if j < l.n_t - 1:
            s, up, out = p.shard[j], p.up[j], self.moving.at[i % 3]
            behind = up * p.below + (1 - up) * p.above
            for c in self.term_copies(i):
                c.wait()

            @pl.when(behind == 1)
            def _():
                self.come(m, s, 1 - up)
                add_rows(out, *terms)

            @pl.when(behind == 0)
            def _():
                add_rows(out, *terms[:2])

            l.send(out, self.ring.at[m, s, 1 - up], self.z_send.at[i], self.z_recv.at[m, s, 1 - up], {"tensor": l.z + 2 * up - 1},
                   ("z", i), again=lambda: (self.moving.at[i % 3], self.z_send.at[i]))
        else:
            if self.storing is not None:
                self.out_copy(self.storing).wait()
            for c in self.term_copies(i):
                c.wait()
            add_rows(self.final, *terms[:2])
            for way, there in ((0, p.below), (1, p.above)):
                @pl.when(there == 1)
                def _():
                    self.come(m, l.z, way)
                    add_rows(self.final, self.final, terms[2])
            self.out_copy(m).start()
            self.storing = m

    def last_step(self, i):
        self.flush(i)
        for level in range(1, self.levels - 1):
            self.middle(i, level)
        self.collect(i)
        self.pass_on(i)

    def close(self):
        self.out_copy(self.storing).wait()


class Spread:
    def __init__(self, links, places, block, out, send, recv):
        self.l, self.places, self.block, self.out, self.send, self.recv = links, places, block, out, send, recv

    def pass_on(self, source, at, way, k):
        l, p = self.l, self.places
        l.send(source, self.out.at[at], self.send.at[way, k], self.recv.at[way, k], {"tensor": l.z + 1 - 2 * way},
               again=lambda: (self.out.at[0], self.send.at[way, k]),
               when=lambda: ((p.above, p.below)[way] == 1) if k == 0 else self.passes(way, k))

    def passes(self, way, k):
        z, n = self.l.z, self.l.n_t
        return (z >= k) & (z < n - 1) if way == 0 else (z < n - k) & (z > 0)

    def start(self):
        p = self.places
        for way, there in ((0, p.above), (1, p.below)):
            @pl.when(there == 1)
            def _():
                self.pass_on(self.block, self.l.z, way, 0)

    def step(self, k):
        l = self.l
        for way in range(2):
            at = l.z + k * (2 * way - 1)

            @pl.when(l.z >= k if way == 0 else l.z < l.n_t - k)
            def _():
                l.arrived(self.out.at[at], self.recv.at[way, k - 1], self.send.at[way, k - 1], {"tensor": l.down})

            if k < l.n_t - 1:
                @pl.when(self.passes(way, k))
                def _():
                    self.pass_on(self.out.at[at], at, way, k)


class Total:
    def __init__(self, links, block, buf, send, recv):
        self.l, self.block, self.buf, self.s, self.r = links, block, buf, send, recv
        self.levels = len(links.bits)
        self.count = self.levels + links.n_t

    def step(self, s):
        l, buf = self.l, self.buf
        if s == 0:
            buf[1] = self.block[...]
        else:
            l.arrived(buf.at[2 * s], self.r.at[s - 1], self.s.at[s - 1], {"tensor": l.up})
            if s <= self.levels:
                buf[2 * s + 1] = buf[2 * s - 1] + buf[2 * s]
        if s < self.levels:
            l.send(buf.at[2 * s + 1], buf.at[2 * s + 2], self.s.at[s], self.r.at[s], {"dp": l.flip(l.bits[s])})
        elif s < self.count - 1:
            src = 2 * s + 1 if s == self.levels else 2 * s
            l.send(buf.at[src], buf.at[2 * s + 2], self.s.at[s], self.r.at[s], {"tensor": l.down})

    def result(self):
        total = self.buf[2 * self.levels + 1]
        for k in range(1, self.l.n_t):
            total = total + self.buf[2 * (self.levels + k)]
        return total


def row_loop(rows, step, body):
    def turn(r, _):
        body(pl.ds(pl.multiple_of(r * step, step), step))
        return 0

    lax.fori_loop(0, rows // step, turn, 0)


def norm_rows(source, gain, out):
    def body(at):
        h = source[at, :].astype(F32)
        r = lax.rsqrt(jnp.mean(h * h, axis=1, keepdims=True) + EPS)
        out[at, :] = (h * r * gain).astype(BF16)

    row_loop(source.shape[0], 32, body)


def own_block(ref, z, rows):
    per = ref.shape[1] // rows
    return ref.at[z // per, pl.ds(pl.multiple_of(lax.rem(z, per) * rows, rows), rows), :]


def attend_slot(qkv, o, mask):
    heads = o.shape[1] // HEAD_SIZE
    for h in range(heads):
        q, k, v = (slice((t * heads + h) * HEAD_SIZE, (t * heads + h + 1) * HEAD_SIZE) for t in range(3))
        p = probabilities(qkv[:, q], qkv[:, k], mask).astype(BF16)
        o[:, q] = to_queries(p, qkv[:, v]).astype(BF16)


class Loader:
    def __init__(self, buf, sem, blocks):
        self.buf, self.sem, self.blocks = buf, sem, blocks

    def copy(self, j):
        slot = j % self.buf.shape[0]
        return pltpu.make_async_copy(self.blocks[j], self.buf.at[slot], self.sem.at[slot])

    def start(self, j):
        if j < len(self.blocks):
            self.copy(j).start()

    def wait(self, j):
        self.copy(j).wait()
        return self.buf.at[j % self.buf.shape[0]]


def forward_kernel(
    n_dp, n_t, a_own, i_own, d_own, x0, gains, seg_col, seg_row, obs_col, cos_in, sin_in,
    full, xs, qkv_out, o_out, h2_out, act_out, slope_out, out, held,
    x, n, proj, qkv, o, h2, acc, act, slope, outb, mask, wbuf, cos, sin,
    c_sem, w_sem, s_sem, y_send, y_recv, x_sem, z_send, z_recv, p_send, p_recv,
    *lend_sems,
):
    l, l1 = Links(n_dp, n_t), Links(n_dp, n_t)
    section = lax.axis_index("section")
    first, second = section == 0, section != 0
    own = (a_own, i_own, d_own)
    _, parts0, parts1 = gather_parts(a_own.shape[0] // n_dp)
    g0 = Gather(l, own, full, parts0, z_send, z_recv, p_send, p_recv)
    g1 = Gather(l1, own, full, parts1, z_send, z_recv, p_send, p_recv)
    lend0, lend1 = Lend(l, own, full, held, *lend_sems), Lend(l1, own, full, held, *lend_sems)
    other = {"section": 1 - section}
    l.greet([{"tensor": l.up}, other] + [{"dp": l.flip(b)} for b in l.bits])
    rows, d = x.shape
    wide = o.shape[2]

    def block(m, slot):
        return own[m] if slot == 0 else full.at[m, slot]

    order = [(0, s) for s in range(n_t)] + [(m, s) for s in range(n_t) for m in (1, 2)]
    load = Loader(wbuf, w_sem, [block(m, s) for m, s in order])
    stores = []

    def store(src, dst, sem):
        copy = pltpu.make_async_copy(src, dst, sem)
        copy.start()
        stores.append(copy)

    walks, here = (g0.walk(lend0), g1.walk()), (set(), set())

    def until(section, m, slot):
        while slot > 0 and (m, slot) not in here[section]:
            here[section].add(next(walks[section]))

    def tick(*sections):
        for at in sections:
            @pl.when((first, second)[at])
            def _():
                here[at].add(next(walks[at], None))

    tables = [pltpu.make_async_copy(t, to, c_sem.at[i]) for i, (t, to) in enumerate(((cos_in, cos), (sin_in, sin)))]
    for c in tables:
        c.start()

    @pl.when(first)
    def _():
        lend0.give()
        g0.start()
        copy = pltpu.make_async_copy(x0, x, x_sem)
        copy.start()
        copy.wait()

    write_mask(mask, seg_col, seg_row, obs_col)
    for c in tables:
        c.wait()

    @pl.when(second)
    def _():
        lending = lend1.serve()
        next(lending)
        g1.start()
        for _ in lending:
            pass
        until(1, 0, n_t - 1)
        load.start(0)
        load.start(1)
        until(1, 2, n_t - 2)
        pltpu.make_async_remote_copy(
            src_ref=outb, dst_ref=x, send_sem=y_send, recv_sem=y_recv, device_id=other, device_id_type=MESH
        ).wait_recv()

    store(x, xs, s_sem.at[0])
    norm_rows(x, gains[0:1, :], n)
    for s in range(n_t):
        @pl.when(first)
        def _():
            until(0, 0, s)
            load.start(s)

        @pl.when(second)
        def _():
            load.start(s + 2)

        w = load.wait(s)
        proj[:, 0:3 * wide] = dot_nt(n[...], w[0:3 * wide, :])

        def turn_rows(at):
            v = proj[at, 0:2 * wide]
            qkv[s, at, 0:2 * wide] = (v * cos[at, :] + partner(v) * sin[at, :]).astype(BF16)
            qkv[s, at, 2 * wide:3 * wide] = proj[at, 2 * wide:3 * wide].astype(BF16)

        row_loop(rows, 32, turn_rows)
        tick(0)
        attend_slot(qkv.at[s], o.at[s], mask)
        tick(0, 1)
        term = dot_nn(o[s], w[3 * wide:, :])
        if s == 0:
            acc[...] = term
        else:
            acc[...] = acc[...] + term
        store(qkv.at[s], qkv_out.at[s], s_sem.at[1 + s])
        store(o.at[s], o_out.at[s], s_sem.at[1 + n_t + s])

    def middle(at):
        h = x[at, :].astype(F32) + acc[at, :]
        h2[at, :] = h
        acc[at, :] = h
        r = lax.rsqrt(jnp.mean(h * h, axis=1, keepdims=True) + EPS)
        n[at, :] = (h * r * gains[1:2, :]).astype(BF16)

    row_loop(rows, 32, middle)
    store(h2, h2_out, s_sem.at[1 + 2 * n_t])
    spare = 2 + 2 * n_t
    for s in range(n_t):
        j = n_t + 2 * s

        @pl.when(first)
        def _():
            until(0, 2, s)
            load.start(j)
            load.start(j + 1)

        @pl.when(second)
        def _():
            if s == n_t - 1:
                until(1, 2, s)
                load.start(j)
                load.start(j + 1)
            elif s < n_t - 2:
                until(1, 1, s + 1)
                load.start(j + 2)

        w = load.wait(j)
        proj[...] = dot_nn(n[...], w[...])
        if s >= 2:
            for copy in stores[-4:-2]:
                copy.wait()
            del stores[-4:-2]

        def silu(at):
            u = proj[at, :]
            sig = lax.logistic(u)
            act[s % 2, at, :] = (u * sig).astype(BF16)
            slope[s % 2, at, :] = (sig * (1.0 + u * (1.0 - sig))).astype(BF16)

        row_loop(rows, 32, silu)
        tick(*((1,) if s == 0 else (0, 1)))

        @pl.when(second)
        def _():
            if s < n_t - 2:
                until(1, 2, s + 1)
                load.start(j + 3)

        w = load.wait(j + 1)
        acc[...] = acc[...] + dot_nn(act[s % 2], w[...])
        store(act.at[s % 2], act_out.at[s], s_sem.at[spare + 2 * (s % 2)])
        store(slope.at[s % 2], slope_out.at[s], s_sem.at[spare + 2 * (s % 2) + 1])

    def finish(at):
        outb[at, :] = acc[at, :].astype(BF16)

    row_loop(rows, 32, finish)
    assert all(len(h - {None}) == 3 * (n_t - 1) for h in here)
    over = pltpu.make_async_remote_copy(
        src_ref=outb, dst_ref=x, send_sem=y_send, recv_sem=y_recv, device_id=other, device_id_type=MESH
    )

    @pl.when(first)
    def _():
        over.start()

    store(outb, out, x_sem)
    for copy in stores:
        copy.wait()

    @pl.when(first)
    def _():
        over.wait_send()
        l.drain()

    @pl.when(second)
    def _():
        l1.drain()


def run_forward(a_own, i_own, d_own, x0, gains, seg, obs, tables):
    n_dp, n_t = lax.axis_size("dp"), lax.axis_size("tensor")
    rows, d = x0.shape
    wide = a_own.shape[0] // 4
    lent, parts, _ = gather_parts(a_own.shape[0] // n_dp)
    count = 3 * (n_t - 1) * len(parts)
    dma = pltpu.SemaphoreType.DMA
    hbm, vmem = pl.BlockSpec(memory_space=pl.ANY), pl.BlockSpec(memory_space=pltpu.VMEM)

    def shape(*s, t=BF16):
        return jax.ShapeDtypeStruct(s, t)

    return pl.pallas_call(
        functools.partial(forward_kernel, n_dp, n_t),
        out_shape=[
            shape(3, n_t, *a_own.shape), shape(rows, d), shape(n_t, rows, 3 * wide), shape(n_t, rows, wide),
            shape(rows, d, t=F32), shape(n_t, rows, i_own.shape[1]), shape(n_t, rows, i_own.shape[1]), shape(rows, d),
            shape(3, n_t, n_dp, lent, d),
        ],
        in_specs=[hbm] * 4 + [vmem] * 4 + [hbm] * 2,
        out_specs=[hbm] * 9,
        scratch_shapes=[
            pltpu.VMEM((rows, d), BF16),
            pltpu.VMEM((rows, d), BF16),
            pltpu.VMEM((rows, d), F32),
            pltpu.VMEM((n_t, rows, 3 * wide), BF16),
            pltpu.VMEM((n_t, rows, wide), BF16),
            pltpu.VMEM((rows, d), F32),
            pltpu.VMEM((rows, d), F32),
            pltpu.VMEM((2, rows, d), BF16),
            pltpu.VMEM((2, rows, d), BF16),
            pltpu.VMEM((rows, d), BF16),
            pltpu.VMEM((2 * QB, ROW), F32),
            pltpu.VMEM((3,) + a_own.shape, BF16),
            pltpu.VMEM(tables[0].shape, F32),
            pltpu.VMEM(tables[1].shape, F32),
            dma((2,)),
            dma((3,)), dma((6 + 2 * n_t,)), dma(()), dma(()), dma(()),
            dma((count,)), dma((count,)), dma((count, n_dp)), dma((count, n_dp)),
            dma((3,)), dma((3,)), dma((3, n_t)), dma((3, n_t)),
            dma((3, n_t, n_dp)), dma((3, n_t, n_dp)), dma((3, n_t, n_dp)), dma((3, n_t, n_dp)),
        ],
        compiler_params=pltpu.CompilerParams(collective_id=0, has_side_effects=True, vmem_limit_bytes=60 * 2**20),
    )(a_own, i_own, d_own, x0, gains, seg[:, None], seg[None, :], obs[:, None], *tables)


def attend_slot_back(qkv, do, dqk, dcat, mask):
    wide = do.shape[1]
    heads = wide // HEAD_SIZE
    for h in range(heads):
        q, k, v = (slice((t * heads + h) * HEAD_SIZE, (t * heads + h + 1) * HEAD_SIZE) for t in range(3))
        qh, kh, vh, dh = qkv[:, q], qkv[:, k], qkv[:, v], do[:, q]
        p = probabilities(qh, kh, mask)
        dcat[:, v] = to_keys(p.astype(BF16), dh).astype(BF16)
        dp = by_window(vh, dh)
        ds = (p * (dp - jnp.sum(p * dp, axis=0, keepdims=True))).astype(BF16)
        dqk[:, q] = to_queries(ds, kh) * SCALE
        dqk[:, k] = to_keys(ds, qh) * SCALE


def outer_product(out, left, right):
    step = left.shape[1] // 2

    def turn(j, _):
        at = pl.ds(pl.multiple_of(j * step, 128), step)
        out[at, :] = dot_tn(left[:, at], right[...]).astype(BF16)
        return 0

    lax.fori_loop(0, 2, turn, 0)


def norm_back_rows(g, dn, h, gain, gain_sum, normed, write):
    gain_sum[...] = jnp.zeros_like(gain_sum)
    step = 32

    def body(at):
        hr, dr = h[at, :].astype(F32), dn[at, :]
        r = lax.rsqrt(jnp.mean(hr * hr, axis=1, keepdims=True) + EPS)
        y = gain * dr
        if normed is not None:
            normed[at, :] = (hr * r * gain).astype(BF16)
        gain_sum[...] += jnp.sum((dr * hr * r).reshape(step // 8, 8, -1), axis=0)
        write(at, g[at, :].astype(F32) + r * y - hr * (r * r * r) * jnp.mean(hr * y, axis=1, keepdims=True))

    row_loop(h.shape[0], step, body)


def backward_kernel(
    n_dp, n_t, a_own, i_own, d_own, full, cot, xs, qkv_in, o_in, h2_in, act_in, slope_in, out_in, gains,
    seg_col, seg_row, obs_col, cos_in, sin_in,
    layer_acts, grad_acts, out_sums, out_gains, hbm_sums, hbm_got, hbm_ring, du_hbm,
    gbuf, act, du, n, h2, x, dn, ga, proj, qkv, o, do, dcat, dhb, mask, wbuf, cos, sin, gain0, gain1, gain_buf,
    c_sem, w_sem, l_sem, o_sem, a_sem, u_sem, q_sem, st_sem, y_send, y_recv, s1_send, s1_recv, s2_send, s2_recv, t_send, t_recv,
    *reduce_refs,
):
    section = lax.axis_index("section")
    first, second = section == 0, section != 0
    other = {"section": 1 - section}
    l, l2, l3 = (Links(n_dp, n_t) for _ in range(3))
    own = (a_own, i_own, d_own)
    rows, d = h2.shape
    wide = do.shape[1]
    places = Places(l)
    slots = places.slot
    order = [(m, j) for j in range(n_t) for m in (2, 1)] + [(0, j) for j in range(n_t)]
    ff = 2 * n_t
    hbm = (hbm_sums, hbm_got, hbm_ring)
    r = Reduce(l, places, order, out_sums, hbm, reduce_refs)
    rm = Reduce(l3, places, order, out_sums, hbm, reduce_refs)
    inner = places.below * places.above == 1
    end_first, inner_first = first & ~inner, first & inner
    r2 = Reduce(l2, places, order, out_sums, hbm, reduce_refs)
    spread1 = Spread(l, places, out_in, layer_acts, s1_send, s1_recv)
    spread1b = Spread(l2, places, out_in, layer_acts, s1_send, s1_recv)
    spread2 = Spread(l, places, dhb, grad_acts, s2_send, s2_recv)
    spread2b = Spread(l2, places, dhb, grad_acts, s2_send, s2_recv)
    load = Loader(wbuf, w_sem, [own[m] if j == n_t - 1 else full.at[m, slots[j]] for m, j in order])

    l.greet([{"tensor": l.up}, {"tensor": l.down}, other] + [{"dp": l.flip(b)} for b in l.bits])
    spread1.start()
    load.start(0)
    load.start(1)

    def local(src, dst, sem):
        return pltpu.make_async_copy(src, dst, sem)

    acts_in = local(out_in, dhb, l_sem.at[0])
    acts_out = local(dhb, layer_acts.at[l.z], l_sem.at[0])
    h2_copy = local(h2_in, h2, l_sem.at[1])
    x_copy = local(xs, x, l_sem.at[2])
    o_copies = [local(o_in.at[slots[j]], o.at[j], o_sem.at[j]) for j in range(n_t)]
    for c in (acts_in, h2_copy, x_copy, *o_copies):
        c.start()

    def act_copy(j):
        return local(act_in.at[slots[j]], act.at[j % 2], a_sem.at[j % 2])

    def slope_copy(j):
        return local(slope_in.at[slots[j]], du.at[j % 2], u_sem.at[j % 2])

    def du_out(j):
        return local(du.at[j % 2], du_hbm.at[slots[j]], st_sem.at[j % 2])

    def du_in(j):
        return local(du_hbm.at[slots[j]], du.at[j % 2], u_sem.at[j % 2])

    def qkv_copy(j):
        return local(qkv_in.at[slots[j]], qkv.at[j % 2], q_sem.at[j % 2])

    act_copy(0).start()
    slope_copy(0).start()
    tables = [local(t, to, c_sem.at[i]) for i, (t, to) in enumerate(((cos_in, cos), (sin_in, sin)))]
    for c in tables:
        c.start()
    write_mask(mask, seg_col, seg_row, obs_col)
    h2_copy.wait()

    @pl.when(first)
    def _():
        norm_rows(h2, gains[1:2, :], n)

    acts_in.wait()
    acts_out.start()
    arrival = pltpu.make_async_remote_copy(
        src_ref=dhb, dst_ref=gbuf, send_sem=y_send, recv_sem=y_recv, device_id=other, device_id_type=MESH
    )
    cot_copy = local(cot, gbuf, l_sem.at[4])

    @pl.when(second)
    def _():
        cot_copy.start()
        cot_copy.wait()

    @pl.when(first)
    def _():
        for k in range(1, n_t - 1):
            spread1.step(k)
        arrival.wait_recv()

    def block_of(reducer, i):
        if i >= 3:
            reducer.clear(i)
        return reducer.block.at[i % 3]

    for j in range(n_t):
        if j + 1 < n_t:
            act_copy(j + 1).start()
            if j + 1 >= 2:
                du_out(j - 1).wait()
            slope_copy(j + 1).start()
        w = load.wait(2 * j)
        proj[...] = dot_nt(gbuf[...], w[...])
        load.start(2 * j + 2)
        slope_copy(j).wait()

        def scale(at):
            du[j % 2, at, :] = (proj[at, :] * du[j % 2, at, :].astype(F32)).astype(BF16)

        row_loop(rows, 32, scale)
        du_out(j).start()
        act_copy(j).wait()

        @pl.when(first)
        def _():
            r.pump()
            outer_product(block_of(r, 2 * j), gbuf, act.at[j % 2])
            r.pump()
            r.push(2 * j)

        w = load.wait(2 * j + 1)
        if j == 0:
            dn[...] = dot_nt(du[j % 2], w[...])
        else:
            dn[...] = dn[...] + dot_nt(du[j % 2], w[...])
        load.start(2 * j + 3)

        @pl.when(first)
        def _():
            r.pump()
            outer_product(block_of(r, 2 * j + 1), n, du.at[j % 2])
            r.pump()
            r.push(2 * j + 1)

        if j >= 2:
            @pl.when(end_first)
            def _():
                r.last_step(j - 2)

    for j in range(max(n_t - 2, 0), n_t):
        du_out(j).wait()

    qkv_copy(0).start()

    def write_middle(at, value):
        h2[at, :] = value
        ga[at, :] = value.astype(BF16)

    norm_back_rows(gbuf, dn, h2, gains[1:2, :], gain1, n, write_middle)
    for c in (*o_copies, *tables):
        c.wait()

    for j in range(n_t):
        if j + 1 < n_t:
            qkv_copy(j + 1).start()
        w = load.wait(ff + j)
        load.start(ff + j + 2)
        do[...] = dot_nt(ga[...], w[3 * wide:, :]).astype(BF16)
        qkv_copy(j).wait()
        @pl.when(first)
        def _():
            r.pump()

        attend_slot_back(qkv.at[j % 2], do, proj, dcat.at[j], mask)

        def turn_back(at):
            v = proj[at, 0:2 * wide]
            dcat[j, at, 0:2 * wide] = (v * cos[at, :] - partner(v) * sin[at, :]).astype(BF16)

        row_loop(rows, 32, turn_back)
        if j == 0:
            dn[...] = dot_nn(dcat[j], w[0:3 * wide, :])
        else:
            dn[...] = dn[...] + dot_nn(dcat[j], w[0:3 * wide, :])
        @pl.when(first)
        def _():
            r.pump()

        if j != 1:
            @pl.when(end_first)
            def _():
                r.last_step((2, None, 3, 4)[j])

        if j < 2:
            @pl.when(inner_first)
            def _():
                rm.last_step(j)
    x_copy.wait()
    acts_out.wait()

    def write_input(at, value):
        dhb[at, :] = value.astype(BF16)

    norm_back_rows(h2, dn, x, gains[0:1, :], gain0, None, write_input)
    over = pltpu.make_async_remote_copy(
        src_ref=dhb, dst_ref=gbuf, send_sem=y_send, recv_sem=y_recv, device_id=other, device_id_type=MESH
    )

    @pl.when(second)
    def _():
        over.start()

    spread2.start()
    grads_out = local(dhb, grad_acts.at[l.z], l_sem.at[0])
    grads_out.start()

    @pl.when(second)
    def _():
        du_in(0).start()
        act_copy(0).start()
        for j in range(n_t):
            if j + 1 < n_t:
                act_copy(j + 1).start()
                du_in(j + 1).start()
            act_copy(j).wait()
            outer_product(block_of(r2, 2 * j), gbuf, act.at[j % 2])
            r2.pump()
            r2.push(2 * j)
            du_in(j).wait()
            outer_product(block_of(r2, 2 * j + 1), n, du.at[j % 2])
            r2.pump()
            r2.push(2 * j + 1)
        spread1b.step(1)
        r2.flush()

    total = Total(l, gain0, gain_buf, t_send, t_recv)
    gain0[0:1, :] = jnp.sum(gain0[...], axis=0, keepdims=True)
    gain0[1:2, :] = jnp.sum(gain1[...], axis=0, keepdims=True)
    norm_rows(x, gains[0:1, :], n)
    for j in range(n_t):
        b = block_of(r, ff + j)
        step = d // 2

        def turn(c, _):
            at = pl.ds(pl.multiple_of(c * step, 128), step)
            b[at, 0:3 * wide] = dot_tn(n[:, at], dcat[j]).astype(BF16)
            b[at, 3 * wide:] = dot_tn(ga[:, at], o[j]).astype(BF16)
            return 0

        lax.fori_loop(0, 2, turn, 0)
        r.pump()
        r.push(ff + j)
    r.flush()

    @pl.when(inner_first)
    def _():
        for i in range(2, 5):
            rm.last_step(i)

    @pl.when(second)
    def _():
        for i in range(5):
            r2.last_step(i)
        for k in range(2, n_t - 1):
            spread1b.step(k)

    for i in range(5, len(order)):
        r.last_step(i)
        if i == 5 or i == 7:
            @pl.when(inner)
            def _():
                spread2.step((i - 3) // 2)
        if i >= 6 and i - 6 < total.count:
            total.step(i - 6)
    for t in range(len(order) - 6, total.count):
        total.step(t)
    l2.recording = False

    @pl.when(~inner)
    def _():
        for k in range(1, n_t - 1):
            spread2b.step(k)

    spread1.step(n_t - 1)
    spread2.step(n_t - 1)
    out_gains[...] = total.result()
    r.close()
    grads_out.wait()

    @pl.when(second)
    def _():
        over.wait_send()

    l.drain()


def run_backward(a_own, i_own, d_own, kept, cot, gains, seg, obs, tables):
    n_dp, n_t = lax.axis_size("dp"), lax.axis_size("tensor")
    rows, d = cot.shape
    wide = a_own.shape[0] // 4
    piece = d // n_dp
    count = 3 * n_t
    steps = len(ring_bits(n_dp)) + n_t
    dma = pltpu.SemaphoreType.DMA
    hbm, vmem = pl.BlockSpec(memory_space=pl.ANY), pl.BlockSpec(memory_space=pltpu.VMEM)

    def shape(*s, t=BF16):
        return jax.ShapeDtypeStruct(s, t)

    def buf(*s, t=BF16):
        return pltpu.VMEM(s, t)

    return pl.pallas_call(
        functools.partial(backward_kernel, n_dp, n_t),
        out_shape=[
            shape(n_t, rows, d), shape(n_t, rows, d), shape(3, piece, d, t=F32), shape(8, d, t=F32),
            *reduce_hbm(n_dp, n_t, count, piece, d), shape(n_t, rows, d),
        ],
        in_specs=[hbm] * 12 + [vmem] * 4 + [hbm] * 2,
        out_specs=[hbm] * 3 + [vmem] + [hbm] * 4,
        scratch_shapes=[
            buf(rows, d), buf(2, rows, d), buf(2, rows, d), buf(rows, d), buf(rows, d, t=F32), buf(rows, d),
            buf(rows, d, t=F32), buf(rows, d), buf(rows, d, t=F32), buf(2, rows, 3 * wide), buf(n_t, rows, wide),
            buf(rows, wide), buf(n_t, rows, 3 * wide), buf(rows, d), buf(2 * QB, ROW, t=F32), buf(3, *a_own.shape),
            buf(*tables[0].shape, t=F32), buf(*tables[1].shape, t=F32),
            buf(8, d, t=F32), buf(8, d, t=F32), buf(2 * steps, 8, d, t=F32),
            dma((2,)), dma((3,)), dma((5,)), dma((n_t,)), dma((2,)), dma((2,)), dma((2,)), dma((2,)), dma(()), dma(()),
            dma((2, n_t)), dma((2, n_t)), dma((2, n_t)), dma((2, n_t)), dma((steps,)), dma((steps,)),
            *reduce_scratch(n_dp, n_t, count, piece, d),
        ],
        compiler_params=pltpu.CompilerParams(collective_id=1, has_side_effects=True, vmem_limit_bytes=62 * 2**20),
    )(a_own, i_own, d_own, kept[0], cot, *kept[1:], gains, seg[:, None], seg[None, :], obs[:, None], *tables)


def own_rows(x, count):
    flat = x.reshape((-1,) + x.shape[2:])
    return lax.dynamic_slice_in_dim(flat, lax.axis_index("tensor") * count, count, 0)


def on_device(tokens, cotangent, seg_ids, observed, w_qkv, w_out, w_in, w_down, norm_gains):
    n_dp, n_t = lax.axis_size("dp"), lax.axis_size("tensor")
    w_qkv, w_out, w_in, w_down, gains = w_qkv[0], w_out[0], w_in[0], w_down[0], norm_gains[0]
    micro, rows, d = tokens.shape
    hd = w_out.shape[0]
    count = micro * rows // n_t
    tables = rope_tables()
    stack = jnp.concatenate([jnp.swapaxes(w_qkv, 1, 2), w_out[None]], axis=0).reshape(4 * hd, d)
    seg, obs = own_rows(seg_ids, count), own_rows(observed, count)
    kept = run_forward(stack, w_in, w_down, own_rows(tokens, count), gains, seg, obs, tables)[:8]
    layer_acts, grad_acts, sums, gain = run_backward(stack, w_in, w_down, kept, own_rows(cotangent, count), gains, seg, obs, tables)[:4]
    piece = d // n_dp
    gain = lax.dynamic_slice_in_dim(gain[:2], lax.axis_index("dp") * piece, piece, 1)
    r_attn, r_in, r_down = sums[0], sums[1], sums[2]
    r_qkv = jnp.stack([r_attn[:, i * hd:(i + 1) * hd] for i in range(3)])
    return (
        layer_acts.reshape(1, micro, rows, d),
        grad_acts.reshape(1, micro, rows, d),
        r_qkv[None],
        r_attn[:, 3 * hd:].T[None],
        r_in[None],
        r_down.T[None],
        gain[None],
    )


def solution(mesh):
    return jax.shard_map(
        on_device,
        mesh=mesh,
        in_specs=(
            P(None, "dp", None),
            P(None, "dp", None),
            P(None, "dp"),
            P(None, "dp"),
            P("section", None, None, "tensor"),
            P("section", "tensor", None),
            P("section", None, "tensor"),
            P("section", "tensor", None),
            P("section", None, None),
        ),
        out_specs=(
            P("section", None, "dp", None),
            P("section", None, "dp", None),
            P("section", None, "dp", "tensor"),
            P("section", "tensor", "dp"),
            P("section", "dp", "tensor"),
            P("section", "tensor", "dp"),
            P("section", None, "dp"),
        ),
        check_vma=False,
    )
```

```python
import functools
import math

import jax
import jax.numpy as jnp
import numpy as np
from jax import lax
from jax.experimental import pallas as pl
from jax.experimental.pallas import tpu as pltpu
from jax.sharding import PartitionSpec as P

HEAD_SIZE = 80
HALF = HEAD_SIZE // 2
ROW = 512
QB = 128
GROUP = 8
EPS = 1e-06
BIG = 1000000000.0
SCALE = 1.0 / math.sqrt(HEAD_SIZE)
BF16 = jnp.bfloat16
F32 = jnp.float32
MESH = pl.DeviceIdType.MESH


def dot_nn(a, b):
    return lax.dot_general(a, b, (((1,), (0,)), ((), ())), preferred_element_type=F32)


def dot_nt(a, b):
    return lax.dot_general(a, b, (((1,), (1,)), ((), ())), preferred_element_type=F32)


def dot_tn(a, b):
    return lax.dot_general(a, b, (((0,), (0,)), ((), ())), preferred_element_type=F32)


def rope_tables():
    freq = 10000.0 ** (-jnp.arange(HALF, dtype=F32) / HALF)
    ang = jnp.arange(ROW, dtype=F32)[:, None] * freq[None, :]
    cos, sin = jnp.cos(ang), jnp.sin(ang)
    cos_full = jnp.tile(jnp.concatenate([cos, cos], axis=1), (1, GROUP))
    sin_full = jnp.tile(jnp.concatenate([-sin, sin], axis=1), (1, GROUP))
    return cos_full, sin_full


def partner(x):
    width = x.shape[1]
    lane = lax.broadcasted_iota(jnp.int32, x.shape, 1)
    first = lax.rem(lane, HEAD_SIZE) < HALF
    return jnp.where(first, pltpu.roll(x, width - HALF, 1), pltpu.roll(x, HALF, 1))


def windows():
    return [max(i - 1, 0) * QB for i in range(ROW // QB)]


def write_mask(mask, seg_col, seg_row, obs_col):
    for i, k0 in enumerate(windows()):
        keys, queries = slice(k0, k0 + 2 * QB), slice(i * QB, (i + 1) * QB)
        shape = (2 * QB, QB)
        kj = lax.broadcasted_iota(jnp.int32, shape, 0) + k0
        qi = lax.broadcasted_iota(jnp.int32, shape, 1) + i * QB
        same = seg_col[keys, :] == seg_row[:, queries]
        seen = (obs_col[keys, :] == 1) | (kj == qi)
        mask[:, queries] = (same & (kj <= qi) & seen).astype(F32)


def query_block(x, i):
    return x[:, i * QB:(i + 1) * QB]


def by_window(keys, queries):
    return jnp.concatenate(
        [dot_nt(keys[k0:k0 + 2 * QB], queries[i * QB:(i + 1) * QB]) for i, k0 in enumerate(windows())], axis=1
    )


def to_queries(weights, keys):
    return jnp.concatenate(
        [dot_tn(query_block(weights, i), keys[k0:k0 + 2 * QB]) for i, k0 in enumerate(windows())], axis=0
    )


def to_keys(weights, queries):
    blocks = [None] * (ROW // QB)
    for i, k0 in enumerate(windows()):
        term = dot_nn(query_block(weights, i), queries[i * QB:(i + 1) * QB])
        for j in range(2):
            at, part = k0 // QB + j, term[j * QB:(j + 1) * QB]
            blocks[at] = part if blocks[at] is None else blocks[at] + part
    return jnp.concatenate(blocks, axis=0)


def probabilities(q, k, mask):
    s = jnp.where(mask[...] > 0, by_window(k, q) * SCALE, -BIG)
    e = jnp.exp(s - jnp.max(s, axis=0, keepdims=True))
    return e * (1.0 / jnp.sum(e, axis=0, keepdims=True))


def ring_bits(n):
    return [1 << i for i in range(n.bit_length() - 1)]


def low_bit(j):
    return j & -j


class Links:
    def __init__(self, n_dp, n_t):
        self.n_dp, self.n_t = n_dp, n_t
        self.me, self.z = lax.axis_index("dp"), lax.axis_index("tensor")
        self.down = lax.rem(self.z + n_t - 1, n_t)
        self.up = lax.rem(self.z + 1, n_t)
        self.bits = ring_bits(n_dp)
        self.sent, self.recording = {}, True

    def flip(self, bit):
        return self.me + bit - 2 * bit * lax.rem(self.me // bit, 2)

    def mix(self, j):
        at = self.me
        for bit in self.bits:
            if j & bit:
                at = at + bit - 2 * bit * lax.rem(self.me // bit, 2)
        return at

    def place(self, table):
        n = self.n_t
        return sum(v * (1 - ((self.z - k) * (self.z - k) + n * n - 1) // (n * n)) for k, v in enumerate(table))

    def own_bit(self, bit):
        return lax.rem(self.me // bit, 2)

    def greet(self, axes):
        barrier = pltpu.get_barrier_semaphore()
        for where in axes:
            pl.semaphore_signal(barrier, inc=1, device_id=where, device_id_type=MESH)
        pl.semaphore_wait(barrier, len(axes))

    def send(self, src, dst, send_sem, recv_sem, where, tag=None, again=None, when=None):
        pltpu.make_async_remote_copy(
            src_ref=src, dst_ref=dst, send_sem=send_sem, recv_sem=recv_sem, device_id=where, device_id_type=MESH
        ).start()
        if self.recording:
            self.sent.setdefault(tag, []).append((again or (lambda: (src, send_sem)), when))

    def finish(self, tag):
        def left(again):
            ref, sem = again()
            pltpu.make_async_remote_copy(
                src_ref=ref, dst_ref=ref, send_sem=sem, recv_sem=sem, device_id={"tensor": self.down}, device_id_type=MESH
            ).wait_send()

        for again, when in self.sent.pop(tag, ()):
            if when is None:
                left(again)
            else:
                pl.when(when())(functools.partial(left, again))

    def arrived(self, ref, sem, send_sem, where):
        pltpu.make_async_remote_copy(
            src_ref=ref, dst_ref=ref, send_sem=send_sem, recv_sem=sem, device_id=where, device_id_type=MESH
        ).wait_recv()

    def drain(self):
        for tag in list(self.sent):
            self.finish(tag)


class Gather:
    def __init__(self, links, own, full, parts, z_send, z_recv, p_send, p_recv):
        self.l, self.own, self.full, self.parts = links, own, full, parts
        self.z_send, self.z_recv, self.p_send, self.p_recv = z_send, z_recv, p_send, p_recv
        self.rows = own[0].shape[0] // links.n_dp
        self.units = [(m, k, h) for m, k in gather_order(links.n_t) for h in range(len(parts))]
        self.at = {u: i for i, u in enumerate(self.units)}

    def piece(self, m, slot, index, h):
        off, size = self.parts[h]
        first = pl.multiple_of(index * self.rows + off, 16)
        if slot == 0:
            return self.own[m].at[pl.ds(first, size), :]
        return self.full.at[m, slot, pl.ds(first, size), :]

    def like(self, h):
        return self.full.at[0, 1, pl.ds(0, self.parts[h][1]), :]

    def send_z(self, m, k, h):
        l = self.l
        i = self.at[(m, k, h)]
        l.send(self.piece(m, k - 1, l.me, h), self.piece(m, k, l.me, h), self.z_send.at[i], self.z_recv.at[i], {"tensor": l.down},
               again=lambda: (self.like(h), self.z_send.at[i]))

    def advance(self, taken):
        for unit in due(self.units, self.issued, taken, 2 * len(self.parts)):
            self.send_z(*unit)
            self.issued += 1

    def start(self):
        self.issued = 0
        self.advance(0)

    def share(self, i, j):
        m, k, h = self.units[i]
        l = self.l
        for bit in reversed(l.bits):
            if j == 0 or bit < low_bit(j):
                ref = self.piece(m, k, l.mix(j), h)
                l.send(ref, ref, self.p_send.at[i, j ^ bit], self.p_recv.at[i, j ^ bit], {"dp": l.flip(bit)},
                       again=lambda at=j ^ bit: (self.like(h), self.p_send.at[i, at]))

    def take(self, i):
        m, k, h = self.units[i]
        l = self.l
        l.arrived(self.piece(m, k, l.me, h), self.z_recv.at[i], self.z_send.at[i], {"tensor": l.up})
        self.advance(i + 1)
        self.share(i, 0)

    def relay(self, i, bit):
        m, k, h = self.units[i]
        l = self.l
        for j in range(bit, l.n_dp, 2 * bit):
            l.arrived(self.piece(m, k, l.mix(j), h), self.p_recv.at[i, j], self.p_send.at[i, j], {"dp": l.flip(low_bit(j))})
            self.share(i, j)

    def walk(self, lent=None, lag=2):
        hops = self.l.bits[::-1]
        for i in range(len(self.units) + lag + len(hops) - 1):
            if i < len(self.units):
                m, k, h = self.units[i]
                self.take(i)
                if lent is not None and h == 0:
                    lent.take_back(m, k)
            done = None
            for hop, bit in enumerate(hops):
                at = i - lag - hop
                if 0 <= at < len(self.units):
                    self.relay(at, bit)
                    m, k, h = self.units[at]
                    if hop == len(hops) - 1 and h == len(self.parts) - 1:
                        if lent is not None:
                            lent.finish_back(m, k)
                        done = (m, k)
            yield done


class Lend:
    def __init__(self, links, own, full, held, y_send, y_recv, z_send, z_recv, p_send, p_recv, b_send, b_recv):
        self.l, self.own, self.full, self.held = links, own, full, held
        self.y_send, self.y_recv, self.z_send, self.z_recv = y_send, y_recv, z_send, z_recv
        self.p_send, self.p_recv, self.b_send, self.b_recv = p_send, p_recv, b_send, b_recv
        self.rows = own[0].shape[0] // links.n_dp
        self.size = held.shape[3]
        self.even = [j for j in range(0, links.n_dp, 2)]
        self.where = {"section": 1 - lax.axis_index("section")}

    def rows_of(self, j):
        return pl.ds(pl.multiple_of(self.l.mix(j) * self.rows, 16), self.size)

    def like(self):
        return self.held.at[0, 0, 0]

    def send(self, src, dst, sems, at, where):
        self.l.send(src, dst, sems[0].at[at], sems[1].at[at], where, again=lambda: (self.like(), sems[0].at[at]))

    def arrived(self, ref, sems, at):
        self.l.arrived(ref, sems[1].at[at], sems[0].at[at], self.where)

    def give(self):
        for m in range(3):
            self.send(self.own[m].at[self.rows_of(0), :], self.held.at[m, 0, self.l.me], (self.y_send, self.y_recv), (m,), self.where)

    def take_back(self, m, k):
        for j in self.even:
            ref = self.full.at[m, k, self.rows_of(j), :]
            self.arrived(ref, (self.b_send, self.b_recv), (m, k, j))
            self.send(ref, ref, (self.p_send, self.p_recv), (m, k, j + 1), {"dp": self.l.flip(1)})

    def finish_back(self, m, k):
        for j in self.even:
            self.arrived(self.full.at[m, k, self.rows_of(j + 1), :], (self.p_send, self.p_recv), (m, k, j + 1))

    def ring(self, m, k):
        l = self.l
        self.send(self.held.at[m, k - 1, l.me], self.held.at[m, k, l.me], (self.z_send, self.z_recv), (m, k), {"tensor": l.down})

    def back(self, m, k, j):
        l = self.l
        self.send(self.held.at[m, k, l.mix(j)], self.full.at[m, k, self.rows_of(j), :], (self.b_send, self.b_recv), (m, k, j), self.where)

    def share(self, m, k, j):
        l = self.l
        for bit in reversed(l.bits[1:]):
            if j == 0 or bit < low_bit(j):
                ref = self.held.at[m, k, l.mix(j)]
                self.send(ref, ref, (self.p_send, self.p_recv), (m, k, j ^ bit), {"dp": l.flip(bit)})

    def serve(self, lag=1):
        l = self.l
        units = gather_order(l.n_t)
        issued = 0
        started = False
        for i in range(len(units) + lag):
            for m, k in due(units, issued, i, 3):
                if k == 1:
                    self.arrived(self.held.at[m, 0, l.me], (self.y_send, self.y_recv), (m,))
                self.ring(m, k)
                issued += 1
            if issued == len(units) and not started:
                started = True
                yield
            if i < len(units):
                m, k = units[i]
                self.arrived(self.held.at[m, k, l.me], (self.z_send, self.z_recv), (m, k))
                self.share(m, k, 0)
                self.back(m, k, 0)
            if i >= lag:
                m, k = units[i - lag]
                for j in sorted(self.even[1:], key=lambda j: (-low_bit(j), j)):
                    self.arrived(self.held.at[m, k, l.mix(j)], (self.p_send, self.p_recv), (m, k, j))
                    self.share(m, k, j)
                    self.back(m, k, j)


def gather_order(n_t):
    heads = [(0, k) for k in range(1, n_t)]
    rest = [(m, k) for k in range(1, n_t) for m in (1, 2)]
    return [u for pair in zip(heads, rest) for u in pair] + rest[len(heads):]


def due(units, issued, taken, ahead):
    found = []
    while issued < min(len(units), taken + ahead):
        m, k, *h = units[issued]
        if k > 1 and units.index((m, k - 1, *h)) >= taken:
            break
        found.append(units[issued])
        issued += 1
    return found


def gather_parts(rows):
    lent = rows // 4 // 16 * 16
    if rows % 32:
        return lent, [(lent, rows - lent)], [(0, rows)]
    cut = lent + (rows - lent + 31) // 32 * 16
    return lent, [(lent, cut - lent), (cut, rows - cut)], [(0, rows // 2), (rows // 2, rows // 2)]


def level_start(n_dp, level):
    return sum(n_dp >> (t + 1) for t in range(level))


def add_rows(out, *terms):
    rows = out.shape[0]

    def body(r, _):
        at = pl.ds(pl.multiple_of(r * 16, 16), 16)
        total = terms[0][at, :].astype(F32)
        for t in terms[1:]:
            total = total + t[at, :].astype(F32)
        out[at, :] = total.astype(out.dtype)
        return 0

    lax.fori_loop(0, rows // 16, body, 0)


def reduce_scratch(n_dp, n_t, count, rows, c):
    dma = pltpu.SemaphoreType.DMA
    half = n_dp // 2
    return [
        pltpu.VMEM((3, n_dp * rows, c), BF16),
        pltpu.VMEM((2, half, rows, c), BF16),
        pltpu.VMEM((3, rows, c), BF16),
        pltpu.VMEM((3, rows, c), BF16),
        pltpu.VMEM((rows, c), F32),
        dma((count, n_dp)),
        dma((count, n_dp)),
        dma((count,)),
        dma((count // n_t, n_t, 2)),
        dma((2,)),
        dma((2,)),
        dma((3,)),
        dma(()),
    ]


def reduce_hbm(n_dp, n_t, count, rows, c):
    return [
        jax.ShapeDtypeStruct((count, n_dp // 2, rows, c), BF16),
        jax.ShapeDtypeStruct((count, n_dp - 1, rows, c), BF16),
        jax.ShapeDtypeStruct((count // n_t, n_t, 2, rows, c), BF16),
    ]


def line_order(n_t):
    return [sorted(range(n_t), key=lambda s: (-abs(s - z), -max(s, n_t - 1 - s))) for z in range(n_t)]


class Places:
    def __init__(self, links):
        n_t = links.n_t
        orders = line_order(n_t)
        self.shard = [links.place([o[j] for o in orders]) for j in range(n_t)]
        self.slot = [links.place([(o[j] - z) % n_t for z, o in enumerate(orders)]) for j in range(n_t - 1)] + [0]
        self.up = [links.place([int(o[j] > z) for z, o in enumerate(orders)]) for j in range(n_t)]
        self.below = (links.z + n_t - 1) // n_t
        self.above = (2 * n_t - 2 - links.z) // n_t


def travel_order(order):
    if len(order) != 12:
        return list(range(len(order)))
    return [0, 1, 2, 3, 4, 8, 5, 9, 6, 10, 7, 11]


class Reduce:
    def __init__(self, links, places, order, out, hbm, scratch):
        self.l, self.places, self.order, self.out = links, places, order, out
        self.sums, self.got, self.ring = hbm
        (self.block, self.fetched, self.terms, self.moving, self.final,
         self.c_send, self.c_recv, self.z_send, self.z_recv,
         self.f_sem, self.s_sem, self.t_sem, self.o_sem) = scratch
        self.moves = []
        self.queue = travel_order(order)
        self.stored, self.gone = set(), 0
        self.levels = len(links.bits)
        self.rows = self.fetched.shape[2]
        self.storing = None

    def offsets(self, level):
        bits = self.l.bits[level + 1:]
        return [sum(b for n, b in enumerate(bits) if k >> n & 1) for k in range(1 << len(bits))]

    def mine(self, level):
        return lax.rem(self.l.me, 1 << (level + 1))

    def give(self, i, level, source):
        l, bit = self.l, self.l.bits[level]
        there = self.mine(level) + bit - 2 * bit * l.own_bit(bit)
        for n, off in enumerate(self.offsets(level)):
            at = (i, level_start(l.n_dp, level) + n)
            l.send(source(there + off), self.got.at[at], self.c_send.at[at], self.c_recv.at[at], {"dp": l.flip(bit)}, (i, level),
                   again=lambda at=at: (self.got.at[at], self.c_send.at[at]))

    def receive(self, i, level):
        l = self.l
        for n, _ in enumerate(self.offsets(level)):
            at = (i, level_start(l.n_dp, level) + n)
            l.arrived(self.got.at[at], self.c_recv.at[at], self.c_send.at[at], {"dp": l.flip(l.bits[level])})

    def piece(self, i, p):
        return self.block.at[i % 3, pl.ds(pl.multiple_of(p * self.rows, 16), self.rows), :]

    def give_block(self, i):
        self.give(i, 0, lambda p: self.piece(i, p))

    def fetch_copy(self, i):
        return pltpu.make_async_copy(self.got.at[i, pl.ds(0, self.l.n_dp // 2)], self.fetched.at[i % 2], self.f_sem.at[i % 2])

    def fetch(self, i):
        self.receive(i, 0)
        self.fetch_copy(i).start()

    def store_copy(self, i):
        return pltpu.make_async_copy(self.fetched.at[i % 2], self.sums.at[i], self.s_sem.at[i % 2])

    def add_first(self, i):
        self.fetch_copy(i).wait()
        for n in range(self.l.n_dp // 2):
            here = self.fetched.at[i % 2, n]
            add_rows(here, self.piece(i, 2 * n + self.l.own_bit(1)), here)
        self.store_copy(i).start()

    def give_next(self, i):
        self.store_copy(i).wait()
        self.stored.add(i)
        while self.gone < len(self.queue) and self.queue[self.gone] in self.stored:
            at = self.queue[self.gone]
            self.give(at, 1, lambda piece: self.sums.at[at, piece // 2])
            self.gone += 1

    def push(self, i):
        self.give_block(i)
        self.moves.append([i, 0])

    def pump(self):
        for move in list(self.moves):
            i, stage = move
            if stage == 0 and any(o[0] == i - 2 for o in self.moves):
                break
            (self.fetch, self.add_first, self.give_next)[stage](i)
            move[1] += 1
            if move[1] == 3:
                self.moves.remove(move)

    def flush(self, i=None):
        while any(i is None or o[0] == i for o in self.moves):
            self.pump()

    def clear(self, i):
        while any(o[0] == i - 3 and o[1] < 2 for o in self.moves):
            self.pump()
        self.l.finish((i - 3, 0))

    def middle(self, i, level):
        l = self.l
        self.receive(i, level)
        for n, off in enumerate(self.offsets(level)):
            piece = (self.mine(level) + off) // 2
            loads = [
                pltpu.make_async_copy(self.sums.at[i, piece], self.terms.at[0], self.t_sem.at[0]),
                pltpu.make_async_copy(self.got.at[i, level_start(l.n_dp, level) + n], self.terms.at[1], self.t_sem.at[1]),
            ]
            for c in loads:
                c.start()
            for c in loads:
                c.wait()
            add_rows(self.terms.at[2], self.terms.at[0], self.terms.at[1])
            back = pltpu.make_async_copy(self.terms.at[2], self.sums.at[i, piece], self.t_sem.at[2])
            back.start()
            back.wait()
        self.give(i, level + 1, lambda piece: self.sums.at[i, piece // 2])

    def term_copies(self, i):
        l = self.l
        return [
            pltpu.make_async_copy(self.sums.at[i, l.me // 2], self.terms.at[0], self.t_sem.at[0]),
            pltpu.make_async_copy(self.got.at[i, l.n_dp - 2], self.terms.at[1], self.t_sem.at[1]),
        ]

    def collect(self, i):
        self.receive(i, self.levels - 1)
        for c in self.term_copies(i):
            c.start()

    def out_copy(self, m):
        return pltpu.make_async_copy(self.final, self.out.at[m], self.o_sem)

    def come(self, m, s, way):
        l = self.l
        ref = self.ring.at[m, s, way]
        l.arrived(ref, self.z_recv.at[m, s, way], self.z_send.at[0], {"tensor": l.down})
        copy = pltpu.make_async_copy(ref, self.terms.at[2], self.t_sem.at[2])
        copy.start()
        copy.wait()

    def pass_on(self, i, turn):
        l, p = self.l, self.places
        m, j = self.order[i]
        l.finish(("z", turn - 3))
        terms = [self.terms.at[t] for t in range(3)]
        if j < l.n_t - 1:
            s, up, out = p.shard[j], p.up[j], self.moving.at[turn % 3]
            behind = up * p.below + (1 - up) * p.above
            for c in self.term_copies(i):
                c.wait()

            @pl.when(behind == 1)
            def _():
                self.come(m, s, 1 - up)
                add_rows(out, *terms)

            @pl.when(behind == 0)
            def _():
                add_rows(out, *terms[:2])

            l.send(out, self.ring.at[m, s, 1 - up], self.z_send.at[i], self.z_recv.at[m, s, 1 - up], {"tensor": l.z + 2 * up - 1},
                   ("z", turn), again=lambda: (self.moving.at[turn % 3], self.z_send.at[i]))
        else:
            if self.storing is not None:
                self.out_copy(self.storing).wait()
            for c in self.term_copies(i):
                c.wait()
            add_rows(self.final, *terms[:2])
            for way, there in ((0, p.below), (1, p.above)):
                @pl.when(there == 1)
                def _():
                    self.come(m, l.z, way)
                    add_rows(self.final, self.final, terms[2])
            self.out_copy(m).start()
            self.storing = m

    def last_step(self, turn):
        i = self.queue[turn]
        for before in self.queue[:turn + 1]:
            self.flush(before)
        for level in range(1, self.levels - 1):
            self.middle(i, level)
        self.collect(i)
        self.pass_on(i, turn)

    def close(self):
        self.out_copy(self.storing).wait()


class Spread:
    def __init__(self, links, places, block, out, send, recv):
        self.l, self.places, self.block, self.out, self.send, self.recv = links, places, block, out, send, recv

    def pass_on(self, source, at, way, k):
        l, p = self.l, self.places
        l.send(source, self.out.at[at], self.send.at[way, k], self.recv.at[way, k], {"tensor": l.z + 1 - 2 * way},
               again=lambda: (self.out.at[0], self.send.at[way, k]),
               when=lambda: ((p.above, p.below)[way] == 1) if k == 0 else self.passes(way, k))

    def passes(self, way, k):
        z, n = self.l.z, self.l.n_t
        return (z >= k) & (z < n - 1) if way == 0 else (z < n - k) & (z > 0)

    def start(self):
        p = self.places
        for way, there in ((0, p.above), (1, p.below)):
            @pl.when(there == 1)
            def _():
                self.pass_on(self.block, self.l.z, way, 0)

    def step(self, k):
        l = self.l
        for way in range(2):
            at = l.z + k * (2 * way - 1)

            @pl.when(l.z >= k if way == 0 else l.z < l.n_t - k)
            def _():
                l.arrived(self.out.at[at], self.recv.at[way, k - 1], self.send.at[way, k - 1], {"tensor": l.down})

            if k < l.n_t - 1:
                @pl.when(self.passes(way, k))
                def _():
                    self.pass_on(self.out.at[at], at, way, k)


class Total:
    def __init__(self, links, block, buf, send, recv):
        self.l, self.block, self.buf, self.s, self.r = links, block, buf, send, recv
        self.levels = len(links.bits)
        self.count = self.levels + links.n_t

    def step(self, s):
        l, buf = self.l, self.buf
        if s == 0:
            buf[1] = self.block[...]
        else:
            l.arrived(buf.at[2 * s], self.r.at[s - 1], self.s.at[s - 1], {"tensor": l.up})
            if s <= self.levels:
                buf[2 * s + 1] = buf[2 * s - 1] + buf[2 * s]
        if s < self.levels:
            l.send(buf.at[2 * s + 1], buf.at[2 * s + 2], self.s.at[s], self.r.at[s], {"dp": l.flip(l.bits[s])})
        elif s < self.count - 1:
            src = 2 * s + 1 if s == self.levels else 2 * s
            l.send(buf.at[src], buf.at[2 * s + 2], self.s.at[s], self.r.at[s], {"tensor": l.down})

    def result(self):
        total = self.buf[2 * self.levels + 1]
        for k in range(1, self.l.n_t):
            total = total + self.buf[2 * (self.levels + k)]
        return total


def row_loop(rows, step, body):
    def turn(r, _):
        body(pl.ds(pl.multiple_of(r * step, step), step))
        return 0

    lax.fori_loop(0, rows // step, turn, 0)


def column_steps(width):
    return [slice(c, c + 256) for c in range(0, width, 256)]


def norm_rows(source, gain, out):
    def body(at):
        h = source[at, :].astype(F32)
        r = lax.rsqrt(jnp.mean(h * h, axis=1, keepdims=True) + EPS)
        out[at, :] = (h * r * gain).astype(BF16)

    row_loop(source.shape[0], 32, body)


def own_block(ref, z, rows):
    per = ref.shape[1] // rows
    return ref.at[z // per, pl.ds(pl.multiple_of(lax.rem(z, per) * rows, rows), rows), :]


def attend_slot(qkv, o, mask):
    heads = o.shape[1] // HEAD_SIZE
    for h in range(heads):
        q, k, v = (slice((t * heads + h) * HEAD_SIZE, (t * heads + h + 1) * HEAD_SIZE) for t in range(3))
        p = probabilities(qkv[:, q], qkv[:, k], mask).astype(BF16)
        o[:, q] = to_queries(p, qkv[:, v]).astype(BF16)


class Loader:
    def __init__(self, buf, sem, blocks):
        self.buf, self.sem, self.blocks = buf, sem, blocks

    def copy(self, j):
        slot = j % self.buf.shape[0]
        return pltpu.make_async_copy(self.blocks[j], self.buf.at[slot], self.sem.at[slot])

    def start(self, j):
        if j < len(self.blocks):
            self.copy(j).start()

    def wait(self, j):
        self.copy(j).wait()
        return self.buf.at[j % self.buf.shape[0]]


PARTS = 2


def over_part(src, dst, send, recv, where, c):
    size = src.shape[0] // PARTS
    at = pl.ds(c * size, size)
    return pltpu.make_async_remote_copy(
        src_ref=src.at[at, :], dst_ref=dst.at[at, :], send_sem=send.at[c], recv_sem=recv.at[c],
        device_id=where, device_id_type=MESH,
    )


def forward_kernel(
    n_dp, n_t, a_own, i_own, d_own, x0, gains, seg_col, seg_row, obs_col, cos_in, sin_in,
    full, xs, qkv_out, o_out, h2_out, act_out, slope_out, out, held,
    x, n, proj, qkv, o, h2, acc, act, slope, outb, mask, wbuf, cos, sin,
    c_sem, w_sem, s_sem, y_send, y_recv, x_sem, z_send, z_recv, p_send, p_recv,
    *lend_sems,
):
    l, l1 = Links(n_dp, n_t), Links(n_dp, n_t)
    section = lax.axis_index("section")
    first, second = section == 0, section != 0
    own = (a_own, i_own, d_own)
    _, parts0, parts1 = gather_parts(a_own.shape[0] // n_dp)
    g0 = Gather(l, own, full, parts0, z_send, z_recv, p_send, p_recv)
    g1 = Gather(l1, own, full, parts1, z_send, z_recv, p_send, p_recv)
    lend0, lend1 = Lend(l, own, full, held, *lend_sems), Lend(l1, own, full, held, *lend_sems)
    other = {"section": 1 - section}
    l.greet([{"tensor": l.up}, other] + [{"dp": l.flip(b)} for b in l.bits])
    rows, d = x.shape
    wide = o.shape[2]

    def block(m, slot):
        return own[m] if slot == 0 else full.at[m, slot]

    order = [(0, s) for s in range(n_t)] + [(m, s) for s in range(n_t) for m in (1, 2)]
    load = Loader(wbuf, w_sem, [block(m, s) for m, s in order])
    stores = []

    def store(src, dst, sem):
        copy = pltpu.make_async_copy(src, dst, sem)
        copy.start()
        stores.append(copy)

    walks, here = (g0.walk(lend0), g1.walk()), (set(), set())

    def until(section, m, slot):
        while slot > 0 and (m, slot) not in here[section]:
            here[section].add(next(walks[section]))

    def tick(*sections):
        for at in sections:
            @pl.when((first, second)[at])
            def _():
                here[at].add(next(walks[at], None))

    tables = [pltpu.make_async_copy(t, to, c_sem.at[i]) for i, (t, to) in enumerate(((cos_in, cos), (sin_in, sin)))]
    for c in tables:
        c.start()

    @pl.when(first)
    def _():
        lend0.give()
        g0.start()
        copy = pltpu.make_async_copy(x0, x, x_sem)
        copy.start()
        copy.wait()

    write_mask(mask, seg_col, seg_row, obs_col)
    for c in tables:
        c.wait()

    @pl.when(second)
    def _():
        lending = lend1.serve()
        next(lending)
        g1.start()
        for _ in lending:
            pass
        until(1, 0, n_t - 1)
        load.start(0)
        load.start(1)
        until(1, 1, n_t - 2)
        for c in range(PARTS):
            over_part(outb, x, y_send, y_recv, other, c).wait_recv()

    store(x, xs, s_sem.at[0])
    norm_rows(x, gains[0:1, :], n)
    for s in range(n_t):
        @pl.when(first)
        def _():
            until(0, 0, s)
            load.start(s)

        @pl.when(second)
        def _():
            load.start(s + 2)

        w = load.wait(s)
        proj[:, 0:3 * wide] = dot_nt(n[...], w[0:3 * wide, :])

        def turn_rows(at):
            v = proj[at, 0:2 * wide]
            qkv[s, at, 0:2 * wide] = (v * cos[at, :] + partner(v) * sin[at, :]).astype(BF16)
            qkv[s, at, 2 * wide:3 * wide] = proj[at, 2 * wide:3 * wide].astype(BF16)

        row_loop(rows, 32, turn_rows)
        tick(0)
        attend_slot(qkv.at[s], o.at[s], mask)
        tick(0, 1)
        term = dot_nn(o[s], w[3 * wide:, :])
        if s == 0:
            acc[...] = term
        else:
            acc[...] = acc[...] + term
        store(qkv.at[s], qkv_out.at[s], s_sem.at[1 + s])
        store(o.at[s], o_out.at[s], s_sem.at[1 + n_t + s])

    def middle(at):
        h = x[at, :].astype(F32) + acc[at, :]
        h2[at, :] = h
        acc[at, :] = h
        r = lax.rsqrt(jnp.mean(h * h, axis=1, keepdims=True) + EPS)
        n[at, :] = (h * r * gains[1:2, :]).astype(BF16)

    row_loop(rows, 32, middle)
    store(h2, h2_out, s_sem.at[1 + 2 * n_t])
    spare = 2 + 2 * n_t
    for s in range(n_t):
        j = n_t + 2 * s

        @pl.when(first)
        def _():
            until(0, 1 if s == n_t - 1 else 2, s)
            load.start(j)
            if s < n_t - 1:
                load.start(j + 1)

        @pl.when(second)
        def _():
            if s == n_t - 1:
                until(1, 2, s)
                load.start(j)
                load.start(j + 1)
            elif s < n_t - 2:
                until(1, 1, s + 1)
                load.start(j + 2)

        w = load.wait(j)
        if s >= 2:
            for copy in stores[-4:-2]:
                copy.wait()
            del stores[-4:-2]
        for c in column_steps(act.shape[2]):
            u = dot_nn(n[...], w[:, c])
            sig = lax.logistic(u)
            act[s % 2, :, c] = (u * sig).astype(BF16)
            slope[s % 2, :, c] = (sig * (1.0 + u * (1.0 - sig))).astype(BF16)
        tick(*((1,) if s == 0 else (0, 1)))

        @pl.when(first)
        def _():
            if s == n_t - 1:
                until(0, 2, s)
                load.start(j + 1)

        @pl.when(second)
        def _():
            if s < n_t - 2:
                until(1, 2, s + 1)
                load.start(j + 3)

        w = load.wait(j + 1)
        if s < n_t - 1:
            acc[...] = acc[...] + dot_nn(act[s % 2], w[...])
        else:
            for c in range(PARTS):
                at = slice(c * rows // PARTS, (c + 1) * rows // PARTS)
                outb[at, :] = (acc[at, :] + dot_nn(act[s % 2, at, :], w[...])).astype(BF16)

                @pl.when(first)
                def _():
                    over_part(outb, x, y_send, y_recv, other, c).start()

        store(act.at[s % 2], act_out.at[s], s_sem.at[spare + 2 * (s % 2)])
        store(slope.at[s % 2], slope_out.at[s], s_sem.at[spare + 2 * (s % 2) + 1])

    assert all(len(h - {None}) == 3 * (n_t - 1) for h in here)
    store(outb, out, x_sem)
    for copy in stores:
        copy.wait()

    @pl.when(first)
    def _():
        for c in range(PARTS):
            over_part(outb, x, y_send, y_recv, other, c).wait_send()
        l.drain()

    @pl.when(second)
    def _():
        l1.drain()


def run_forward(a_own, i_own, d_own, x0, gains, seg, obs, tables):
    n_dp, n_t = lax.axis_size("dp"), lax.axis_size("tensor")
    rows, d = x0.shape
    wide = a_own.shape[0] // 4
    lent, parts, _ = gather_parts(a_own.shape[0] // n_dp)
    count = 3 * (n_t - 1) * len(parts)
    dma = pltpu.SemaphoreType.DMA
    hbm, vmem = pl.BlockSpec(memory_space=pl.ANY), pl.BlockSpec(memory_space=pltpu.VMEM)

    def shape(*s, t=BF16):
        return jax.ShapeDtypeStruct(s, t)

    return pl.pallas_call(
        functools.partial(forward_kernel, n_dp, n_t),
        out_shape=[
            shape(3, n_t, *a_own.shape), shape(rows, d), shape(n_t, rows, 3 * wide), shape(n_t, rows, wide),
            shape(rows, d, t=F32), shape(n_t, rows, i_own.shape[1]), shape(n_t, rows, i_own.shape[1]), shape(rows, d),
            shape(3, n_t, n_dp, lent, d),
        ],
        in_specs=[hbm] * 4 + [vmem] * 4 + [hbm] * 2,
        out_specs=[hbm] * 9,
        scratch_shapes=[
            pltpu.VMEM((rows, d), BF16),
            pltpu.VMEM((rows, d), BF16),
            pltpu.VMEM((rows, d), F32),
            pltpu.VMEM((n_t, rows, 3 * wide), BF16),
            pltpu.VMEM((n_t, rows, wide), BF16),
            pltpu.VMEM((rows, d), F32),
            pltpu.VMEM((rows, d), F32),
            pltpu.VMEM((2, rows, d), BF16),
            pltpu.VMEM((2, rows, d), BF16),
            pltpu.VMEM((rows, d), BF16),
            pltpu.VMEM((2 * QB, ROW), F32),
            pltpu.VMEM((3,) + a_own.shape, BF16),
            pltpu.VMEM(tables[0].shape, F32),
            pltpu.VMEM(tables[1].shape, F32),
            dma((2,)),
            dma((3,)), dma((6 + 2 * n_t,)), dma((PARTS,)), dma((PARTS,)), dma(()),
            dma((count,)), dma((count,)), dma((count, n_dp)), dma((count, n_dp)),
            dma((3,)), dma((3,)), dma((3, n_t)), dma((3, n_t)),
            dma((3, n_t, n_dp)), dma((3, n_t, n_dp)), dma((3, n_t, n_dp)), dma((3, n_t, n_dp)),
        ],
        compiler_params=pltpu.CompilerParams(collective_id=0, has_side_effects=True, vmem_limit_bytes=60 * 2**20),
    )(a_own, i_own, d_own, x0, gains, seg[:, None], seg[None, :], obs[:, None], *tables)


def attend_slot_back(qkv, do, dqk, dcat, mask):
    wide = do.shape[1]
    heads = wide // HEAD_SIZE
    for h in range(heads):
        q, k, v = (slice((t * heads + h) * HEAD_SIZE, (t * heads + h + 1) * HEAD_SIZE) for t in range(3))
        qh, kh, vh, dh = qkv[:, q], qkv[:, k], qkv[:, v], do[:, q]
        p = probabilities(qh, kh, mask)
        dcat[:, v] = to_keys(p.astype(BF16), dh).astype(BF16)
        dp = by_window(vh, dh)
        ds = (p * (dp - jnp.sum(p * dp, axis=0, keepdims=True))).astype(BF16)
        dqk[:, q] = to_queries(ds, kh) * SCALE
        dqk[:, k] = to_keys(ds, qh) * SCALE


def outer_product(out, left, right):
    step = left.shape[1] // 2

    def turn(j, _):
        at = pl.ds(pl.multiple_of(j * step, 128), step)
        out[at, :] = dot_tn(left[:, at], right[...]).astype(BF16)
        return 0

    lax.fori_loop(0, 2, turn, 0)


def norm_back_rows(g, dn, h, gain, gain_sum, normed, write, part=0, parts=1):
    if part == 0:
        gain_sum[...] = jnp.zeros_like(gain_sum)
    step = 32
    count = h.shape[0] // step // parts

    def body(at):
        hr, dr = h[at, :].astype(F32), dn[at, :]
        r = lax.rsqrt(jnp.mean(hr * hr, axis=1, keepdims=True) + EPS)
        y = gain * dr
        if normed is not None:
            normed[at, :] = (hr * r * gain).astype(BF16)
        gain_sum[...] += jnp.sum((dr * hr * r).reshape(step // 8, 8, -1), axis=0)
        write(at, g[at, :].astype(F32) + r * y - hr * (r * r * r) * jnp.mean(hr * y, axis=1, keepdims=True))

    def turn(r, _):
        body(pl.ds(pl.multiple_of((part * count + r) * step, step), step))
        return 0

    lax.fori_loop(0, count, turn, 0)


def backward_kernel(
    n_dp, n_t, a_own, i_own, d_own, full, cot, xs, qkv_in, o_in, h2_in, act_in, slope_in, out_in, gains,
    seg_col, seg_row, obs_col, cos_in, sin_in,
    layer_acts, grad_acts, out_sums, out_gains, hbm_sums, hbm_got, hbm_ring, du_hbm,
    gbuf, act, du, n, h2, x, dn, ga, proj, qkv, o, do, dcat, dhb, mask, wbuf, cos, sin, gain0, gain1, gain_buf,
    c_sem, w_sem, l_sem, o_sem, a_sem, u_sem, q_sem, st_sem, y_send, y_recv, s1_send, s1_recv, s2_send, s2_recv, t_send, t_recv,
    *reduce_refs,
):
    section = lax.axis_index("section")
    first, second = section == 0, section != 0
    other = {"section": 1 - section}
    l, l2, l3 = (Links(n_dp, n_t) for _ in range(3))
    own = (a_own, i_own, d_own)
    rows, d = h2.shape
    wide = do.shape[1]
    places = Places(l)
    slots = places.slot
    order = [(m, j) for j in range(n_t) for m in (2, 1)] + [(0, j) for j in range(n_t)]
    ff = 2 * n_t
    hbm = (hbm_sums, hbm_got, hbm_ring)
    r = Reduce(l, places, order, out_sums, hbm, reduce_refs)
    rm = Reduce(l3, places, order, out_sums, hbm, reduce_refs)
    inner = places.below * places.above == 1
    end_first, inner_first = first & ~inner, first & inner
    r2 = Reduce(l2, places, order, out_sums, hbm, reduce_refs)
    spread1 = Spread(l, places, out_in, layer_acts, s1_send, s1_recv)
    spread1b = Spread(l2, places, out_in, layer_acts, s1_send, s1_recv)
    spread2 = Spread(l, places, dhb, grad_acts, s2_send, s2_recv)
    spread2b = Spread(l2, places, dhb, grad_acts, s2_send, s2_recv)
    load = Loader(wbuf, w_sem, [own[m] if j == n_t - 1 else full.at[m, slots[j]] for m, j in order])

    l.greet([{"tensor": l.up}, {"tensor": l.down}, other] + [{"dp": l.flip(b)} for b in l.bits])
    cot_copy = pltpu.make_async_copy(cot, gbuf, l_sem.at[4])

    @pl.when(second)
    def _():
        cot_copy.start()

    def local(src, dst, sem):
        return pltpu.make_async_copy(src, dst, sem)

    load.start(0)
    load.start(1)
    spread1.start()

    acts_in = local(out_in, dhb, l_sem.at[0])
    acts_out = local(dhb, layer_acts.at[l.z], l_sem.at[0])
    h2_copy = local(h2_in, h2, l_sem.at[1])
    x_copy = local(xs, x, l_sem.at[2])
    o_copies = [local(o_in.at[slots[j]], o.at[j], o_sem.at[j]) for j in range(n_t)]

    def act_copy(j):
        return local(act_in.at[slots[j]], act.at[j % 2], a_sem.at[j % 2])

    def slope_copy(j):
        return local(slope_in.at[slots[j]], du.at[j % 2], u_sem.at[j % 2])

    def du_out(j):
        return local(du.at[j % 2], du_hbm.at[slots[j]], st_sem.at[j % 2])

    def du_in(j):
        return local(du_hbm.at[slots[j]], du.at[j % 2], u_sem.at[j % 2])

    def qkv_copy(j):
        return local(qkv_in.at[slots[j]], qkv.at[j % 2], q_sem.at[j % 2])

    slope_copy(0).start()
    act_copy(0).start()
    for c in (h2_copy, acts_in, x_copy, *o_copies):
        c.start()
    tables = [local(t, to, c_sem.at[i]) for i, (t, to) in enumerate(((cos_in, cos), (sin_in, sin)))]
    for c in tables:
        c.start()
    write_mask(mask, seg_col, seg_row, obs_col)

    @pl.when(first)
    def _():
        h2_copy.wait()
        norm_rows(h2, gains[1:2, :], n)

    @pl.when(second)
    def _():
        cot_copy.wait()

    @pl.when(first)
    def _():
        for k in range(1, n_t - 1):
            spread1.step(k)
        for c in range(PARTS):
            over_part(dhb, gbuf, y_send, y_recv, other, c).wait_recv()

    def block_of(reducer, i):
        if i >= 3:
            reducer.clear(i)
        return reducer.block.at[i % 3]

    for j in range(n_t):
        if j + 1 < n_t:
            act_copy(j + 1).start()
            if j + 1 >= 2:
                du_out(j - 1).wait()
            slope_copy(j + 1).start()
        act_copy(j).wait()

        @pl.when(first)
        def _():
            outer_product(block_of(r, 2 * j), gbuf, act.at[j % 2])
            r.pump()
            r.push(2 * j)

        w = load.wait(2 * j)
        slope_copy(j).wait()
        for c in column_steps(act.shape[2]):
            du[j % 2, :, c] = (dot_nt(gbuf[...], w[c, :]) * du[j % 2, :, c].astype(F32)).astype(BF16)
        load.start(2 * j + 2)
        du_out(j).start()

        @pl.when(first)
        def _():
            r.pump()

        w = load.wait(2 * j + 1)
        if j == 0:
            dn[...] = dot_nt(du[j % 2], w[...])
        else:
            dn[...] = dn[...] + dot_nt(du[j % 2], w[...])
        load.start(2 * j + 3)

        @pl.when(first)
        def _():
            r.pump()
            outer_product(block_of(r, 2 * j + 1), n, du.at[j % 2])
            r.pump()
            r.push(2 * j + 1)

        if j >= 2:
            @pl.when(end_first)
            def _():
                r.last_step(j - 2)

    for j in range(max(n_t - 2, 0), n_t):
        du_out(j).wait()

    qkv_copy(0).start()
    acts_in.wait()
    acts_out.start()

    @pl.when(second)
    def _():
        h2_copy.wait()

    def write_middle(at, value):
        h2[at, :] = value
        ga[at, :] = value.astype(BF16)

    norm_back_rows(gbuf, dn, h2, gains[1:2, :], gain1, n, write_middle)
    for c in (*o_copies, *tables):
        c.wait()

    for j in range(n_t):
        if j + 1 < n_t:
            qkv_copy(j + 1).start()
        w = load.wait(ff + j)
        load.start(ff + j + 2)
        do[...] = dot_nt(ga[...], w[3 * wide:, :]).astype(BF16)
        qkv_copy(j).wait()
        @pl.when(first)
        def _():
            r.pump()

        attend_slot_back(qkv.at[j % 2], do, proj, dcat.at[j], mask)

        def turn_back(at):
            v = proj[at, 0:2 * wide]
            dcat[j, at, 0:2 * wide] = (v * cos[at, :] - partner(v) * sin[at, :]).astype(BF16)

        row_loop(rows, 32, turn_back)
        if j == 0:
            dn[...] = dot_nn(dcat[j], w[0:3 * wide, :])
        else:
            dn[...] = dn[...] + dot_nn(dcat[j], w[0:3 * wide, :])
        @pl.when(first)
        def _():
            r.pump()

        if j in (0, 2):
            @pl.when(end_first)
            def _():
                r.last_step(2 + j // 2)

        if j < 2:
            @pl.when(inner_first)
            def _():
                rm.last_step(j)
    x_copy.wait()
    acts_out.wait()

    def write_input(at, value):
        dhb[at, :] = value.astype(BF16)

    for c in range(PARTS):
        norm_back_rows(h2, dn, x, gains[0:1, :], gain0, None, write_input, c, PARTS)

        @pl.when(second)
        def _():
            over_part(dhb, gbuf, y_send, y_recv, other, c).start()

    spread2.start()
    grads_out = local(dhb, grad_acts.at[l.z], l_sem.at[0])
    grads_out.start()

    @pl.when(second)
    def _():
        du_in(0).start()
        act_copy(0).start()
        for j in range(n_t):
            if j + 1 < n_t:
                act_copy(j + 1).start()
                du_in(j + 1).start()
            act_copy(j).wait()
            outer_product(block_of(r2, 2 * j), gbuf, act.at[j % 2])
            r2.pump()
            r2.push(2 * j)
            du_in(j).wait()
            outer_product(block_of(r2, 2 * j + 1), n, du.at[j % 2])
            r2.pump()
            r2.push(2 * j + 1)
        spread1b.step(1)
        r2.flush()

    total = Total(l, gain0, gain_buf, t_send, t_recv)
    gain0[0:1, :] = jnp.sum(gain0[...], axis=0, keepdims=True)
    gain0[1:2, :] = jnp.sum(gain1[...], axis=0, keepdims=True)
    norm_rows(x, gains[0:1, :], n)
    for j in range(n_t):
        b = block_of(r, ff + j)
        step = d // 2

        def turn(c, _):
            at = pl.ds(pl.multiple_of(c * step, 128), step)
            b[at, 0:3 * wide] = dot_tn(n[:, at], dcat[j]).astype(BF16)
            b[at, 3 * wide:] = dot_tn(ga[:, at], o[j]).astype(BF16)
            return 0

        lax.fori_loop(0, 2, turn, 0)
        r.pump()
        r.push(ff + j)
    r.flush()

    @pl.when(inner_first)
    def _():
        for i in range(2, 4):
            rm.last_step(i)

    @pl.when(second)
    def _():
        for i in range(4):
            r2.last_step(i)
        for k in range(2, n_t - 1):
            spread1b.step(k)

    for i in range(4, len(order)):
        r.last_step(i)
        if i == 4 or i == 5:
            @pl.when(inner)
            def _():
                spread2.step(i - 3)
        if i >= 6 and i - 6 < total.count:
            total.step(i - 6)
    for t in range(len(order) - 6, total.count):
        total.step(t)
    l2.recording = False

    @pl.when(~inner)
    def _():
        for k in range(1, n_t - 1):
            spread2b.step(k)

    spread1.step(n_t - 1)
    spread2.step(n_t - 1)
    out_gains[...] = total.result()
    r.close()
    grads_out.wait()

    @pl.when(second)
    def _():
        for c in range(PARTS):
            over_part(dhb, gbuf, y_send, y_recv, other, c).wait_send()

    l.drain()


def run_backward(a_own, i_own, d_own, kept, cot, gains, seg, obs, tables):
    n_dp, n_t = lax.axis_size("dp"), lax.axis_size("tensor")
    rows, d = cot.shape
    wide = a_own.shape[0] // 4
    piece = d // n_dp
    count = 3 * n_t
    steps = len(ring_bits(n_dp)) + n_t
    dma = pltpu.SemaphoreType.DMA
    hbm, vmem = pl.BlockSpec(memory_space=pl.ANY), pl.BlockSpec(memory_space=pltpu.VMEM)

    def shape(*s, t=BF16):
        return jax.ShapeDtypeStruct(s, t)

    def buf(*s, t=BF16):
        return pltpu.VMEM(s, t)

    return pl.pallas_call(
        functools.partial(backward_kernel, n_dp, n_t),
        out_shape=[
            shape(n_t, rows, d), shape(n_t, rows, d), shape(3, piece, d, t=F32), shape(8, d, t=F32),
            *reduce_hbm(n_dp, n_t, count, piece, d), shape(n_t, rows, d),
        ],
        in_specs=[hbm] * 12 + [vmem] * 4 + [hbm] * 2,
        out_specs=[hbm] * 3 + [vmem] + [hbm] * 4,
        scratch_shapes=[
            buf(rows, d), buf(2, rows, d), buf(2, rows, d), buf(rows, d), buf(rows, d, t=F32), buf(rows, d),
            buf(rows, d, t=F32), buf(rows, d), buf(rows, d, t=F32), buf(2, rows, 3 * wide), buf(n_t, rows, wide),
            buf(rows, wide), buf(n_t, rows, 3 * wide), buf(rows, d), buf(2 * QB, ROW, t=F32), buf(3, *a_own.shape),
            buf(*tables[0].shape, t=F32), buf(*tables[1].shape, t=F32),
            buf(8, d, t=F32), buf(8, d, t=F32), buf(2 * steps, 8, d, t=F32),
            dma((2,)), dma((3,)), dma((5,)), dma((n_t,)), dma((2,)), dma((2,)), dma((2,)), dma((2,)), dma((PARTS,)), dma((PARTS,)),
            dma((2, n_t)), dma((2, n_t)), dma((2, n_t)), dma((2, n_t)), dma((steps,)), dma((steps,)),
            *reduce_scratch(n_dp, n_t, count, piece, d),
        ],
        compiler_params=pltpu.CompilerParams(collective_id=1, has_side_effects=True, vmem_limit_bytes=62 * 2**20),
    )(a_own, i_own, d_own, kept[0], cot, *kept[1:], gains, seg[:, None], seg[None, :], obs[:, None], *tables)


def own_rows(x, count):
    flat = x.reshape((-1,) + x.shape[2:])
    return lax.dynamic_slice_in_dim(flat, lax.axis_index("tensor") * count, count, 0)


def on_device(tokens, cotangent, seg_ids, observed, w_qkv, w_out, w_in, w_down, norm_gains):
    n_dp, n_t = lax.axis_size("dp"), lax.axis_size("tensor")
    w_qkv, w_out, w_in, w_down, gains = w_qkv[0], w_out[0], w_in[0], w_down[0], norm_gains[0]
    micro, rows, d = tokens.shape
    hd = w_out.shape[0]
    count = micro * rows // n_t
    tables = rope_tables()
    stack = jnp.concatenate([jnp.swapaxes(w_qkv, 1, 2), w_out[None]], axis=0).reshape(4 * hd, d)
    seg, obs = own_rows(seg_ids, count), own_rows(observed, count)
    kept = run_forward(stack, w_in, w_down, own_rows(tokens, count), gains, seg, obs, tables)[:8]
    layer_acts, grad_acts, sums, gain = run_backward(stack, w_in, w_down, kept, own_rows(cotangent, count), gains, seg, obs, tables)[:4]
    piece = d // n_dp
    gain = lax.dynamic_slice_in_dim(gain[:2], lax.axis_index("dp") * piece, piece, 1)
    r_attn, r_in, r_down = sums[0], sums[1], sums[2]
    r_qkv = jnp.stack([r_attn[:, i * hd:(i + 1) * hd] for i in range(3)])
    return (
        layer_acts.reshape(1, micro, rows, d),
        grad_acts.reshape(1, micro, rows, d),
        r_qkv[None],
        r_attn[:, 3 * hd:].T[None],
        r_in[None],
        r_down.T[None],
        gain[None],
    )


def solution(mesh):
    return jax.shard_map(
        on_device,
        mesh=mesh,
        in_specs=(
            P(None, "dp", None),
            P(None, "dp", None),
            P(None, "dp"),
            P(None, "dp"),
            P("section", None, None, "tensor"),
            P("section", "tensor", None),
            P("section", None, "tensor"),
            P("section", "tensor", None),
            P("section", None, None),
        ),
        out_specs=(
            P("section", None, "dp", None),
            P("section", None, "dp", None),
            P("section", None, "dp", "tensor"),
            P("section", "tensor", "dp"),
            P("section", "dp", "tensor"),
            P("section", "tensor", "dp"),
            P("section", None, "dp"),
        ),
        check_vma=False,
    )
```

```python
import functools
import math

import jax
import jax.numpy as jnp
import numpy as np
from jax import lax
from jax.experimental import pallas as pl
from jax.experimental.pallas import tpu as pltpu
from jax.sharding import PartitionSpec as P

HEAD_SIZE = 80
HALF = HEAD_SIZE // 2
ROW = 512
QB = 128
GROUP = 8
EPS = 1e-06
BIG = 1000000000.0
SCALE = 1.0 / math.sqrt(HEAD_SIZE)
BF16 = jnp.bfloat16
F32 = jnp.float32
MESH = pl.DeviceIdType.MESH


def dot_nn(a, b):
    return lax.dot_general(a, b, (((1,), (0,)), ((), ())), preferred_element_type=F32)


def dot_nt(a, b):
    return lax.dot_general(a, b, (((1,), (1,)), ((), ())), preferred_element_type=F32)


def dot_tn(a, b):
    return lax.dot_general(a, b, (((0,), (0,)), ((), ())), preferred_element_type=F32)


def rope_tables():
    freq = 10000.0 ** (-np.arange(HALF) / HALF)
    ang = np.arange(ROW)[:, None] * freq[None, :]
    cos, sin = np.cos(ang), np.sin(ang)
    cos_full = np.tile(np.concatenate([cos, cos], axis=1), (1, GROUP))
    sin_full = np.tile(np.concatenate([-sin, sin], axis=1), (1, GROUP))
    return jnp.asarray(cos_full, F32), jnp.asarray(sin_full, F32)


def write_halves(halves):
    lane = lax.broadcasted_iota(jnp.int32, halves.shape, 1)
    halves[...] = (lax.rem(lane, HEAD_SIZE) < HALF).astype(F32)


def partner(x, halves):
    return jnp.where(halves[0:1, :] > 0, pltpu.roll(x, x.shape[1] - HALF, 1), pltpu.roll(x, HALF, 1))


def windows():
    return [max(i - 1, 0) * QB for i in range(ROW // QB)]


def own_row(ref, z):
    per = ref.shape[1] // ROW
    at = pl.multiple_of(lax.rem(z, per) * ROW, ROW)
    return ref[pl.ds(z // per, 1), pl.ds(at, ROW)].astype(F32)


def column(row):
    return jnp.transpose(jnp.broadcast_to(row, (128, ROW)))[:, 0:1]


def write_mask(mask, seg_ids, observed, z):
    seg_row = own_row(seg_ids, z)
    seg_col, obs_col = column(seg_row), column(own_row(observed, z))
    for i, k0 in enumerate(windows()):
        keys, queries = slice(k0, k0 + 2 * QB), slice(i * QB, (i + 1) * QB)
        shape = (2 * QB, QB)
        kj = lax.broadcasted_iota(jnp.int32, shape, 0) + k0
        qi = lax.broadcasted_iota(jnp.int32, shape, 1) + i * QB
        same = seg_col[keys, :] == seg_row[:, queries]
        seen = (obs_col[keys, :] == 1.0) | (kj == qi)
        mask[:, queries] = (same & (kj <= qi) & seen).astype(F32)


def query_block(x, i):
    return x[:, i * QB:(i + 1) * QB]


def by_window(keys, queries):
    return jnp.concatenate(
        [dot_nt(keys[k0:k0 + 2 * QB], queries[i * QB:(i + 1) * QB]) for i, k0 in enumerate(windows())], axis=1
    )


def to_queries(weights, keys):
    return jnp.concatenate(
        [dot_tn(query_block(weights, i), keys[k0:k0 + 2 * QB]) for i, k0 in enumerate(windows())], axis=0
    )


def to_keys(weights, queries):
    blocks = [None] * (ROW // QB)
    for i, k0 in enumerate(windows()):
        term = dot_nn(query_block(weights, i), queries[i * QB:(i + 1) * QB])
        for j in range(2):
            at, part = k0 // QB + j, term[j * QB:(j + 1) * QB]
            blocks[at] = part if blocks[at] is None else blocks[at] + part
    return jnp.concatenate(blocks, axis=0)


def probabilities(q, k, mask):
    s = jnp.where(mask[...] > 0, by_window(k, q) * SCALE, -BIG)
    e = jnp.exp(s - jnp.max(s, axis=0, keepdims=True))
    return e * (1.0 / jnp.sum(e, axis=0, keepdims=True))


def ring_bits(n):
    return [1 << i for i in range(n.bit_length() - 1)]


def low_bit(j):
    return j & -j


class Links:
    def __init__(self, n_dp, n_t):
        self.n_dp, self.n_t = n_dp, n_t
        self.me, self.z = lax.axis_index("dp"), lax.axis_index("tensor")
        self.down = lax.rem(self.z + n_t - 1, n_t)
        self.up = lax.rem(self.z + 1, n_t)
        self.bits = ring_bits(n_dp)
        self.sent, self.recording = {}, True

    def flip(self, bit):
        return self.me + bit - 2 * bit * lax.rem(self.me // bit, 2)

    def mix(self, j):
        at = self.me
        for bit in self.bits:
            if j & bit:
                at = at + bit - 2 * bit * lax.rem(self.me // bit, 2)
        return at

    def place(self, table):
        n = self.n_t
        return sum(v * (1 - ((self.z - k) * (self.z - k) + n * n - 1) // (n * n)) for k, v in enumerate(table))

    def own_bit(self, bit):
        return lax.rem(self.me // bit, 2)

    def greet(self, axes):
        barrier = pltpu.get_barrier_semaphore()
        for where in axes:
            pl.semaphore_signal(barrier, inc=1, device_id=where, device_id_type=MESH)
        pl.semaphore_wait(barrier, len(axes))

    def send(self, src, dst, send_sem, recv_sem, where, tag=None, again=None, when=None):
        pltpu.make_async_remote_copy(
            src_ref=src, dst_ref=dst, send_sem=send_sem, recv_sem=recv_sem, device_id=where, device_id_type=MESH
        ).start()
        if self.recording:
            self.sent.setdefault(tag, []).append((again or (lambda: (src, send_sem)), when))

    def finish(self, tag):
        def left(again):
            ref, sem = again()
            pltpu.make_async_remote_copy(
                src_ref=ref, dst_ref=ref, send_sem=sem, recv_sem=sem, device_id={"tensor": self.down}, device_id_type=MESH
            ).wait_send()

        for again, when in self.sent.pop(tag, ()):
            if when is None:
                left(again)
            else:
                pl.when(when())(functools.partial(left, again))

    def arrived(self, ref, sem, send_sem, where):
        pltpu.make_async_remote_copy(
            src_ref=ref, dst_ref=ref, send_sem=send_sem, recv_sem=sem, device_id=where, device_id_type=MESH
        ).wait_recv()

    def drain(self):
        for tag in list(self.sent):
            self.finish(tag)


class Gather:
    def __init__(self, links, own, full, parts, z_send, z_recv, p_send, p_recv):
        self.l, self.own, self.full, self.parts = links, own, full, parts
        self.z_send, self.z_recv, self.p_send, self.p_recv = z_send, z_recv, p_send, p_recv
        self.rows = own[0].shape[0] // links.n_dp
        self.units = [(m, k, h) for m, k in gather_order(links.n_t) for h in range(len(parts))]
        self.at = {u: i for i, u in enumerate(self.units)}

    def piece(self, m, slot, index, h):
        off, size = self.parts[h]
        first = pl.multiple_of(index * self.rows + off, 16)
        if slot == 0:
            return self.own[m].at[pl.ds(first, size), :]
        return self.full.at[m, slot, pl.ds(first, size), :]

    def like(self, h):
        return self.full.at[0, 1, pl.ds(0, self.parts[h][1]), :]

    def send_z(self, m, k, h):
        l = self.l
        i = self.at[(m, k, h)]
        l.send(self.piece(m, k - 1, l.me, h), self.piece(m, k, l.me, h), self.z_send.at[i], self.z_recv.at[i], {"tensor": l.down},
               again=lambda: (self.like(h), self.z_send.at[i]))

    def advance(self, taken):
        for unit in due(self.units, self.issued, taken, 2 * len(self.parts)):
            self.send_z(*unit)
            self.issued += 1

    def start(self):
        self.issued = 0
        self.advance(0)

    def share(self, i, j):
        m, k, h = self.units[i]
        l = self.l
        for bit in reversed(l.bits):
            if j == 0 or bit < low_bit(j):
                ref = self.piece(m, k, l.mix(j), h)
                l.send(ref, ref, self.p_send.at[i, j ^ bit], self.p_recv.at[i, j ^ bit], {"dp": l.flip(bit)},
                       again=lambda at=j ^ bit: (self.like(h), self.p_send.at[i, at]))

    def take(self, i):
        m, k, h = self.units[i]
        l = self.l
        l.arrived(self.piece(m, k, l.me, h), self.z_recv.at[i], self.z_send.at[i], {"tensor": l.up})
        self.advance(i + 1)
        self.share(i, 0)

    def relay(self, i, bit):
        m, k, h = self.units[i]
        l = self.l
        for j in range(bit, l.n_dp, 2 * bit):
            l.arrived(self.piece(m, k, l.mix(j), h), self.p_recv.at[i, j], self.p_send.at[i, j], {"dp": l.flip(low_bit(j))})
            self.share(i, j)

    def walk(self, lent=None, lag=2):
        hops = self.l.bits[::-1]
        for i in range(len(self.units) + lag + len(hops) - 1):
            if i < len(self.units):
                m, k, h = self.units[i]
                self.take(i)
                if lent is not None and h == 0:
                    lent.take_back(m, k)
            done = None
            for hop, bit in enumerate(hops):
                at = i - lag - hop
                if 0 <= at < len(self.units):
                    self.relay(at, bit)
                    m, k, h = self.units[at]
                    if hop == len(hops) - 1 and h == len(self.parts) - 1:
                        if lent is not None:
                            lent.finish_back(m, k)
                        done = (m, k)
            yield done


class Lend:
    def __init__(self, links, own, full, held, y_send, y_recv, z_send, z_recv, p_send, p_recv, b_send, b_recv):
        self.l, self.own, self.full, self.held = links, own, full, held
        self.y_send, self.y_recv, self.z_send, self.z_recv = y_send, y_recv, z_send, z_recv
        self.p_send, self.p_recv, self.b_send, self.b_recv = p_send, p_recv, b_send, b_recv
        self.rows = own[0].shape[0] // links.n_dp
        self.size = held.shape[3]
        self.even = [j for j in range(0, links.n_dp, 2)]
        self.where = {"section": 1 - lax.axis_index("section")}

    def rows_of(self, j):
        return pl.ds(pl.multiple_of(self.l.mix(j) * self.rows, 16), self.size)

    def like(self):
        return self.held.at[0, 0, 0]

    def send(self, src, dst, sems, at, where):
        self.l.send(src, dst, sems[0].at[at], sems[1].at[at], where, again=lambda: (self.like(), sems[0].at[at]))

    def arrived(self, ref, sems, at):
        self.l.arrived(ref, sems[1].at[at], sems[0].at[at], self.where)

    def give(self):
        for m in range(3):
            self.send(self.own[m].at[self.rows_of(0), :], self.held.at[m, 0, self.l.me], (self.y_send, self.y_recv), (m,), self.where)

    def take_back(self, m, k):
        for j in self.even:
            ref = self.full.at[m, k, self.rows_of(j), :]
            self.arrived(ref, (self.b_send, self.b_recv), (m, k, j))
            self.send(ref, ref, (self.p_send, self.p_recv), (m, k, j + 1), {"dp": self.l.flip(1)})

    def finish_back(self, m, k):
        for j in self.even:
            self.arrived(self.full.at[m, k, self.rows_of(j + 1), :], (self.p_send, self.p_recv), (m, k, j + 1))

    def ring(self, m, k):
        l = self.l
        self.send(self.held.at[m, k - 1, l.me], self.held.at[m, k, l.me], (self.z_send, self.z_recv), (m, k), {"tensor": l.down})

    def back(self, m, k, j):
        l = self.l
        self.send(self.held.at[m, k, l.mix(j)], self.full.at[m, k, self.rows_of(j), :], (self.b_send, self.b_recv), (m, k, j), self.where)

    def share(self, m, k, j):
        l = self.l
        for bit in reversed(l.bits[1:]):
            if j == 0 or bit < low_bit(j):
                ref = self.held.at[m, k, l.mix(j)]
                self.send(ref, ref, (self.p_send, self.p_recv), (m, k, j ^ bit), {"dp": l.flip(bit)})

    def serve(self, lag=1):
        l = self.l
        units = gather_order(l.n_t)
        issued = 0
        started = False
        for i in range(len(units) + lag):
            for m, k in due(units, issued, i, 3):
                if k == 1:
                    self.arrived(self.held.at[m, 0, l.me], (self.y_send, self.y_recv), (m,))
                self.ring(m, k)
                issued += 1
            if issued == len(units) and not started:
                started = True
                yield
            if i < len(units):
                m, k = units[i]
                self.arrived(self.held.at[m, k, l.me], (self.z_send, self.z_recv), (m, k))
                self.share(m, k, 0)
                self.back(m, k, 0)
            if i >= lag:
                m, k = units[i - lag]
                for j in sorted(self.even[1:], key=lambda j: (-low_bit(j), j)):
                    self.arrived(self.held.at[m, k, l.mix(j)], (self.p_send, self.p_recv), (m, k, j))
                    self.share(m, k, j)
                    self.back(m, k, j)


def gather_order(n_t):
    heads = [(0, k) for k in range(1, n_t)]
    rest = [(m, k) for k in range(1, n_t) for m in (1, 2)]
    return [u for pair in zip(heads, rest) for u in pair] + rest[len(heads):]


def due(units, issued, taken, ahead):
    found = []
    while issued < min(len(units), taken + ahead):
        m, k, *h = units[issued]
        if k > 1 and units.index((m, k - 1, *h)) >= taken:
            break
        found.append(units[issued])
        issued += 1
    return found


def gather_parts(rows):
    lent = rows // 4 // 16 * 16
    if rows % 32:
        return lent, [(lent, rows - lent)], [(0, rows)]
    cut = lent + (rows - lent + 31) // 32 * 16
    return lent, [(lent, cut - lent), (cut, rows - cut)], [(0, rows // 2), (rows // 2, rows // 2)]


def level_start(n_dp, level):
    return sum(n_dp >> (t + 1) for t in range(level))


def add_rows(out, *terms):
    rows = out.shape[0]

    def body(r, _):
        at = pl.ds(pl.multiple_of(r * 16, 16), 16)
        total = terms[0][at, :].astype(F32)
        for t in terms[1:]:
            total = total + t[at, :].astype(F32)
        out[at, :] = total.astype(out.dtype)
        return 0

    lax.fori_loop(0, rows // 16, body, 0)


def reduce_scratch(n_dp, n_t, count, rows, c):
    dma = pltpu.SemaphoreType.DMA
    half = n_dp // 2
    return [
        pltpu.VMEM((3, n_dp * rows, c), BF16),
        pltpu.VMEM((2, half, rows, c), BF16),
        pltpu.VMEM((3, rows, c), BF16),
        pltpu.VMEM((3, rows, c), BF16),
        pltpu.VMEM((rows, c), F32),
        dma((count, n_dp)),
        dma((count, n_dp)),
        dma((count,)),
        dma((count // n_t, n_t, 2)),
        dma((2,)),
        dma((2,)),
        dma((3,)),
        dma(()),
    ]


def reduce_hbm(n_dp, n_t, count, rows, c):
    return [
        jax.ShapeDtypeStruct((count, n_dp // 2, rows, c), BF16),
        jax.ShapeDtypeStruct((count, n_dp - 1, rows, c), BF16),
        jax.ShapeDtypeStruct((count // n_t, n_t, 2, rows, c), BF16),
    ]


def line_order(n_t):
    return [sorted(range(n_t), key=lambda s: (-abs(s - z), -max(s, n_t - 1 - s))) for z in range(n_t)]


class Places:
    def __init__(self, links):
        n_t = links.n_t
        orders = line_order(n_t)
        self.shard = [links.place([o[j] for o in orders]) for j in range(n_t)]
        self.slot = [links.place([(o[j] - z) % n_t for z, o in enumerate(orders)]) for j in range(n_t - 1)] + [0]
        self.up = [links.place([int(o[j] > z) for z, o in enumerate(orders)]) for j in range(n_t)]
        self.below = (links.z + n_t - 1) // n_t
        self.above = (2 * n_t - 2 - links.z) // n_t


def travel_order(order):
    if len(order) != 12:
        return list(range(len(order)))
    return [0, 1, 2, 3, 4, 8, 5, 9, 6, 10, 7, 11]


class Reduce:
    def __init__(self, links, places, order, out, hbm, scratch):
        self.l, self.places, self.order, self.out = links, places, order, out
        self.sums, self.got, self.ring = hbm
        (self.block, self.fetched, self.terms, self.moving, self.final,
         self.c_send, self.c_recv, self.z_send, self.z_recv,
         self.f_sem, self.s_sem, self.t_sem, self.o_sem) = scratch
        self.moves = []
        self.queue = travel_order(order)
        self.stored, self.gone = set(), 0
        self.levels = len(links.bits)
        self.rows = self.fetched.shape[2]
        self.storing = None

    def offsets(self, level):
        bits = self.l.bits[level + 1:]
        return [sum(b for n, b in enumerate(bits) if k >> n & 1) for k in range(1 << len(bits))]

    def mine(self, level):
        return lax.rem(self.l.me, 1 << (level + 1))

    def give(self, i, level, source):
        l, bit = self.l, self.l.bits[level]
        there = self.mine(level) + bit - 2 * bit * l.own_bit(bit)
        for n, off in enumerate(self.offsets(level)):
            at = (i, level_start(l.n_dp, level) + n)
            l.send(source(there + off), self.got.at[at], self.c_send.at[at], self.c_recv.at[at], {"dp": l.flip(bit)}, (i, level),
                   again=lambda at=at: (self.got.at[at], self.c_send.at[at]))

    def receive(self, i, level):
        l = self.l
        for n, _ in enumerate(self.offsets(level)):
            at = (i, level_start(l.n_dp, level) + n)
            l.arrived(self.got.at[at], self.c_recv.at[at], self.c_send.at[at], {"dp": l.flip(l.bits[level])})

    def piece(self, i, p):
        return self.block.at[i % 3, pl.ds(pl.multiple_of(p * self.rows, 16), self.rows), :]

    def give_block(self, i):
        self.give(i, 0, lambda p: self.piece(i, p))

    def fetch_copy(self, i):
        return pltpu.make_async_copy(self.got.at[i, pl.ds(0, self.l.n_dp // 2)], self.fetched.at[i % 2], self.f_sem.at[i % 2])

    def fetch(self, i):
        self.receive(i, 0)
        self.fetch_copy(i).start()

    def store_copy(self, i):
        return pltpu.make_async_copy(self.fetched.at[i % 2], self.sums.at[i], self.s_sem.at[i % 2])

    def add_first(self, i):
        self.fetch_copy(i).wait()
        for n in range(self.l.n_dp // 2):
            here = self.fetched.at[i % 2, n]
            add_rows(here, self.piece(i, 2 * n + self.l.own_bit(1)), here)
        self.store_copy(i).start()

    def give_next(self, i):
        self.store_copy(i).wait()
        self.stored.add(i)
        while self.gone < len(self.queue) and self.queue[self.gone] in self.stored:
            at = self.queue[self.gone]
            self.give(at, 1, lambda piece: self.sums.at[at, piece // 2])
            self.gone += 1

    def push(self, i):
        self.give_block(i)
        self.moves.append([i, 0])

    def pump(self):
        for move in list(self.moves):
            i, stage = move
            if stage == 0 and any(o[0] == i - 2 for o in self.moves):
                break
            (self.fetch, self.add_first, self.give_next)[stage](i)
            move[1] += 1
            if move[1] == 3:
                self.moves.remove(move)

    def flush(self, i=None):
        while any(i is None or o[0] == i for o in self.moves):
            self.pump()

    def clear(self, i):
        while any(o[0] == i - 3 and o[1] < 2 for o in self.moves):
            self.pump()
        self.l.finish((i - 3, 0))

    def middle(self, i, level):
        l = self.l
        self.receive(i, level)
        for n, off in enumerate(self.offsets(level)):
            piece = (self.mine(level) + off) // 2
            loads = [
                pltpu.make_async_copy(self.sums.at[i, piece], self.terms.at[0], self.t_sem.at[0]),
                pltpu.make_async_copy(self.got.at[i, level_start(l.n_dp, level) + n], self.terms.at[1], self.t_sem.at[1]),
            ]
            for c in loads:
                c.start()
            for c in loads:
                c.wait()
            add_rows(self.terms.at[2], self.terms.at[0], self.terms.at[1])
            back = pltpu.make_async_copy(self.terms.at[2], self.sums.at[i, piece], self.t_sem.at[2])
            back.start()
            back.wait()
        self.give(i, level + 1, lambda piece: self.sums.at[i, piece // 2])

    def term_copies(self, i):
        l = self.l
        return [
            pltpu.make_async_copy(self.sums.at[i, l.me // 2], self.terms.at[0], self.t_sem.at[0]),
            pltpu.make_async_copy(self.got.at[i, l.n_dp - 2], self.terms.at[1], self.t_sem.at[1]),
        ]

    def collect(self, i):
        self.receive(i, self.levels - 1)
        for c in self.term_copies(i):
            c.start()

    def out_copy(self, m):
        return pltpu.make_async_copy(self.final, self.out.at[m], self.o_sem)

    def come(self, m, s, way):
        l = self.l
        ref = self.ring.at[m, s, way]
        l.arrived(ref, self.z_recv.at[m, s, way], self.z_send.at[0], {"tensor": l.down})
        copy = pltpu.make_async_copy(ref, self.terms.at[2], self.t_sem.at[2])
        copy.start()
        copy.wait()

    def pass_on(self, i, turn):
        l, p = self.l, self.places
        m, j = self.order[i]
        l.finish(("z", turn - 3))
        terms = [self.terms.at[t] for t in range(3)]
        if j < l.n_t - 1:
            s, up, out = p.shard[j], p.up[j], self.moving.at[turn % 3]
            behind = up * p.below + (1 - up) * p.above
            for c in self.term_copies(i):
                c.wait()

            @pl.when(behind == 1)
            def _():
                self.come(m, s, 1 - up)
                add_rows(out, *terms)

            @pl.when(behind == 0)
            def _():
                add_rows(out, *terms[:2])

            l.send(out, self.ring.at[m, s, 1 - up], self.z_send.at[i], self.z_recv.at[m, s, 1 - up], {"tensor": l.z + 2 * up - 1},
                   ("z", turn), again=lambda: (self.moving.at[turn % 3], self.z_send.at[i]))
        else:
            if self.storing is not None:
                self.out_copy(self.storing).wait()
            for c in self.term_copies(i):
                c.wait()
            add_rows(self.final, *terms[:2])
            for way, there in ((0, p.below), (1, p.above)):
                @pl.when(there == 1)
                def _():
                    self.come(m, l.z, way)
                    add_rows(self.final, self.final, terms[2])
            self.out_copy(m).start()
            self.storing = m

    def last_step(self, turn):
        i = self.queue[turn]
        for before in self.queue[:turn + 1]:
            self.flush(before)
        for level in range(1, self.levels - 1):
            self.middle(i, level)
        self.collect(i)
        self.pass_on(i, turn)

    def close(self):
        self.out_copy(self.storing).wait()


class Spread:
    def __init__(self, links, places, block, out, send, recv):
        self.l, self.places, self.block, self.out, self.send, self.recv = links, places, block, out, send, recv

    def pass_on(self, source, at, way, k):
        l, p = self.l, self.places
        l.send(source, self.out.at[at], self.send.at[way, k], self.recv.at[way, k], {"tensor": l.z + 1 - 2 * way},
               again=lambda: (self.out.at[0], self.send.at[way, k]),
               when=lambda: ((p.above, p.below)[way] == 1) if k == 0 else self.passes(way, k))

    def passes(self, way, k):
        z, n = self.l.z, self.l.n_t
        return (z >= k) & (z < n - 1) if way == 0 else (z < n - k) & (z > 0)

    def start(self):
        p = self.places
        for way, there in ((0, p.above), (1, p.below)):
            @pl.when(there == 1)
            def _():
                self.pass_on(self.block, self.l.z, way, 0)

    def step(self, k):
        l = self.l
        for way in range(2):
            at = l.z + k * (2 * way - 1)

            @pl.when(l.z >= k if way == 0 else l.z < l.n_t - k)
            def _():
                l.arrived(self.out.at[at], self.recv.at[way, k - 1], self.send.at[way, k - 1], {"tensor": l.down})

            if k < l.n_t - 1:
                @pl.when(self.passes(way, k))
                def _():
                    self.pass_on(self.out.at[at], at, way, k)


class Total:
    def __init__(self, links, block, buf, send, recv):
        self.l, self.block, self.buf, self.s, self.r = links, block, buf, send, recv
        self.levels = len(links.bits)
        self.count = self.levels + links.n_t

    def step(self, s):
        l, buf = self.l, self.buf
        if s == 0:
            buf[1] = self.block[...]
        else:
            l.arrived(buf.at[2 * s], self.r.at[s - 1], self.s.at[s - 1], {"tensor": l.up})
            if s <= self.levels:
                buf[2 * s + 1] = buf[2 * s - 1] + buf[2 * s]
        if s < self.levels:
            l.send(buf.at[2 * s + 1], buf.at[2 * s + 2], self.s.at[s], self.r.at[s], {"dp": l.flip(l.bits[s])})
        elif s < self.count - 1:
            src = 2 * s + 1 if s == self.levels else 2 * s
            l.send(buf.at[src], buf.at[2 * s + 2], self.s.at[s], self.r.at[s], {"tensor": l.down})

    def result(self):
        total = self.buf[2 * self.levels + 1]
        for k in range(1, self.l.n_t):
            total = total + self.buf[2 * (self.levels + k)]
        return total


def row_loop(rows, step, body):
    def turn(r, _):
        body(pl.ds(pl.multiple_of(r * step, step), step))
        return 0

    lax.fori_loop(0, rows // step, turn, 0)


def column_steps(width):
    return [slice(c, c + 256) for c in range(0, width, 256)]


def norm_rows(source, gain, out):
    def body(at):
        h = source[at, :].astype(F32)
        r = lax.rsqrt(jnp.mean(h * h, axis=1, keepdims=True) + EPS)
        out[at, :] = (h * r * gain).astype(BF16)

    row_loop(source.shape[0], 32, body)


def own_block(ref, z, rows):
    per = ref.shape[1] // rows
    return ref.at[z // per, pl.ds(pl.multiple_of(lax.rem(z, per) * rows, rows), rows), :]


def attend_slot(qkv, o, mask):
    heads = o.shape[1] // HEAD_SIZE
    for h in range(heads):
        q, k, v = (slice((t * heads + h) * HEAD_SIZE, (t * heads + h + 1) * HEAD_SIZE) for t in range(3))
        p = probabilities(qkv[:, q], qkv[:, k], mask).astype(BF16)
        o[:, q] = to_queries(p, qkv[:, v]).astype(BF16)


class Loader:
    def __init__(self, buf, sem, blocks):
        self.buf, self.sem, self.blocks = buf, sem, blocks

    def copies(self, j):
        slot, first, found = j % self.buf.shape[0], 0, []
        block = self.blocks[j]
        for n, ref in enumerate(block if isinstance(block, tuple) else (block,)):
            to = self.buf.at[slot, pl.ds(first, ref.shape[0]), :]
            found.append(pltpu.make_async_copy(ref, to, self.sem.at[n, slot]))
            first += ref.shape[0]
        return found

    def start(self, j):
        if j < len(self.blocks):
            for c in self.copies(j):
                c.start()

    def wait(self, j):
        for c in self.copies(j):
            c.wait()
        return self.buf.at[j % self.buf.shape[0]]


PARTS = 2


def over_part(src, dst, send, recv, where, c):
    size = src.shape[0] // PARTS
    at = pl.ds(c * size, size)
    return pltpu.make_async_remote_copy(
        src_ref=src.at[at, :], dst_ref=dst.at[at, :], send_sem=send.at[c], recv_sem=recv.at[c],
        device_id=where, device_id_type=MESH,
    )


def forward_kernel(
    n_dp, n_t, q_own, o_own, i_own, d_own, x0, gains, seg_ids, observed, cos_in, sin_in,
    full, xs, qkv_out, o_out, h2_out, act_out, slope_out, out, mask_out, held,
    stack, x, n, proj, qkv, o, h2, acc, act, slope, outb, mask, wbuf, cos, sin, halves,
    a_sem, c_sem, w_sem, s_sem, y_send, y_recv, x_sem, z_send, z_recv, p_send, p_recv,
    *lend_sems,
):
    l, l1 = Links(n_dp, n_t), Links(n_dp, n_t)
    section = lax.axis_index("section")
    first, second = section == 0, section != 0
    own = (stack, i_own, d_own)
    _, parts0, parts1 = gather_parts(stack.shape[0] // n_dp)
    stacked = [
        pltpu.make_async_copy(ref, stack.at[pl.ds(at, ref.shape[0]), :], a_sem.at[n])
        for n, (ref, at) in enumerate(((q_own, 0), (o_own, q_own.shape[0])))
    ]
    for c in stacked:
        c.start()
    g0 = Gather(l, own, full, parts0, z_send, z_recv, p_send, p_recv)
    g1 = Gather(l1, own, full, parts1, z_send, z_recv, p_send, p_recv)
    lend0, lend1 = Lend(l, own, full, held, *lend_sems), Lend(l1, own, full, held, *lend_sems)
    other = {"section": 1 - section}
    l.greet([{"tensor": l.up}, other] + [{"dp": l.flip(b)} for b in l.bits])
    rows, d = x.shape
    wide = o.shape[2]

    def block(m, slot):
        return own[m] if slot == 0 else full.at[m, slot]

    order = [(0, s) for s in range(n_t)] + [(m, s) for s in range(n_t) for m in (1, 2)]
    load = Loader(wbuf, w_sem, [block(m, s) for m, s in order])
    stores = []

    def store(src, dst, sem):
        copy = pltpu.make_async_copy(src, dst, sem)
        copy.start()
        stores.append(copy)

    walks, here = (g0.walk(lend0), g1.walk()), (set(), set())

    def until(section, m, slot):
        while slot > 0 and (m, slot) not in here[section]:
            here[section].add(next(walks[section]))

    def tick(*sections):
        for at in sections:
            @pl.when((first, second)[at])
            def _():
                here[at].add(next(walks[at], None))

    tables = [pltpu.make_async_copy(t, to, c_sem.at[i]) for i, (t, to) in enumerate(((cos_in, cos), (sin_in, sin)))]
    for c in tables:
        c.start()
    for c in stacked:
        c.wait()

    @pl.when(first)
    def _():
        lend0.give()
        g0.start()
        copy = pltpu.make_async_copy(own_block(x0, l.z, rows), x, x_sem)
        copy.start()
        copy.wait()

    write_mask(mask, seg_ids, observed, l.z)
    write_halves(halves)
    store(mask, mask_out, c_sem.at[2])
    for c in tables:
        c.wait()

    @pl.when(second)
    def _():
        lending = lend1.serve()
        next(lending)
        g1.start()
        for _ in lending:
            pass
        until(1, 0, n_t - 1)
        load.start(0)
        load.start(1)
        until(1, 1, n_t - 2)
        for c in range(PARTS):
            over_part(outb, x, y_send, y_recv, other, c).wait_recv()

    store(x, xs, s_sem.at[0])
    norm_rows(x, gains[0:1, :], n)
    for s in range(n_t):
        @pl.when(first)
        def _():
            until(0, 0, s)
            load.start(s)

        @pl.when(second)
        def _():
            load.start(s + 2)

        w = load.wait(s)
        proj[:, 0:3 * wide] = dot_nt(n[...], w[0:3 * wide, :])

        def turn_rows(at):
            v = proj[at, 0:2 * wide]
            qkv[s, at, 0:2 * wide] = (v * cos[at, :] + partner(v, halves) * sin[at, :]).astype(BF16)
            qkv[s, at, 2 * wide:3 * wide] = proj[at, 2 * wide:3 * wide].astype(BF16)

        row_loop(rows, 32, turn_rows)
        tick(0)
        attend_slot(qkv.at[s], o.at[s], mask)
        tick(0, 1)
        term = dot_nn(o[s], w[3 * wide:, :])
        if s == 0:
            acc[...] = term
        else:
            acc[...] = acc[...] + term
        store(qkv.at[s], qkv_out.at[s], s_sem.at[1 + s])
        store(o.at[s], o_out.at[s], s_sem.at[1 + n_t + s])

    def middle(at):
        h = x[at, :].astype(F32) + acc[at, :]
        h2[at, :] = h
        acc[at, :] = h
        r = lax.rsqrt(jnp.mean(h * h, axis=1, keepdims=True) + EPS)
        n[at, :] = (h * r * gains[1:2, :]).astype(BF16)

    row_loop(rows, 32, middle)
    store(h2, h2_out, s_sem.at[1 + 2 * n_t])
    spare = 2 + 2 * n_t
    for s in range(n_t):
        j = n_t + 2 * s

        @pl.when(first)
        def _():
            until(0, 1 if s == n_t - 1 else 2, s)
            load.start(j)
            if s < n_t - 1:
                load.start(j + 1)

        @pl.when(second)
        def _():
            if s == n_t - 1:
                until(1, 2, s)
                load.start(j)
                load.start(j + 1)
            elif s < n_t - 2:
                until(1, 1, s + 1)
                load.start(j + 2)

        w = load.wait(j)
        if s >= 2:
            for copy in stores[-4:-2]:
                copy.wait()
            del stores[-4:-2]
        for c in column_steps(act.shape[2]):
            u = dot_nn(n[...], w[:, c])
            sig = lax.logistic(u)
            act[s % 2, :, c] = (u * sig).astype(BF16)
            slope[s % 2, :, c] = (sig * (1.0 + u * (1.0 - sig))).astype(BF16)
        tick(*((1,) if s == 0 else (0, 1)))

        @pl.when(first)
        def _():
            if s == n_t - 1:
                until(0, 2, s)
                load.start(j + 1)

        @pl.when(second)
        def _():
            if s < n_t - 2:
                until(1, 2, s + 1)
                load.start(j + 3)

        w = load.wait(j + 1)
        if s < n_t - 1:
            acc[...] = acc[...] + dot_nn(act[s % 2], w[...])
        else:
            for c in range(PARTS):
                at = slice(c * rows // PARTS, (c + 1) * rows // PARTS)
                outb[at, :] = (acc[at, :] + dot_nn(act[s % 2, at, :], w[...])).astype(BF16)

                @pl.when(first)
                def _():
                    over_part(outb, x, y_send, y_recv, other, c).start()

        store(act.at[s % 2], act_out.at[s], s_sem.at[spare + 2 * (s % 2)])
        store(slope.at[s % 2], slope_out.at[s], s_sem.at[spare + 2 * (s % 2) + 1])

    assert all(len(h - {None}) == 3 * (n_t - 1) for h in here)
    store(outb, out, x_sem)
    for copy in stores:
        copy.wait()

    @pl.when(first)
    def _():
        for c in range(PARTS):
            over_part(outb, x, y_send, y_recv, other, c).wait_send()
        l.drain()

    @pl.when(second)
    def _():
        l1.drain()


def run_forward(q_own, o_own, i_own, d_own, x0, gains, seg, obs, tables):
    n_dp, n_t = lax.axis_size("dp"), lax.axis_size("tensor")
    wide, d = o_own.shape
    rows = x0.shape[0] * x0.shape[1] // n_t
    whole = (4 * wide, d)
    lent, parts, _ = gather_parts(whole[0] // n_dp)
    count = 3 * (n_t - 1) * len(parts)
    dma = pltpu.SemaphoreType.DMA
    hbm, vmem = pl.BlockSpec(memory_space=pl.ANY), pl.BlockSpec(memory_space=pltpu.VMEM)

    def shape(*s, t=BF16):
        return jax.ShapeDtypeStruct(s, t)

    return pl.pallas_call(
        functools.partial(forward_kernel, n_dp, n_t),
        out_shape=[
            shape(3, n_t, *whole), shape(rows, d), shape(n_t, rows, 3 * wide), shape(n_t, rows, wide),
            shape(rows, d, t=F32), shape(n_t, rows, i_own.shape[1]), shape(n_t, rows, i_own.shape[1]), shape(rows, d),
            shape(2 * QB, ROW, t=F32), shape(3, n_t, n_dp, lent, d),
        ],
        in_specs=[hbm] * 5 + [vmem] * 3 + [hbm] * 2,
        out_specs=[hbm] * 10,
        scratch_shapes=[
            pltpu.VMEM(whole, BF16),
            pltpu.VMEM((rows, d), BF16),
            pltpu.VMEM((rows, d), BF16),
            pltpu.VMEM((rows, d), F32),
            pltpu.VMEM((n_t, rows, 3 * wide), BF16),
            pltpu.VMEM((n_t, rows, wide), BF16),
            pltpu.VMEM((rows, d), F32),
            pltpu.VMEM((rows, d), F32),
            pltpu.VMEM((2, rows, d), BF16),
            pltpu.VMEM((2, rows, d), BF16),
            pltpu.VMEM((rows, d), BF16),
            pltpu.VMEM((2 * QB, ROW), F32),
            pltpu.VMEM((3,) + whole, BF16),
            pltpu.VMEM(tables[0].shape, F32),
            pltpu.VMEM(tables[1].shape, F32),
            pltpu.VMEM((8, tables[0].shape[1]), F32),
            dma((2,)), dma((3,)), dma((2, 3)), dma((6 + 2 * n_t,)), dma((PARTS,)), dma((PARTS,)), dma(()),
            dma((count,)), dma((count,)), dma((count, n_dp)), dma((count, n_dp)),
            dma((3,)), dma((3,)), dma((3, n_t)), dma((3, n_t)),
            dma((3, n_t, n_dp)), dma((3, n_t, n_dp)), dma((3, n_t, n_dp)), dma((3, n_t, n_dp)),
        ],
        compiler_params=pltpu.CompilerParams(collective_id=0, has_side_effects=True, vmem_limit_bytes=60 * 2**20),
    )(q_own, o_own, i_own, d_own, x0, gains, seg, obs, *tables)


def attend_slot_back(qkv, do, dqk, dcat, mask):
    wide = do.shape[1]
    heads = wide // HEAD_SIZE
    for h in range(heads):
        q, k, v = (slice((t * heads + h) * HEAD_SIZE, (t * heads + h + 1) * HEAD_SIZE) for t in range(3))
        qh, kh, vh, dh = qkv[:, q], qkv[:, k], qkv[:, v], do[:, q]
        p = probabilities(qh, kh, mask)
        dcat[:, v] = to_keys(p.astype(BF16), dh).astype(BF16)
        dp = by_window(vh, dh)
        ds = (p * (dp - jnp.sum(p * dp, axis=0, keepdims=True))).astype(BF16)
        dqk[:, q] = to_queries(ds, kh) * SCALE
        dqk[:, k] = to_keys(ds, qh) * SCALE


def outer_product(out, left, right):
    step = left.shape[1] // 2

    def turn(j, _):
        at = pl.ds(pl.multiple_of(j * step, 128), step)
        out[at, :] = dot_tn(left[:, at], right[...]).astype(BF16)
        return 0

    lax.fori_loop(0, 2, turn, 0)


def norm_back_rows(g, dn, h, gain, gain_sum, normed, write, part=0, parts=1):
    if part == 0:
        gain_sum[...] = jnp.zeros_like(gain_sum)
    step = 32
    count = h.shape[0] // step // parts

    def body(at):
        hr, dr = h[at, :].astype(F32), dn[at, :]
        r = lax.rsqrt(jnp.mean(hr * hr, axis=1, keepdims=True) + EPS)
        y = gain * dr
        if normed is not None:
            normed[at, :] = (hr * r * gain).astype(BF16)
        gain_sum[...] += jnp.sum((dr * hr * r).reshape(step // 8, 8, -1), axis=0)
        write(at, g[at, :].astype(F32) + r * y - hr * (r * r * r) * jnp.mean(hr * y, axis=1, keepdims=True))

    def turn(r, _):
        body(pl.ds(pl.multiple_of((part * count + r) * step, step), step))
        return 0

    lax.fori_loop(0, count, turn, 0)


def backward_kernel(
    n_dp, n_t, q_own, o_own, i_own, d_own, full, cot, xs, qkv_in, o_in, h2_in, act_in, slope_in, out_in, mask_in, gains,
    cos_in, sin_in,
    layer_acts, grad_acts, out_sums, out_gains, hbm_sums, hbm_got, hbm_ring, du_hbm,
    gbuf, act, du, n, h2, x, dn, ga, proj, qkv, o, do, dcat, dhb, mask, wbuf, cos, sin, halves, gain0, gain1, gain_buf,
    c_sem, w_sem, l_sem, o_sem, a_sem, u_sem, q_sem, st_sem, y_send, y_recv, s1_send, s1_recv, s2_send, s2_recv, t_send, t_recv,
    *reduce_refs,
):
    section = lax.axis_index("section")
    first, second = section == 0, section != 0
    other = {"section": 1 - section}
    l, l2, l3 = (Links(n_dp, n_t) for _ in range(3))
    own = ((q_own, o_own), i_own, d_own)
    rows, d = h2.shape
    wide = do.shape[1]
    places = Places(l)
    slots = places.slot
    order = [(m, j) for j in range(n_t) for m in (2, 1)] + [(0, j) for j in range(n_t)]
    ff = 2 * n_t
    hbm = (hbm_sums, hbm_got, hbm_ring)
    r = Reduce(l, places, order, out_sums, hbm, reduce_refs)
    rm = Reduce(l3, places, order, out_sums, hbm, reduce_refs)
    inner = places.below * places.above == 1
    end_first, inner_first = first & ~inner, first & inner
    r2 = Reduce(l2, places, order, out_sums, hbm, reduce_refs)
    spread1 = Spread(l, places, out_in, layer_acts, s1_send, s1_recv)
    spread1b = Spread(l2, places, out_in, layer_acts, s1_send, s1_recv)
    spread2 = Spread(l, places, dhb, grad_acts, s2_send, s2_recv)
    spread2b = Spread(l2, places, dhb, grad_acts, s2_send, s2_recv)
    load = Loader(wbuf, w_sem, [own[m] if j == n_t - 1 else full.at[m, slots[j]] for m, j in order])

    l.greet([{"tensor": l.up}, {"tensor": l.down}, other] + [{"dp": l.flip(b)} for b in l.bits])
    cot_copy = pltpu.make_async_copy(own_block(cot, l.z, rows), gbuf, l_sem.at[4])

    @pl.when(second)
    def _():
        cot_copy.start()

    def local(src, dst, sem):
        return pltpu.make_async_copy(src, dst, sem)

    load.start(0)
    load.start(1)
    spread1.start()

    acts_in = local(out_in, dhb, l_sem.at[0])
    acts_out = local(dhb, layer_acts.at[l.z], l_sem.at[0])
    h2_copy = local(h2_in, h2, l_sem.at[1])
    x_copy = local(xs, x, l_sem.at[2])
    o_copies = [local(o_in.at[slots[j]], o.at[j], o_sem.at[j]) for j in range(n_t)]

    def act_copy(j):
        return local(act_in.at[slots[j]], act.at[j % 2], a_sem.at[j % 2])

    def slope_copy(j):
        return local(slope_in.at[slots[j]], du.at[j % 2], u_sem.at[j % 2])

    def du_out(j):
        return local(du.at[j % 2], du_hbm.at[slots[j]], st_sem.at[j % 2])

    def du_in(j):
        return local(du_hbm.at[slots[j]], du.at[j % 2], u_sem.at[j % 2])

    def qkv_copy(j):
        return local(qkv_in.at[slots[j]], qkv.at[j % 2], q_sem.at[j % 2])

    slope_copy(0).start()
    act_copy(0).start()
    for c in (h2_copy, acts_in, x_copy, *o_copies):
        c.start()
    tables = [local(t, to, c_sem.at[i]) for i, (t, to) in enumerate(((cos_in, cos), (sin_in, sin), (mask_in, mask)))]
    for c in tables:
        c.start()
    write_halves(halves)

    @pl.when(first)
    def _():
        h2_copy.wait()
        norm_rows(h2, gains[1:2, :], n)

    @pl.when(second)
    def _():
        cot_copy.wait()

    @pl.when(first)
    def _():
        for k in range(1, n_t - 1):
            spread1.step(k)
        for c in range(PARTS):
            over_part(dhb, gbuf, y_send, y_recv, other, c).wait_recv()

    def block_of(reducer, i):
        if i >= 3:
            reducer.clear(i)
        return reducer.block.at[i % 3]

    for j in range(n_t):
        if j + 1 < n_t:
            act_copy(j + 1).start()
            if j + 1 >= 2:
                du_out(j - 1).wait()
            slope_copy(j + 1).start()
        act_copy(j).wait()

        @pl.when(first)
        def _():
            outer_product(block_of(r, 2 * j), gbuf, act.at[j % 2])
            r.pump()
            r.push(2 * j)

        w = load.wait(2 * j)
        slope_copy(j).wait()
        for c in column_steps(act.shape[2]):
            du[j % 2, :, c] = (dot_nt(gbuf[...], w[c, :]) * du[j % 2, :, c].astype(F32)).astype(BF16)
        load.start(2 * j + 2)
        du_out(j).start()

        @pl.when(first)
        def _():
            r.pump()

        w = load.wait(2 * j + 1)
        if j == 0:
            dn[...] = dot_nt(du[j % 2], w[...])
        else:
            dn[...] = dn[...] + dot_nt(du[j % 2], w[...])
        load.start(2 * j + 3)

        @pl.when(first)
        def _():
            r.pump()
            outer_product(block_of(r, 2 * j + 1), n, du.at[j % 2])
            r.pump()
            r.push(2 * j + 1)

        if j >= 2:
            @pl.when(end_first)
            def _():
                r.last_step(j - 2)

    for j in range(max(n_t - 2, 0), n_t):
        du_out(j).wait()

    qkv_copy(0).start()
    acts_in.wait()
    acts_out.start()

    @pl.when(second)
    def _():
        h2_copy.wait()

    def write_middle(at, value):
        h2[at, :] = value
        ga[at, :] = value.astype(BF16)

    norm_back_rows(gbuf, dn, h2, gains[1:2, :], gain1, n, write_middle)
    for c in (*o_copies, *tables):
        c.wait()

    for j in range(n_t):
        if j + 1 < n_t:
            qkv_copy(j + 1).start()
        w = load.wait(ff + j)
        load.start(ff + j + 2)
        do[...] = dot_nt(ga[...], w[3 * wide:, :]).astype(BF16)
        qkv_copy(j).wait()
        @pl.when(first)
        def _():
            r.pump()

        attend_slot_back(qkv.at[j % 2], do, proj, dcat.at[j], mask)

        def turn_back(at):
            v = proj[at, 0:2 * wide]
            dcat[j, at, 0:2 * wide] = (v * cos[at, :] - partner(v, halves) * sin[at, :]).astype(BF16)

        row_loop(rows, 32, turn_back)
        if j == 0:
            dn[...] = dot_nn(dcat[j], w[0:3 * wide, :])
        else:
            dn[...] = dn[...] + dot_nn(dcat[j], w[0:3 * wide, :])
        @pl.when(first)
        def _():
            r.pump()

        if j in (0, 2):
            @pl.when(end_first)
            def _():
                r.last_step(2 + j // 2)

        if j < 2:
            @pl.when(inner_first)
            def _():
                rm.last_step(j)
    x_copy.wait()
    acts_out.wait()

    def write_input(at, value):
        dhb[at, :] = value.astype(BF16)

    for c in range(PARTS):
        norm_back_rows(h2, dn, x, gains[0:1, :], gain0, None, write_input, c, PARTS)

        @pl.when(second)
        def _():
            over_part(dhb, gbuf, y_send, y_recv, other, c).start()

    spread2.start()
    grads_out = local(dhb, grad_acts.at[l.z], l_sem.at[0])
    grads_out.start()

    @pl.when(second)
    def _():
        du_in(0).start()
        act_copy(0).start()
        for j in range(n_t):
            if j + 1 < n_t:
                act_copy(j + 1).start()
                du_in(j + 1).start()
            act_copy(j).wait()
            outer_product(block_of(r2, 2 * j), gbuf, act.at[j % 2])
            r2.pump()
            r2.push(2 * j)
            du_in(j).wait()
            outer_product(block_of(r2, 2 * j + 1), n, du.at[j % 2])
            r2.pump()
            r2.push(2 * j + 1)
        spread1b.step(1)
        r2.flush()

    total = Total(l, gain0, gain_buf, t_send, t_recv)
    gain0[0:1, :] = jnp.sum(gain0[...], axis=0, keepdims=True)
    gain0[1:2, :] = jnp.sum(gain1[...], axis=0, keepdims=True)
    norm_rows(x, gains[0:1, :], n)
    for j in range(n_t):
        b = block_of(r, ff + j)
        step = d // 2

        def turn(c, _):
            at = pl.ds(pl.multiple_of(c * step, 128), step)
            b[at, 0:3 * wide] = dot_tn(n[:, at], dcat[j]).astype(BF16)
            b[at, 3 * wide:] = dot_tn(ga[:, at], o[j]).astype(BF16)
            return 0

        lax.fori_loop(0, 2, turn, 0)
        r.pump()
        r.push(ff + j)
    r.flush()

    @pl.when(inner_first)
    def _():
        for i in range(2, 4):
            rm.last_step(i)

    @pl.when(second)
    def _():
        for i in range(4):
            r2.last_step(i)
        for k in range(2, n_t - 1):
            spread1b.step(k)

    for i in range(4, len(order)):
        r.last_step(i)
        if i == 4 or i == 5:
            @pl.when(inner)
            def _():
                spread2.step(i - 3)
        if i >= 6 and i - 6 < total.count:
            total.step(i - 6)
    for t in range(len(order) - 6, total.count):
        total.step(t)
    l2.recording = False

    @pl.when(~inner)
    def _():
        for k in range(1, n_t - 1):
            spread2b.step(k)

    spread1.step(n_t - 1)
    spread2.step(n_t - 1)
    out_gains[...] = total.result()
    r.close()
    grads_out.wait()

    @pl.when(second)
    def _():
        for c in range(PARTS):
            over_part(dhb, gbuf, y_send, y_recv, other, c).wait_send()

    l.drain()


def run_backward(q_own, o_own, i_own, d_own, kept, cot, gains, tables):
    n_dp, n_t = lax.axis_size("dp"), lax.axis_size("tensor")
    wide, d = o_own.shape
    rows = cot.shape[0] * cot.shape[1] // n_t
    piece = d // n_dp
    count = 3 * n_t
    steps = len(ring_bits(n_dp)) + n_t
    dma = pltpu.SemaphoreType.DMA
    hbm, vmem = pl.BlockSpec(memory_space=pl.ANY), pl.BlockSpec(memory_space=pltpu.VMEM)

    def shape(*s, t=BF16):
        return jax.ShapeDtypeStruct(s, t)

    def buf(*s, t=BF16):
        return pltpu.VMEM(s, t)

    return pl.pallas_call(
        functools.partial(backward_kernel, n_dp, n_t),
        out_shape=[
            shape(n_t, rows, d), shape(n_t, rows, d), shape(3, piece, d, t=F32), shape(8, d, t=F32),
            *reduce_hbm(n_dp, n_t, count, piece, d), shape(n_t, rows, d),
        ],
        in_specs=[hbm] * 14 + [vmem] + [hbm] * 2,
        out_specs=[hbm] * 3 + [vmem] + [hbm] * 4,
        scratch_shapes=[
            buf(rows, d), buf(2, rows, d), buf(2, rows, d), buf(rows, d), buf(rows, d, t=F32), buf(rows, d),
            buf(rows, d, t=F32), buf(rows, d), buf(rows, d, t=F32), buf(2, rows, 3 * wide), buf(n_t, rows, wide),
            buf(rows, wide), buf(n_t, rows, 3 * wide), buf(rows, d), buf(2 * QB, ROW, t=F32), buf(3, 4 * wide, d),
            buf(*tables[0].shape, t=F32), buf(*tables[1].shape, t=F32), buf(8, tables[0].shape[1], t=F32),
            buf(8, d, t=F32), buf(8, d, t=F32), buf(2 * steps, 8, d, t=F32),
            dma((3,)), dma((2, 3)), dma((5,)), dma((n_t,)), dma((2,)), dma((2,)), dma((2,)), dma((2,)), dma((PARTS,)), dma((PARTS,)),
            dma((2, n_t)), dma((2, n_t)), dma((2, n_t)), dma((2, n_t)), dma((steps,)), dma((steps,)),
            *reduce_scratch(n_dp, n_t, count, piece, d),
        ],
        compiler_params=pltpu.CompilerParams(collective_id=1, has_side_effects=True, vmem_limit_bytes=62 * 2**20),
    )(q_own, o_own, i_own, d_own, kept[0], cot, *kept[1:], gains, *tables)


def finish_kernel(n_dp, layer_in, grad_in, sums, gain, layer_out, grad_out, qkv, out, w_in, down, gain_out, rows, heads, wide, sem, heads_sem, wide_sem):
    arrays = ((layer_in, layer_out), (grad_in, grad_out))
    n = layer_in.shape[0]

    def load(i):
        return pltpu.make_async_copy(arrays[i // n][0].at[i % n], rows.at[i], sem.at[0, i])

    def store(i):
        return pltpu.make_async_copy(rows.at[i], arrays[i // n][1].at[i % n], sem.at[1, i])

    heads_in = pltpu.make_async_copy(sums.at[0], heads, heads_sem)
    wide_in = [pltpu.make_async_copy(sums.at[1 + m], wide.at[m], wide_sem.at[0, m]) for m in range(2)]
    wide_out = [pltpu.make_async_copy(wide.at[m], to, wide_sem.at[1, m]) for m, to in enumerate((w_in, down))]
    heads_in.start()
    for c in wide_in:
        c.start()
    for i in range(2 * n):
        load(i).start()
    hd = out.shape[0]
    me = lax.axis_index("dp")
    for k in range(n_dp):
        @pl.when(me == k)
        def _():
            gain_out[...] = gain[0:2, k * gain_out.shape[1]:(k + 1) * gain_out.shape[1]]

    for c, o in zip(wide_in, wide_out):
        c.wait()
        o.start()
    for i in range(2 * n):
        load(i).wait()
        store(i).start()
    heads_in.wait()
    for t in range(3):
        qkv[t] = heads[:, t * hd:(t + 1) * hd]
    out[...] = jnp.transpose(heads[:, 3 * hd:])
    for o in wide_out:
        o.wait()
    for i in range(2 * n):
        store(i).wait()


def lay_out(layer_acts, grad_acts, sums, gain, n_dp):
    n, rows, d = layer_acts.shape
    piece, hd = sums.shape[1], sums.shape[2] // 4
    hbm, vmem = pl.BlockSpec(memory_space=pl.ANY), pl.BlockSpec(memory_space=pltpu.VMEM)
    dma = pltpu.SemaphoreType.DMA
    acts = jax.ShapeDtypeStruct(layer_acts.shape, BF16)

    def shape(*s):
        return jax.ShapeDtypeStruct(s, F32)

    return pl.pallas_call(
        functools.partial(finish_kernel, n_dp),
        out_shape=[acts, acts, shape(3, piece, hd), shape(hd, piece), shape(piece, d), shape(piece, d), shape(2, d // n_dp)],
        in_specs=[hbm, hbm, hbm, vmem],
        out_specs=[hbm, hbm, vmem, vmem, hbm, hbm, vmem],
        scratch_shapes=[
            pltpu.VMEM((2 * n, rows, d), BF16), pltpu.VMEM((piece, d), F32), pltpu.VMEM((2, piece, d), F32),
            dma((2, 2 * n)), dma(()), dma((2, 2)),
        ],
        compiler_params=pltpu.CompilerParams(vmem_limit_bytes=62 * 2**20),
    )(layer_acts, grad_acts, sums, gain)


def on_device(tokens, cotangent, seg_ids, observed, w_qkv, w_out, w_in, w_down, norm_gains):
    n_dp, n_t = lax.axis_size("dp"), lax.axis_size("tensor")
    w_qkv, w_out, w_in, w_down, gains = w_qkv[0], w_out[0], w_in[0], w_down[0], norm_gains[0]
    micro, rows, d = tokens.shape
    hd = w_out.shape[0]
    tables = rope_tables()
    heads = jnp.swapaxes(w_qkv, 1, 2).reshape(3 * hd, d)
    kept = run_forward(heads, w_out, w_in, w_down, tokens, gains, seg_ids, observed, tables)[:9]
    layer_acts, grad_acts, sums, gain = run_backward(heads, w_out, w_in, w_down, kept, cotangent, gains, tables)[:4]
    layer_acts, grad_acts, r_qkv, r_out, r_in, r_down, gain = lay_out(layer_acts, grad_acts, sums, gain, n_dp)
    return (
        layer_acts.reshape(1, micro, rows, d),
        grad_acts.reshape(1, micro, rows, d),
        r_qkv[None],
        r_out[None],
        r_in[None],
        r_down.T[None],
        gain[None],
    )


def solution(mesh):
    return jax.shard_map(
        on_device,
        mesh=mesh,
        in_specs=(
            P(None, "dp", None),
            P(None, "dp", None),
            P(None, "dp"),
            P(None, "dp"),
            P("section", None, None, "tensor"),
            P("section", "tensor", None),
            P("section", None, "tensor"),
            P("section", "tensor", None),
            P("section", None, None),
        ),
        out_specs=(
            P("section", None, "dp", None),
            P("section", None, "dp", None),
            P("section", None, "dp", "tensor"),
            P("section", "tensor", "dp"),
            P("section", "dp", "tensor"),
            P("section", "tensor", "dp"),
            P("section", None, "dp"),
        ),
        check_vma=False,
    )
```

```python
import functools
import math

import jax
import jax.numpy as jnp
import numpy as np
from jax import lax
from jax.experimental import pallas as pl
from jax.experimental.pallas import tpu as pltpu
from jax.sharding import PartitionSpec as P

HEAD_SIZE = 80
HALF = HEAD_SIZE // 2
ROW = 512
QB = 128
GROUP = 8
EPS = 1e-06
BIG = 1000000000.0
SCALE = 1.0 / math.sqrt(HEAD_SIZE)
BF16 = jnp.bfloat16
F32 = jnp.float32
MESH = pl.DeviceIdType.MESH


def dot_nn(a, b):
    return lax.dot_general(a, b, (((1,), (0,)), ((), ())), preferred_element_type=F32)


def dot_nt(a, b):
    return lax.dot_general(a, b, (((1,), (1,)), ((), ())), preferred_element_type=F32)


def dot_tn(a, b):
    return lax.dot_general(a, b, (((0,), (0,)), ((), ())), preferred_element_type=F32)


def rope_tables():
    freq = 10000.0 ** (-np.arange(HALF) / HALF)
    ang = np.arange(ROW)[:, None] * freq[None, :]
    cos, sin = np.cos(ang), np.sin(ang)
    cos_full = np.tile(np.concatenate([cos, cos], axis=1), (1, GROUP))
    sin_full = np.tile(np.concatenate([-sin, sin], axis=1), (1, GROUP))
    return jnp.asarray(cos_full, F32), jnp.asarray(sin_full, F32)


def write_halves(halves):
    lane = lax.broadcasted_iota(jnp.int32, halves.shape, 1)
    halves[...] = (lax.rem(lane, HEAD_SIZE) < HALF).astype(F32)


def partner(x, halves):
    return jnp.where(halves[0:1, :] > 0, pltpu.roll(x, x.shape[1] - HALF, 1), pltpu.roll(x, HALF, 1))


def windows():
    return [max(i - 1, 0) * QB for i in range(ROW // QB)]


def own_row(ref, z):
    per = ref.shape[1] // ROW
    at = pl.multiple_of(lax.rem(z, per) * ROW, ROW)
    return ref[pl.ds(z // per, 1), pl.ds(at, ROW)].astype(F32)


def column(row):
    return jnp.transpose(jnp.broadcast_to(row, (128, ROW)))[:, 0:1]


def write_mask(mask, seg_ids, observed, z):
    seg_row = own_row(seg_ids, z)
    seg_col, obs_col = column(seg_row), column(own_row(observed, z))
    for i, k0 in enumerate(windows()):
        keys, queries = slice(k0, k0 + 2 * QB), slice(i * QB, (i + 1) * QB)
        shape = (2 * QB, QB)
        kj = lax.broadcasted_iota(jnp.int32, shape, 0) + k0
        qi = lax.broadcasted_iota(jnp.int32, shape, 1) + i * QB
        same = seg_col[keys, :] == seg_row[:, queries]
        seen = (obs_col[keys, :] == 1.0) | (kj == qi)
        mask[:, queries] = (same & (kj <= qi) & seen).astype(F32)


def query_block(x, i):
    return x[:, i * QB:(i + 1) * QB]


def by_window(keys, queries):
    return jnp.concatenate(
        [dot_nt(keys[k0:k0 + 2 * QB], queries[i * QB:(i + 1) * QB]) for i, k0 in enumerate(windows())], axis=1
    )


def to_queries(weights, keys):
    return jnp.concatenate(
        [dot_tn(query_block(weights, i), keys[k0:k0 + 2 * QB]) for i, k0 in enumerate(windows())], axis=0
    )


def to_keys(weights, queries):
    blocks = [None] * (ROW // QB)
    for i, k0 in enumerate(windows()):
        term = dot_nn(query_block(weights, i), queries[i * QB:(i + 1) * QB])
        for j in range(2):
            at, part = k0 // QB + j, term[j * QB:(j + 1) * QB]
            blocks[at] = part if blocks[at] is None else blocks[at] + part
    return jnp.concatenate(blocks, axis=0)


def probabilities(q, k, mask):
    s = jnp.where(mask[...] > 0, by_window(k, q) * SCALE, -BIG)
    e = jnp.exp(s - jnp.max(s, axis=0, keepdims=True))
    return e * (1.0 / jnp.sum(e, axis=0, keepdims=True))


def ring_bits(n):
    return [1 << i for i in range(n.bit_length() - 1)]


def low_bit(j):
    return j & -j


class Links:
    def __init__(self, n_dp, n_t):
        self.n_dp, self.n_t = n_dp, n_t
        self.me, self.z = lax.axis_index("dp"), lax.axis_index("tensor")
        self.down = lax.rem(self.z + n_t - 1, n_t)
        self.up = lax.rem(self.z + 1, n_t)
        self.bits = ring_bits(n_dp)
        self.sent, self.recording = {}, True

    def flip(self, bit):
        return self.me + bit - 2 * bit * lax.rem(self.me // bit, 2)

    def mix(self, j):
        at = self.me
        for bit in self.bits:
            if j & bit:
                at = at + bit - 2 * bit * lax.rem(self.me // bit, 2)
        return at

    def place(self, table):
        n = self.n_t
        return sum(v * (1 - ((self.z - k) * (self.z - k) + n * n - 1) // (n * n)) for k, v in enumerate(table))

    def own_bit(self, bit):
        return lax.rem(self.me // bit, 2)

    def greet(self, axes):
        barrier = pltpu.get_barrier_semaphore()
        for where in axes:
            pl.semaphore_signal(barrier, inc=1, device_id=where, device_id_type=MESH)
        pl.semaphore_wait(barrier, len(axes))

    def send(self, src, dst, send_sem, recv_sem, where, tag=None, again=None, when=None):
        pltpu.make_async_remote_copy(
            src_ref=src, dst_ref=dst, send_sem=send_sem, recv_sem=recv_sem, device_id=where, device_id_type=MESH
        ).start()
        if self.recording:
            self.sent.setdefault(tag, []).append((again or (lambda: (src, send_sem)), when))

    def finish(self, tag):
        def left(again):
            ref, sem = again()
            pltpu.make_async_remote_copy(
                src_ref=ref, dst_ref=ref, send_sem=sem, recv_sem=sem, device_id={"tensor": self.down}, device_id_type=MESH
            ).wait_send()

        for again, when in self.sent.pop(tag, ()):
            if when is None:
                left(again)
            else:
                pl.when(when())(functools.partial(left, again))

    def arrived(self, ref, sem, send_sem, where):
        pltpu.make_async_remote_copy(
            src_ref=ref, dst_ref=ref, send_sem=send_sem, recv_sem=sem, device_id=where, device_id_type=MESH
        ).wait_recv()

    def drain(self):
        for tag in list(self.sent):
            self.finish(tag)


class Gather:
    def __init__(self, links, own, full, parts, z_send, z_recv, p_send, p_recv):
        self.l, self.own, self.full, self.parts = links, own, full, parts
        self.z_send, self.z_recv, self.p_send, self.p_recv = z_send, z_recv, p_send, p_recv
        self.rows = own[0].shape[0] // links.n_dp
        self.units = [(m, k, h) for m, k in gather_order(links.n_t) for h in range(len(parts))]
        self.at = {u: i for i, u in enumerate(self.units)}

    def piece(self, m, slot, index, h):
        off, size = self.parts[h]
        first = pl.multiple_of(index * self.rows + off, 16)
        if slot == 0:
            return self.own[m].at[pl.ds(first, size), :]
        return self.full.at[m, slot, pl.ds(first, size), :]

    def like(self, h):
        return self.full.at[0, 1, pl.ds(0, self.parts[h][1]), :]

    def send_z(self, m, k, h):
        l = self.l
        i = self.at[(m, k, h)]
        l.send(self.piece(m, k - 1, l.me, h), self.piece(m, k, l.me, h), self.z_send.at[i], self.z_recv.at[i], {"tensor": l.down},
               again=lambda: (self.like(h), self.z_send.at[i]))

    def advance(self, taken):
        for unit in due(self.units, self.issued, taken, 2 * len(self.parts)):
            self.send_z(*unit)
            self.issued += 1

    def start(self):
        self.issued = 0
        self.advance(0)

    def share(self, i, j):
        m, k, h = self.units[i]
        l = self.l
        for bit in reversed(l.bits):
            if j == 0 or bit < low_bit(j):
                ref = self.piece(m, k, l.mix(j), h)
                l.send(ref, ref, self.p_send.at[i, j ^ bit], self.p_recv.at[i, j ^ bit], {"dp": l.flip(bit)},
                       again=lambda at=j ^ bit: (self.like(h), self.p_send.at[i, at]))

    def take(self, i):
        m, k, h = self.units[i]
        l = self.l
        l.arrived(self.piece(m, k, l.me, h), self.z_recv.at[i], self.z_send.at[i], {"tensor": l.up})
        self.advance(i + 1)
        self.share(i, 0)

    def relay(self, i, bit):
        m, k, h = self.units[i]
        l = self.l
        for j in range(bit, l.n_dp, 2 * bit):
            l.arrived(self.piece(m, k, l.mix(j), h), self.p_recv.at[i, j], self.p_send.at[i, j], {"dp": l.flip(low_bit(j))})
            self.share(i, j)

    def walk(self, lent=None, lag=2):
        hops = self.l.bits[::-1]
        for i in range(len(self.units) + lag + len(hops) - 1):
            if i < len(self.units):
                m, k, h = self.units[i]
                self.take(i)
                if lent is not None and h == 0:
                    lent.take_back(m, k)
            done = None
            for hop, bit in enumerate(hops):
                at = i - lag - hop
                if 0 <= at < len(self.units):
                    self.relay(at, bit)
                    m, k, h = self.units[at]
                    if hop == len(hops) - 1 and h == len(self.parts) - 1:
                        if lent is not None:
                            lent.finish_back(m, k)
                        done = (m, k)
            yield done


class Lend:
    def __init__(self, links, own, full, held, y_send, y_recv, z_send, z_recv, p_send, p_recv, b_send, b_recv):
        self.l, self.own, self.full, self.held = links, own, full, held
        self.y_send, self.y_recv, self.z_send, self.z_recv = y_send, y_recv, z_send, z_recv
        self.p_send, self.p_recv, self.b_send, self.b_recv = p_send, p_recv, b_send, b_recv
        self.rows = own[0].shape[0] // links.n_dp
        self.size = held.shape[3]
        self.even = [j for j in range(0, links.n_dp, 2)]
        self.where = {"section": 1 - lax.axis_index("section")}

    def rows_of(self, j):
        return pl.ds(pl.multiple_of(self.l.mix(j) * self.rows, 16), self.size)

    def like(self):
        return self.held.at[0, 0, 0]

    def send(self, src, dst, sems, at, where):
        self.l.send(src, dst, sems[0].at[at], sems[1].at[at], where, again=lambda: (self.like(), sems[0].at[at]))

    def arrived(self, ref, sems, at):
        self.l.arrived(ref, sems[1].at[at], sems[0].at[at], self.where)

    def give(self):
        for m in range(3):
            self.send(self.own[m].at[self.rows_of(0), :], self.held.at[m, 0, self.l.me], (self.y_send, self.y_recv), (m,), self.where)

    def take_back(self, m, k):
        for j in self.even:
            ref = self.full.at[m, k, self.rows_of(j), :]
            self.arrived(ref, (self.b_send, self.b_recv), (m, k, j))
            self.send(ref, ref, (self.p_send, self.p_recv), (m, k, j + 1), {"dp": self.l.flip(1)})

    def finish_back(self, m, k):
        for j in self.even:
            self.arrived(self.full.at[m, k, self.rows_of(j + 1), :], (self.p_send, self.p_recv), (m, k, j + 1))

    def ring(self, m, k):
        l = self.l
        self.send(self.held.at[m, k - 1, l.me], self.held.at[m, k, l.me], (self.z_send, self.z_recv), (m, k), {"tensor": l.down})

    def back(self, m, k, j):
        l = self.l
        self.send(self.held.at[m, k, l.mix(j)], self.full.at[m, k, self.rows_of(j), :], (self.b_send, self.b_recv), (m, k, j), self.where)

    def share(self, m, k, j):
        l = self.l
        for bit in reversed(l.bits[1:]):
            if j == 0 or bit < low_bit(j):
                ref = self.held.at[m, k, l.mix(j)]
                self.send(ref, ref, (self.p_send, self.p_recv), (m, k, j ^ bit), {"dp": l.flip(bit)})

    def serve(self, lag=1):
        l = self.l
        units = gather_order(l.n_t)
        issued = 0
        started = False
        for i in range(len(units) + lag):
            for m, k in due(units, issued, i, 3):
                if k == 1:
                    self.arrived(self.held.at[m, 0, l.me], (self.y_send, self.y_recv), (m,))
                self.ring(m, k)
                issued += 1
            if issued == len(units) and not started:
                started = True
                yield
            if i < len(units):
                m, k = units[i]
                self.arrived(self.held.at[m, k, l.me], (self.z_send, self.z_recv), (m, k))
                self.share(m, k, 0)
                self.back(m, k, 0)
            if i >= lag:
                m, k = units[i - lag]
                for j in sorted(self.even[1:], key=lambda j: (-low_bit(j), j)):
                    self.arrived(self.held.at[m, k, l.mix(j)], (self.p_send, self.p_recv), (m, k, j))
                    self.share(m, k, j)
                    self.back(m, k, j)


def gather_order(n_t):
    heads = [(0, k) for k in range(1, n_t)]
    rest = [(m, k) for k in range(1, n_t) for m in (1, 2)]
    return [u for pair in zip(heads, rest) for u in pair] + rest[len(heads):]


def due(units, issued, taken, ahead):
    found = []
    while issued < min(len(units), taken + ahead):
        m, k, *h = units[issued]
        if k > 1 and units.index((m, k - 1, *h)) >= taken:
            break
        found.append(units[issued])
        issued += 1
    return found


def gather_parts(rows):
    lent = rows // 4 // 16 * 16
    if rows % 32:
        return lent, [(lent, rows - lent)], [(0, rows)]
    cut = lent + (rows - lent + 31) // 32 * 16
    return lent, [(lent, cut - lent), (cut, rows - cut)], [(0, rows // 2), (rows // 2, rows // 2)]


def level_start(n_dp, level):
    return sum(n_dp >> (t + 1) for t in range(level))


def add_rows(out, *terms):
    rows = out.shape[0]
    step = 64 if rows % 64 == 0 else 16

    def body(r, _):
        at = pl.ds(pl.multiple_of(r * step, step), step)
        total = terms[0][at, :].astype(F32)
        for t in terms[1:]:
            total = total + t[at, :].astype(F32)
        out[at, :] = total.astype(out.dtype)
        return 0

    lax.fori_loop(0, rows // step, body, 0)


def reduce_scratch(n_dp, n_t, count, rows, c):
    dma = pltpu.SemaphoreType.DMA
    half = n_dp // 2
    return [
        pltpu.VMEM((3, n_dp * rows, c), BF16),
        pltpu.VMEM((2, half, rows, c), BF16),
        pltpu.VMEM((3, rows, c), BF16),
        pltpu.VMEM((3, rows, c), BF16),
        pltpu.VMEM((rows, c), F32),
        dma((count, n_dp)),
        dma((count, n_dp)),
        dma((count,)),
        dma((count // n_t, n_t, 2)),
        dma((2,)),
        dma((2,)),
        dma((3,)),
        dma(()),
    ]


def reduce_hbm(n_dp, n_t, count, rows, c):
    return [
        jax.ShapeDtypeStruct((count, n_dp // 2, rows, c), BF16),
        jax.ShapeDtypeStruct((count, n_dp - 1, rows, c), BF16),
        jax.ShapeDtypeStruct((count // n_t, n_t, 2, rows, c), BF16),
    ]


def line_order(n_t):
    return [sorted(range(n_t), key=lambda s: (-abs(s - z), -max(s, n_t - 1 - s))) for z in range(n_t)]


class Places:
    def __init__(self, links):
        n_t = links.n_t
        orders = line_order(n_t)
        self.shard = [links.place([o[j] for o in orders]) for j in range(n_t)]
        self.slot = [links.place([(o[j] - z) % n_t for z, o in enumerate(orders)]) for j in range(n_t - 1)] + [0]
        self.up = [links.place([int(o[j] > z) for z, o in enumerate(orders)]) for j in range(n_t)]
        self.below = (links.z + n_t - 1) // n_t
        self.above = (2 * n_t - 2 - links.z) // n_t


def travel_order(order):
    if len(order) != 12:
        return list(range(len(order)))
    return [0, 1, 2, 3, 4, 8, 5, 9, 6, 10, 7, 11]


class Reduce:
    def __init__(self, links, places, order, out, hbm, scratch):
        self.l, self.places, self.order, self.out = links, places, order, out
        self.sums, self.got, self.ring = hbm
        (self.block, self.fetched, self.terms, self.moving, self.final,
         self.c_send, self.c_recv, self.z_send, self.z_recv,
         self.f_sem, self.s_sem, self.t_sem, self.o_sem) = scratch
        self.moves = []
        self.queue = travel_order(order)
        self.stored, self.gone = set(), 0
        self.levels = len(links.bits)
        self.rows = self.fetched.shape[2]
        self.storing = None

    def offsets(self, level):
        bits = self.l.bits[level + 1:]
        return [sum(b for n, b in enumerate(bits) if k >> n & 1) for k in range(1 << len(bits))]

    def mine(self, level):
        return lax.rem(self.l.me, 1 << (level + 1))

    def give(self, i, level, source):
        l, bit = self.l, self.l.bits[level]
        there = self.mine(level) + bit - 2 * bit * l.own_bit(bit)
        for n, off in enumerate(self.offsets(level)):
            at = (i, level_start(l.n_dp, level) + n)
            l.send(source(there + off), self.got.at[at], self.c_send.at[at], self.c_recv.at[at], {"dp": l.flip(bit)}, (i, level),
                   again=lambda at=at: (self.got.at[at], self.c_send.at[at]))

    def receive(self, i, level):
        l = self.l
        for n, _ in enumerate(self.offsets(level)):
            at = (i, level_start(l.n_dp, level) + n)
            l.arrived(self.got.at[at], self.c_recv.at[at], self.c_send.at[at], {"dp": l.flip(l.bits[level])})

    def piece(self, i, p):
        return self.block.at[i % 3, pl.ds(pl.multiple_of(p * self.rows, 16), self.rows), :]

    def give_block(self, i):
        self.give(i, 0, lambda p: self.piece(i, p))

    def fetch_copy(self, i):
        return pltpu.make_async_copy(self.got.at[i, pl.ds(0, self.l.n_dp // 2)], self.fetched.at[i % 2], self.f_sem.at[i % 2])

    def fetch(self, i):
        self.receive(i, 0)
        self.fetch_copy(i).start()

    def store_copy(self, i):
        return pltpu.make_async_copy(self.fetched.at[i % 2], self.sums.at[i], self.s_sem.at[i % 2])

    def add_first(self, i):
        self.fetch_copy(i).wait()
        for n in range(self.l.n_dp // 2):
            here = self.fetched.at[i % 2, n]
            add_rows(here, self.piece(i, 2 * n + self.l.own_bit(1)), here)
        self.store_copy(i).start()

    def give_next(self, i):
        self.store_copy(i).wait()
        self.stored.add(i)
        while self.gone < len(self.queue) and self.queue[self.gone] in self.stored:
            at = self.queue[self.gone]
            self.give(at, 1, lambda piece: self.sums.at[at, piece // 2])
            self.gone += 1

    def push(self, i):
        self.give_block(i)
        self.moves.append([i, 0])

    def pump(self):
        for move in list(self.moves):
            i, stage = move
            if stage == 0 and any(o[0] == i - 2 for o in self.moves):
                break
            (self.fetch, self.add_first, self.give_next)[stage](i)
            move[1] += 1
            if move[1] == 3:
                self.moves.remove(move)

    def flush(self, i=None):
        while any(i is None or o[0] == i for o in self.moves):
            self.pump()

    def clear(self, i):
        while any(o[0] == i - 3 and o[1] < 2 for o in self.moves):
            self.pump()
        self.l.finish((i - 3, 0))

    def middle(self, i, level):
        l = self.l
        self.receive(i, level)
        for n, off in enumerate(self.offsets(level)):
            piece = (self.mine(level) + off) // 2
            loads = [
                pltpu.make_async_copy(self.sums.at[i, piece], self.terms.at[0], self.t_sem.at[0]),
                pltpu.make_async_copy(self.got.at[i, level_start(l.n_dp, level) + n], self.terms.at[1], self.t_sem.at[1]),
            ]
            for c in loads:
                c.start()
            for c in loads:
                c.wait()
            add_rows(self.terms.at[2], self.terms.at[0], self.terms.at[1])
            back = pltpu.make_async_copy(self.terms.at[2], self.sums.at[i, piece], self.t_sem.at[2])
            back.start()
            back.wait()
        self.give(i, level + 1, lambda piece: self.sums.at[i, piece // 2])

    def term_copies(self, i):
        l = self.l
        return [
            pltpu.make_async_copy(self.sums.at[i, l.me // 2], self.terms.at[0], self.t_sem.at[0]),
            pltpu.make_async_copy(self.got.at[i, l.n_dp - 2], self.terms.at[1], self.t_sem.at[1]),
        ]

    def collect(self, i):
        self.receive(i, self.levels - 1)
        for c in self.term_copies(i):
            c.start()

    def out_copy(self, m):
        return pltpu.make_async_copy(self.final, self.out.at[m], self.o_sem)

    def come(self, m, s, way):
        l = self.l
        ref = self.ring.at[m, s, way]
        l.arrived(ref, self.z_recv.at[m, s, way], self.z_send.at[0], {"tensor": l.down})
        copy = pltpu.make_async_copy(ref, self.terms.at[2], self.t_sem.at[2])
        copy.start()
        copy.wait()

    def pass_on(self, i, turn):
        l, p = self.l, self.places
        m, j = self.order[i]
        l.finish(("z", turn - 3))
        terms = [self.terms.at[t] for t in range(3)]
        if j < l.n_t - 1:
            s, up, out = p.shard[j], p.up[j], self.moving.at[turn % 3]
            behind = up * p.below + (1 - up) * p.above
            for c in self.term_copies(i):
                c.wait()

            @pl.when(behind == 1)
            def _():
                self.come(m, s, 1 - up)
                add_rows(out, *terms)

            @pl.when(behind == 0)
            def _():
                add_rows(out, *terms[:2])

            l.send(out, self.ring.at[m, s, 1 - up], self.z_send.at[i], self.z_recv.at[m, s, 1 - up], {"tensor": l.z + 2 * up - 1},
                   ("z", turn), again=lambda: (self.moving.at[turn % 3], self.z_send.at[i]))
        else:
            if self.storing is not None:
                self.out_copy(self.storing).wait()
            for c in self.term_copies(i):
                c.wait()
            add_rows(self.final, *terms[:2])
            for way, there in ((0, p.below), (1, p.above)):
                @pl.when(there == 1)
                def _():
                    self.come(m, l.z, way)
                    add_rows(self.final, self.final, terms[2])
            self.out_copy(m).start()
            self.storing = m

    def last_step(self, turn):
        i = self.queue[turn]
        for before in self.queue[:turn + 1]:
            self.flush(before)
        for level in range(1, self.levels - 1):
            self.middle(i, level)
        self.collect(i)
        self.pass_on(i, turn)

    def close(self):
        self.out_copy(self.storing).wait()


class Spread:
    def __init__(self, links, places, block, out, send, recv):
        self.l, self.places, self.block, self.out, self.send, self.recv = links, places, block, out, send, recv

    def pass_on(self, source, at, way, k):
        l, p = self.l, self.places
        l.send(source, self.out.at[at], self.send.at[way, k], self.recv.at[way, k], {"tensor": l.z + 1 - 2 * way},
               again=lambda: (self.out.at[0], self.send.at[way, k]),
               when=lambda: ((p.above, p.below)[way] == 1) if k == 0 else self.passes(way, k))

    def passes(self, way, k):
        z, n = self.l.z, self.l.n_t
        return (z >= k) & (z < n - 1) if way == 0 else (z < n - k) & (z > 0)

    def start(self):
        p = self.places
        for way, there in ((0, p.above), (1, p.below)):
            @pl.when(there == 1)
            def _():
                self.pass_on(self.block, self.l.z, way, 0)

    def step(self, k):
        l = self.l
        for way in range(2):
            at = l.z + k * (2 * way - 1)

            @pl.when(l.z >= k if way == 0 else l.z < l.n_t - k)
            def _():
                l.arrived(self.out.at[at], self.recv.at[way, k - 1], self.send.at[way, k - 1], {"tensor": l.down})

            if k < l.n_t - 1:
                @pl.when(self.passes(way, k))
                def _():
                    self.pass_on(self.out.at[at], at, way, k)


class Total:
    def __init__(self, links, block, buf, send, recv):
        self.l, self.block, self.buf, self.s, self.r = links, block, buf, send, recv
        self.levels = len(links.bits)
        self.count = self.levels + links.n_t

    def step(self, s):
        l, buf = self.l, self.buf
        if s == 0:
            buf[1] = self.block[...]
        else:
            l.arrived(buf.at[2 * s], self.r.at[s - 1], self.s.at[s - 1], {"tensor": l.up})
            if s <= self.levels:
                buf[2 * s + 1] = buf[2 * s - 1] + buf[2 * s]
        if s < self.levels:
            l.send(buf.at[2 * s + 1], buf.at[2 * s + 2], self.s.at[s], self.r.at[s], {"dp": l.flip(l.bits[s])})
        elif s < self.count - 1:
            src = 2 * s + 1 if s == self.levels else 2 * s
            l.send(buf.at[src], buf.at[2 * s + 2], self.s.at[s], self.r.at[s], {"tensor": l.down})

    def result(self):
        total = self.buf[2 * self.levels + 1]
        for k in range(1, self.l.n_t):
            total = total + self.buf[2 * (self.levels + k)]
        return total


def row_loop(rows, step, body):
    def turn(r, _):
        body(pl.ds(pl.multiple_of(r * step, step), step))
        return 0

    lax.fori_loop(0, rows // step, turn, 0)


def column_steps(width):
    return [slice(c, c + 256) for c in range(0, width, 256)]


def norm_rows(source, gain, out):
    def body(at):
        h = source[at, :].astype(F32)
        r = lax.rsqrt(jnp.mean(h * h, axis=1, keepdims=True) + EPS)
        out[at, :] = (h * r * gain).astype(BF16)

    row_loop(source.shape[0], 64, body)


def own_block(ref, z, rows):
    per = ref.shape[1] // rows
    return ref.at[z // per, pl.ds(pl.multiple_of(lax.rem(z, per) * rows, rows), rows), :]


def attend_slot(qkv, o, mask):
    heads = o.shape[1] // HEAD_SIZE
    for h in range(heads):
        q, k, v = (slice((t * heads + h) * HEAD_SIZE, (t * heads + h + 1) * HEAD_SIZE) for t in range(3))
        p = probabilities(qkv[:, q], qkv[:, k], mask).astype(BF16)
        o[:, q] = to_queries(p, qkv[:, v]).astype(BF16)


class Loader:
    def __init__(self, buf, sem, blocks):
        self.buf, self.sem, self.blocks = buf, sem, blocks

    def copies(self, j):
        slot, first, found = j % self.buf.shape[0], 0, []
        block = self.blocks[j]
        for n, ref in enumerate(block if isinstance(block, tuple) else (block,)):
            to = self.buf.at[slot, pl.ds(first, ref.shape[0]), :]
            found.append(pltpu.make_async_copy(ref, to, self.sem.at[n, slot]))
            first += ref.shape[0]
        return found

    def start(self, j):
        if j < len(self.blocks):
            for c in self.copies(j):
                c.start()

    def wait(self, j):
        for c in self.copies(j):
            c.wait()
        return self.buf.at[j % self.buf.shape[0]]


PARTS = 2


def over_part(src, dst, send, recv, where, c):
    size = src.shape[0] // PARTS
    at = pl.ds(c * size, size)
    return pltpu.make_async_remote_copy(
        src_ref=src.at[at, :], dst_ref=dst.at[at, :], send_sem=send.at[c], recv_sem=recv.at[c],
        device_id=where, device_id_type=MESH,
    )


def forward_kernel(
    n_dp, n_t, q_own, o_own, i_own, d_own, x0, gains, seg_ids, observed, cos_in, sin_in,
    full, xs, qkv_out, o_out, h2_out, act_out, slope_out, out, mask_out, held,
    stack, x, n, proj, qkv, o, h2, acc, act, slope, outb, mask, wbuf, cos, sin, halves,
    a_sem, c_sem, w_sem, s_sem, y_send, y_recv, x_sem, z_send, z_recv, p_send, p_recv,
    *lend_sems,
):
    l, l1 = Links(n_dp, n_t), Links(n_dp, n_t)
    section = lax.axis_index("section")
    first, second = section == 0, section != 0
    own = (stack, i_own, d_own)
    _, parts0, parts1 = gather_parts(stack.shape[0] // n_dp)
    stacked = [
        pltpu.make_async_copy(ref, stack.at[pl.ds(at, ref.shape[0]), :], a_sem.at[n])
        for n, (ref, at) in enumerate(((q_own, 0), (o_own, q_own.shape[0])))
    ]
    for c in stacked:
        c.start()
    g0 = Gather(l, own, full, parts0, z_send, z_recv, p_send, p_recv)
    g1 = Gather(l1, own, full, parts1, z_send, z_recv, p_send, p_recv)
    lend0, lend1 = Lend(l, own, full, held, *lend_sems), Lend(l1, own, full, held, *lend_sems)
    other = {"section": 1 - section}
    l.greet([{"tensor": l.up}, other] + [{"dp": l.flip(b)} for b in l.bits])
    rows, d = x.shape
    wide = o.shape[2]

    def block(m, slot):
        return own[m] if slot == 0 else full.at[m, slot]

    order = [(0, s) for s in range(n_t)] + [(m, s) for s in range(n_t) for m in (1, 2)]
    load = Loader(wbuf, w_sem, [block(m, s) for m, s in order])
    stores = []

    def store(src, dst, sem):
        copy = pltpu.make_async_copy(src, dst, sem)
        copy.start()
        stores.append(copy)

    walks, here = (g0.walk(lend0), g1.walk()), (set(), set())

    def until(section, m, slot):
        while slot > 0 and (m, slot) not in here[section]:
            here[section].add(next(walks[section]))

    def tick(*sections):
        for at in sections:
            @pl.when((first, second)[at])
            def _():
                here[at].add(next(walks[at], None))

    tables = [pltpu.make_async_copy(t, to, c_sem.at[i]) for i, (t, to) in enumerate(((cos_in, cos), (sin_in, sin)))]
    for c in tables:
        c.start()
    for c in stacked:
        c.wait()

    @pl.when(first)
    def _():
        lend0.give()
        g0.start()
        copy = pltpu.make_async_copy(own_block(x0, l.z, rows), x, x_sem)
        copy.start()
        copy.wait()

    write_mask(mask, seg_ids, observed, l.z)
    write_halves(halves)
    store(mask, mask_out, c_sem.at[2])
    for c in tables:
        c.wait()

    @pl.when(second)
    def _():
        lending = lend1.serve()
        next(lending)
        g1.start()
        for _ in lending:
            pass
        until(1, 0, n_t - 1)
        load.start(0)
        load.start(1)
        until(1, 1, n_t - 2)
        for c in range(PARTS):
            over_part(outb, x, y_send, y_recv, other, c).wait_recv()

    store(x, xs, s_sem.at[0])
    norm_rows(x, gains[0:1, :], n)
    for s in range(n_t):
        @pl.when(first)
        def _():
            until(0, 0, s)
            load.start(s)

        @pl.when(second)
        def _():
            load.start(s + 2)

        w = load.wait(s)
        proj[:, 0:3 * wide] = dot_nt(n[...], w[0:3 * wide, :])

        def turn_rows(at):
            v = proj[at, 0:2 * wide]
            qkv[s, at, 0:2 * wide] = (v * cos[at, :] + partner(v, halves) * sin[at, :]).astype(BF16)
            qkv[s, at, 2 * wide:3 * wide] = proj[at, 2 * wide:3 * wide].astype(BF16)

        row_loop(rows, 128, turn_rows)
        tick(0)
        attend_slot(qkv.at[s], o.at[s], mask)
        tick(0, 1)
        term = dot_nn(o[s], w[3 * wide:, :])
        if s == 0:
            acc[...] = term
        else:
            acc[...] = acc[...] + term
        store(qkv.at[s], qkv_out.at[s], s_sem.at[1 + s])
        store(o.at[s], o_out.at[s], s_sem.at[1 + n_t + s])

    def middle(at):
        h = x[at, :].astype(F32) + acc[at, :]
        h2[at, :] = h
        acc[at, :] = h
        r = lax.rsqrt(jnp.mean(h * h, axis=1, keepdims=True) + EPS)
        n[at, :] = (h * r * gains[1:2, :]).astype(BF16)

    row_loop(rows, 64, middle)
    store(h2, h2_out, s_sem.at[1 + 2 * n_t])
    spare = 2 + 2 * n_t
    for s in range(n_t):
        j = n_t + 2 * s

        @pl.when(first)
        def _():
            until(0, 1 if s == n_t - 1 else 2, s)
            load.start(j)
            if s < n_t - 1:
                load.start(j + 1)

        @pl.when(second)
        def _():
            if s == n_t - 1:
                until(1, 2, s)
                load.start(j)
                load.start(j + 1)
            elif s < n_t - 2:
                until(1, 1, s + 1)
                load.start(j + 2)

        w = load.wait(j)
        if s >= 2:
            for copy in stores[-4:-2]:
                copy.wait()
            del stores[-4:-2]
        for c in column_steps(act.shape[2]):
            u = dot_nn(n[...], w[:, c])
            sig = lax.logistic(u)
            act[s % 2, :, c] = (u * sig).astype(BF16)
            slope[s % 2, :, c] = (sig * (1.0 + u * (1.0 - sig))).astype(BF16)
        tick(*((1,) if s == 0 else (0, 1)))

        @pl.when(first)
        def _():
            if s == n_t - 1:
                until(0, 2, s)
                load.start(j + 1)

        @pl.when(second)
        def _():
            if s < n_t - 2:
                until(1, 2, s + 1)
                load.start(j + 3)

        w = load.wait(j + 1)
        if s < n_t - 1:
            acc[...] = acc[...] + dot_nn(act[s % 2], w[...])
        else:
            for c in range(PARTS):
                at = slice(c * rows // PARTS, (c + 1) * rows // PARTS)
                outb[at, :] = (acc[at, :] + dot_nn(act[s % 2, at, :], w[...])).astype(BF16)

                @pl.when(first)
                def _():
                    over_part(outb, x, y_send, y_recv, other, c).start()

        store(act.at[s % 2], act_out.at[s], s_sem.at[spare + 2 * (s % 2)])
        store(slope.at[s % 2], slope_out.at[s], s_sem.at[spare + 2 * (s % 2) + 1])

    assert all(len(h - {None}) == 3 * (n_t - 1) for h in here)
    store(outb, out, x_sem)
    for copy in stores:
        copy.wait()

    @pl.when(first)
    def _():
        for c in range(PARTS):
            over_part(outb, x, y_send, y_recv, other, c).wait_send()
        l.drain()

    @pl.when(second)
    def _():
        l1.drain()


def run_forward(q_own, o_own, i_own, d_own, x0, gains, seg, obs, tables):
    n_dp, n_t = lax.axis_size("dp"), lax.axis_size("tensor")
    wide, d = o_own.shape
    rows = x0.shape[0] * x0.shape[1] // n_t
    whole = (4 * wide, d)
    lent, parts, _ = gather_parts(whole[0] // n_dp)
    count = 3 * (n_t - 1) * len(parts)
    dma = pltpu.SemaphoreType.DMA
    hbm, vmem = pl.BlockSpec(memory_space=pl.ANY), pl.BlockSpec(memory_space=pltpu.VMEM)

    def shape(*s, t=BF16):
        return jax.ShapeDtypeStruct(s, t)

    return pl.pallas_call(
        functools.partial(forward_kernel, n_dp, n_t),
        out_shape=[
            shape(3, n_t, *whole), shape(rows, d), shape(n_t, rows, 3 * wide), shape(n_t, rows, wide),
            shape(rows, d, t=F32), shape(n_t, rows, i_own.shape[1]), shape(n_t, rows, i_own.shape[1]), shape(rows, d),
            shape(2 * QB, ROW, t=F32), shape(3, n_t, n_dp, lent, d),
        ],
        in_specs=[hbm] * 5 + [vmem] * 3 + [hbm] * 2,
        out_specs=[hbm] * 10,
        scratch_shapes=[
            pltpu.VMEM(whole, BF16),
            pltpu.VMEM((rows, d), BF16),
            pltpu.VMEM((rows, d), BF16),
            pltpu.VMEM((rows, d), F32),
            pltpu.VMEM((n_t, rows, 3 * wide), BF16),
            pltpu.VMEM((n_t, rows, wide), BF16),
            pltpu.VMEM((rows, d), F32),
            pltpu.VMEM((rows, d), F32),
            pltpu.VMEM((2, rows, d), BF16),
            pltpu.VMEM((2, rows, d), BF16),
            pltpu.VMEM((rows, d), BF16),
            pltpu.VMEM((2 * QB, ROW), F32),
            pltpu.VMEM((3,) + whole, BF16),
            pltpu.VMEM(tables[0].shape, F32),
            pltpu.VMEM(tables[1].shape, F32),
            pltpu.VMEM((8, tables[0].shape[1]), F32),
            dma((2,)), dma((3,)), dma((2, 3)), dma((6 + 2 * n_t,)), dma((PARTS,)), dma((PARTS,)), dma(()),
            dma((count,)), dma((count,)), dma((count, n_dp)), dma((count, n_dp)),
            dma((3,)), dma((3,)), dma((3, n_t)), dma((3, n_t)),
            dma((3, n_t, n_dp)), dma((3, n_t, n_dp)), dma((3, n_t, n_dp)), dma((3, n_t, n_dp)),
        ],
        compiler_params=pltpu.CompilerParams(collective_id=0, has_side_effects=True, vmem_limit_bytes=60 * 2**20),
    )(q_own, o_own, i_own, d_own, x0, gains, seg, obs, *tables)


def attend_slot_back(qkv, do, dqk, dcat, mask):
    wide = do.shape[1]
    heads = wide // HEAD_SIZE
    for h in range(heads):
        q, k, v = (slice((t * heads + h) * HEAD_SIZE, (t * heads + h + 1) * HEAD_SIZE) for t in range(3))
        qh, kh, vh, dh = qkv[:, q], qkv[:, k], qkv[:, v], do[:, q]
        p = probabilities(qh, kh, mask)
        dcat[:, v] = to_keys(p.astype(BF16), dh).astype(BF16)
        dp = by_window(vh, dh)
        ds = (p * (dp - jnp.sum(p * dp, axis=0, keepdims=True))).astype(BF16)
        dqk[:, q] = to_queries(ds, kh) * SCALE
        dqk[:, k] = to_keys(ds, qh) * SCALE


def outer_product(out, left, right):
    step = left.shape[1] // 2

    def turn(j, _):
        at = pl.ds(pl.multiple_of(j * step, 128), step)
        out[at, :] = dot_tn(left[:, at], right[...]).astype(BF16)
        return 0

    lax.fori_loop(0, 2, turn, 0)


def norm_back_rows(g, dn, h, gain, gain_sum, normed, write, part=0, parts=1):
    if part == 0:
        gain_sum[...] = jnp.zeros_like(gain_sum)
    step = 64
    count = h.shape[0] // step // parts

    def body(at):
        hr, dr = h[at, :].astype(F32), dn[at, :]
        r = lax.rsqrt(jnp.mean(hr * hr, axis=1, keepdims=True) + EPS)
        y = gain * dr
        if normed is not None:
            normed[at, :] = (hr * r * gain).astype(BF16)
        gain_sum[...] += jnp.sum((dr * hr * r).reshape(step // 8, 8, -1), axis=0)
        write(at, g[at, :].astype(F32) + r * y - hr * (r * r * r) * jnp.mean(hr * y, axis=1, keepdims=True))

    def turn(r, _):
        body(pl.ds(pl.multiple_of((part * count + r) * step, step), step))
        return 0

    lax.fori_loop(0, count, turn, 0)


def backward_kernel(
    n_dp, n_t, q_own, o_own, i_own, d_own, full, cot, xs, qkv_in, o_in, h2_in, act_in, slope_in, out_in, mask_in, gains,
    cos_in, sin_in,
    layer_acts, grad_acts, out_sums, out_gains, hbm_sums, hbm_got, hbm_ring, du_hbm,
    gbuf, act, du, n, h2, x, dn, ga, proj, qkv, o, do, dcat, dhb, mask, wbuf, cos, sin, halves, gain0, gain1, gain_buf,
    c_sem, w_sem, l_sem, o_sem, a_sem, u_sem, q_sem, st_sem, y_send, y_recv, s1_send, s1_recv, s2_send, s2_recv, t_send, t_recv,
    *reduce_refs,
):
    section = lax.axis_index("section")
    first, second = section == 0, section != 0
    other = {"section": 1 - section}
    l, l2, l3 = (Links(n_dp, n_t) for _ in range(3))
    own = ((q_own, o_own), i_own, d_own)
    rows, d = h2.shape
    wide = do.shape[1]
    places = Places(l)
    slots = places.slot
    order = [(m, j) for j in range(n_t) for m in (2, 1)] + [(0, j) for j in range(n_t)]
    ff = 2 * n_t
    hbm = (hbm_sums, hbm_got, hbm_ring)
    r = Reduce(l, places, order, out_sums, hbm, reduce_refs)
    rm = Reduce(l3, places, order, out_sums, hbm, reduce_refs)
    inner = places.below * places.above == 1
    end_first, inner_first = first & ~inner, first & inner
    r2 = Reduce(l2, places, order, out_sums, hbm, reduce_refs)
    spread1 = Spread(l, places, out_in, layer_acts, s1_send, s1_recv)
    spread1b = Spread(l2, places, out_in, layer_acts, s1_send, s1_recv)
    spread2 = Spread(l, places, dhb, grad_acts, s2_send, s2_recv)
    spread2b = Spread(l2, places, dhb, grad_acts, s2_send, s2_recv)
    load = Loader(wbuf, w_sem, [own[m] if j == n_t - 1 else full.at[m, slots[j]] for m, j in order])

    l.greet([{"tensor": l.up}, {"tensor": l.down}, other] + [{"dp": l.flip(b)} for b in l.bits])
    cot_copy = pltpu.make_async_copy(own_block(cot, l.z, rows), gbuf, l_sem.at[4])

    @pl.when(second)
    def _():
        cot_copy.start()

    def local(src, dst, sem):
        return pltpu.make_async_copy(src, dst, sem)

    load.start(0)
    load.start(1)
    spread1.start()

    acts_in = local(out_in, dhb, l_sem.at[0])
    acts_out = local(dhb, layer_acts.at[l.z], l_sem.at[0])
    h2_copy = local(h2_in, h2, l_sem.at[1])
    x_copy = local(xs, x, l_sem.at[2])
    o_copies = [local(o_in.at[slots[j]], o.at[j], o_sem.at[j]) for j in range(n_t)]

    def act_copy(j):
        return local(act_in.at[slots[j]], act.at[j % 2], a_sem.at[j % 2])

    def slope_copy(j):
        return local(slope_in.at[slots[j]], du.at[j % 2], u_sem.at[j % 2])

    def du_out(j):
        return local(du.at[j % 2], du_hbm.at[slots[j]], st_sem.at[j % 2])

    def du_in(j):
        return local(du_hbm.at[slots[j]], du.at[j % 2], u_sem.at[j % 2])

    def qkv_copy(j):
        return local(qkv_in.at[slots[j]], qkv.at[j % 2], q_sem.at[j % 2])

    slope_copy(0).start()
    act_copy(0).start()
    for c in (h2_copy, acts_in, x_copy, *o_copies):
        c.start()
    tables = [local(t, to, c_sem.at[i]) for i, (t, to) in enumerate(((cos_in, cos), (sin_in, sin), (mask_in, mask)))]
    for c in tables:
        c.start()
    write_halves(halves)

    @pl.when(first)
    def _():
        h2_copy.wait()
        norm_rows(h2, gains[1:2, :], n)

    @pl.when(second)
    def _():
        cot_copy.wait()

    @pl.when(first)
    def _():
        for k in range(1, n_t - 1):
            spread1.step(k)
        for c in range(PARTS):
            over_part(dhb, gbuf, y_send, y_recv, other, c).wait_recv()

    def block_of(reducer, i):
        if i >= 3:
            reducer.clear(i)
        return reducer.block.at[i % 3]

    for j in range(n_t):
        if j + 1 < n_t:
            act_copy(j + 1).start()
            if j + 1 >= 2:
                du_out(j - 1).wait()
            slope_copy(j + 1).start()
        act_copy(j).wait()

        @pl.when(first)
        def _():
            outer_product(block_of(r, 2 * j), gbuf, act.at[j % 2])
            r.pump()
            r.push(2 * j)

        w = load.wait(2 * j)
        slope_copy(j).wait()
        for c in column_steps(act.shape[2]):
            du[j % 2, :, c] = (dot_nt(gbuf[...], w[c, :]) * du[j % 2, :, c].astype(F32)).astype(BF16)
        load.start(2 * j + 2)
        du_out(j).start()

        @pl.when(first)
        def _():
            r.pump()

        w = load.wait(2 * j + 1)
        if j == 0:
            dn[...] = dot_nt(du[j % 2], w[...])
        else:
            dn[...] = dn[...] + dot_nt(du[j % 2], w[...])
        load.start(2 * j + 3)

        @pl.when(first)
        def _():
            r.pump()
            outer_product(block_of(r, 2 * j + 1), n, du.at[j % 2])
            r.pump()
            r.push(2 * j + 1)

        if j >= 2:
            @pl.when(end_first)
            def _():
                r.last_step(j - 2)

    for j in range(max(n_t - 2, 0), n_t):
        du_out(j).wait()

    qkv_copy(0).start()
    acts_in.wait()
    acts_out.start()

    @pl.when(second)
    def _():
        h2_copy.wait()

    def write_middle(at, value):
        h2[at, :] = value
        ga[at, :] = value.astype(BF16)

    norm_back_rows(gbuf, dn, h2, gains[1:2, :], gain1, n, write_middle)
    for c in (*o_copies, *tables):
        c.wait()

    for j in range(n_t):
        if j + 1 < n_t:
            qkv_copy(j + 1).start()
        w = load.wait(ff + j)
        load.start(ff + j + 2)
        do[...] = dot_nt(ga[...], w[3 * wide:, :]).astype(BF16)
        qkv_copy(j).wait()
        @pl.when(first)
        def _():
            r.pump()

        attend_slot_back(qkv.at[j % 2], do, proj, dcat.at[j], mask)

        def turn_back(at):
            v = proj[at, 0:2 * wide]
            dcat[j, at, 0:2 * wide] = (v * cos[at, :] - partner(v, halves) * sin[at, :]).astype(BF16)

        row_loop(rows, 128, turn_back)
        if j == 0:
            dn[...] = dot_nn(dcat[j], w[0:3 * wide, :])
        else:
            dn[...] = dn[...] + dot_nn(dcat[j], w[0:3 * wide, :])
        @pl.when(first)
        def _():
            r.pump()

        if j in (0, 2):
            @pl.when(end_first)
            def _():
                r.last_step(2 + j // 2)

        if j < 2:
            @pl.when(inner_first)
            def _():
                rm.last_step(j)
    x_copy.wait()
    acts_out.wait()

    def write_input(at, value):
        dhb[at, :] = value.astype(BF16)

    for c in range(PARTS):
        norm_back_rows(h2, dn, x, gains[0:1, :], gain0, None, write_input, c, PARTS)

        @pl.when(second)
        def _():
            over_part(dhb, gbuf, y_send, y_recv, other, c).start()

    spread2.start()
    grads_out = local(dhb, grad_acts.at[l.z], l_sem.at[0])
    grads_out.start()

    @pl.when(second)
    def _():
        du_in(0).start()
        act_copy(0).start()
        for j in range(n_t):
            if j + 1 < n_t:
                act_copy(j + 1).start()
                du_in(j + 1).start()
            act_copy(j).wait()
            outer_product(block_of(r2, 2 * j), gbuf, act.at[j % 2])
            r2.pump()
            r2.push(2 * j)
            du_in(j).wait()
            outer_product(block_of(r2, 2 * j + 1), n, du.at[j % 2])
            r2.pump()
            r2.push(2 * j + 1)
        spread1b.step(1)
        r2.flush()

    total = Total(l, gain0, gain_buf, t_send, t_recv)
    gain0[0:1, :] = jnp.sum(gain0[...], axis=0, keepdims=True)
    gain0[1:2, :] = jnp.sum(gain1[...], axis=0, keepdims=True)
    norm_rows(x, gains[0:1, :], n)
    for j in range(n_t):
        b = block_of(r, ff + j)
        step = d // 2

        def turn(c, _):
            at = pl.ds(pl.multiple_of(c * step, 128), step)
            b[at, 0:3 * wide] = dot_tn(n[:, at], dcat[j]).astype(BF16)
            b[at, 3 * wide:] = dot_tn(ga[:, at], o[j]).astype(BF16)
            return 0

        lax.fori_loop(0, 2, turn, 0)
        r.pump()
        r.push(ff + j)
    r.flush()

    @pl.when(inner_first)
    def _():
        for i in range(2, 4):
            rm.last_step(i)

    @pl.when(second)
    def _():
        for i in range(4):
            r2.last_step(i)
        for k in range(2, n_t - 1):
            spread1b.step(k)

    for i in range(4, len(order)):
        r.last_step(i)
        if i == 4 or i == 5:
            @pl.when(inner)
            def _():
                spread2.step(i - 3)
        if i >= 6 and i - 6 < total.count:
            total.step(i - 6)
    for t in range(len(order) - 6, total.count):
        total.step(t)
    l2.recording = False

    @pl.when(~inner)
    def _():
        for k in range(1, n_t - 1):
            spread2b.step(k)

    spread1.step(n_t - 1)
    spread2.step(n_t - 1)
    out_gains[...] = total.result()
    r.close()
    grads_out.wait()

    @pl.when(second)
    def _():
        for c in range(PARTS):
            over_part(dhb, gbuf, y_send, y_recv, other, c).wait_send()

    l.drain()


def run_backward(q_own, o_own, i_own, d_own, kept, cot, gains, tables):
    n_dp, n_t = lax.axis_size("dp"), lax.axis_size("tensor")
    wide, d = o_own.shape
    rows = cot.shape[0] * cot.shape[1] // n_t
    piece = d // n_dp
    count = 3 * n_t
    steps = len(ring_bits(n_dp)) + n_t
    dma = pltpu.SemaphoreType.DMA
    hbm, vmem = pl.BlockSpec(memory_space=pl.ANY), pl.BlockSpec(memory_space=pltpu.VMEM)

    def shape(*s, t=BF16):
        return jax.ShapeDtypeStruct(s, t)

    def buf(*s, t=BF16):
        return pltpu.VMEM(s, t)

    return pl.pallas_call(
        functools.partial(backward_kernel, n_dp, n_t),
        out_shape=[
            shape(n_t, rows, d), shape(n_t, rows, d), shape(3, piece, d, t=F32), shape(8, d, t=F32),
            *reduce_hbm(n_dp, n_t, count, piece, d), shape(n_t, rows, d),
        ],
        in_specs=[hbm] * 14 + [vmem] + [hbm] * 2,
        out_specs=[hbm] * 3 + [vmem] + [hbm] * 4,
        scratch_shapes=[
            buf(rows, d), buf(2, rows, d), buf(2, rows, d), buf(rows, d), buf(rows, d, t=F32), buf(rows, d),
            buf(rows, d, t=F32), buf(rows, d), buf(rows, d, t=F32), buf(2, rows, 3 * wide), buf(n_t, rows, wide),
            buf(rows, wide), buf(n_t, rows, 3 * wide), buf(rows, d), buf(2 * QB, ROW, t=F32), buf(3, 4 * wide, d),
            buf(*tables[0].shape, t=F32), buf(*tables[1].shape, t=F32), buf(8, tables[0].shape[1], t=F32),
            buf(8, d, t=F32), buf(8, d, t=F32), buf(2 * steps, 8, d, t=F32),
            dma((3,)), dma((2, 3)), dma((5,)), dma((n_t,)), dma((2,)), dma((2,)), dma((2,)), dma((2,)), dma((PARTS,)), dma((PARTS,)),
            dma((2, n_t)), dma((2, n_t)), dma((2, n_t)), dma((2, n_t)), dma((steps,)), dma((steps,)),
            *reduce_scratch(n_dp, n_t, count, piece, d),
        ],
        compiler_params=pltpu.CompilerParams(collective_id=1, has_side_effects=True, vmem_limit_bytes=62 * 2**20),
    )(q_own, o_own, i_own, d_own, kept[0], cot, *kept[1:], gains, *tables)


def finish_kernel(n_dp, layer_in, grad_in, sums, gain, layer_out, grad_out, qkv, out, w_in, down, gain_out, rows, heads, wide, sem, heads_sem, wide_sem):
    arrays = ((layer_in, layer_out), (grad_in, grad_out))
    n = layer_in.shape[0]

    def load(i):
        return pltpu.make_async_copy(arrays[i // n][0].at[i % n], rows.at[i], sem.at[0, i])

    def store(i):
        return pltpu.make_async_copy(rows.at[i], arrays[i // n][1].at[i % n], sem.at[1, i])

    heads_in = pltpu.make_async_copy(sums.at[0], heads, heads_sem)
    wide_in = [pltpu.make_async_copy(sums.at[1 + m], wide.at[m], wide_sem.at[0, m]) for m in range(2)]
    wide_out = [pltpu.make_async_copy(wide.at[m], to, wide_sem.at[1, m]) for m, to in enumerate((w_in, down))]
    heads_in.start()
    for c in wide_in:
        c.start()
    for i in range(2 * n):
        load(i).start()
    hd = out.shape[0]
    me = lax.axis_index("dp")
    for k in range(n_dp):
        @pl.when(me == k)
        def _():
            gain_out[...] = gain[0:2, k * gain_out.shape[1]:(k + 1) * gain_out.shape[1]]

    for c, o in zip(wide_in, wide_out):
        c.wait()
        o.start()
    for i in range(2 * n):
        load(i).wait()
        store(i).start()
    heads_in.wait()
    for t in range(3):
        qkv[t] = heads[:, t * hd:(t + 1) * hd]
    out[...] = jnp.transpose(heads[:, 3 * hd:])
    for o in wide_out:
        o.wait()
    for i in range(2 * n):
        store(i).wait()


def lay_out(layer_acts, grad_acts, sums, gain, n_dp):
    n, rows, d = layer_acts.shape
    piece, hd = sums.shape[1], sums.shape[2] // 4
    hbm, vmem = pl.BlockSpec(memory_space=pl.ANY), pl.BlockSpec(memory_space=pltpu.VMEM)
    dma = pltpu.SemaphoreType.DMA
    acts = jax.ShapeDtypeStruct(layer_acts.shape, BF16)

    def shape(*s):
        return jax.ShapeDtypeStruct(s, F32)

    return pl.pallas_call(
        functools.partial(finish_kernel, n_dp),
        out_shape=[acts, acts, shape(3, piece, hd), shape(hd, piece), shape(piece, d), shape(piece, d), shape(2, d // n_dp)],
        in_specs=[hbm, hbm, hbm, vmem],
        out_specs=[hbm, hbm, vmem, vmem, hbm, hbm, vmem],
        scratch_shapes=[
            pltpu.VMEM((2 * n, rows, d), BF16), pltpu.VMEM((piece, d), F32), pltpu.VMEM((2, piece, d), F32),
            dma((2, 2 * n)), dma(()), dma((2, 2)),
        ],
        compiler_params=pltpu.CompilerParams(vmem_limit_bytes=62 * 2**20),
    )(layer_acts, grad_acts, sums, gain)


def on_device(tokens, cotangent, seg_ids, observed, w_qkv, w_out, w_in, w_down, norm_gains):
    n_dp, n_t = lax.axis_size("dp"), lax.axis_size("tensor")
    w_qkv, w_out, w_in, w_down, gains = w_qkv[0], w_out[0], w_in[0], w_down[0], norm_gains[0]
    micro, rows, d = tokens.shape
    hd = w_out.shape[0]
    tables = rope_tables()
    heads = jnp.swapaxes(w_qkv, 1, 2).reshape(3 * hd, d)
    kept = run_forward(heads, w_out, w_in, w_down, tokens, gains, seg_ids, observed, tables)[:9]
    layer_acts, grad_acts, sums, gain = run_backward(heads, w_out, w_in, w_down, kept, cotangent, gains, tables)[:4]
    layer_acts, grad_acts, r_qkv, r_out, r_in, r_down, gain = lay_out(layer_acts, grad_acts, sums, gain, n_dp)
    return (
        layer_acts.reshape(1, micro, rows, d),
        grad_acts.reshape(1, micro, rows, d),
        r_qkv[None],
        r_out[None],
        r_in[None],
        r_down.T[None],
        gain[None],
    )


def solution(mesh):
    return jax.shard_map(
        on_device,
        mesh=mesh,
        in_specs=(
            P(None, "dp", None),
            P(None, "dp", None),
            P(None, "dp"),
            P(None, "dp"),
            P("section", None, None, "tensor"),
            P("section", "tensor", None),
            P("section", None, "tensor"),
            P("section", "tensor", None),
            P("section", None, None),
        ),
        out_specs=(
            P("section", None, "dp", None),
            P("section", None, "dp", None),
            P("section", None, "dp", "tensor"),
            P("section", "tensor", "dp"),
            P("section", "dp", "tensor"),
            P("section", "tensor", "dp"),
            P("section", None, "dp"),
        ),
        check_vma=False,
    )
```
